32 devices in a mesh: grp: 2 (over y), lvl: 4 (over x, core), col: 4 (over z).
Axes of the slice: x: 2, y: 2, z: 4, core: 2. Of those that a mesh axis runs over, the one named last changes fastest.
Arguments:
- inverse_diag: float32 [64, 256, 256], P(('grp', 'lvl')), parts along dimension 0, may hold values from 0 to 2, as said below
- down_block: float32 [64, 256, 256], P(('grp', 'lvl')), parts along dimension 0, may hold values from 0 to 2, as said below
- up_block: float32 [64, 256, 256], P(('grp', 'lvl')), parts along dimension 0, may hold values from 0 to 1, as said below
- reward: float32 [64, 64, 256], P(('grp', 'lvl'), 'col'), parts along dimension 0, may hold values from -6 to 6
Outputs:
- values: float32 [64, 64, 256], P(('grp', 'lvl'), 'col'), parts along dimension 0
The draws below stay inside these ranges and needn't reach their ends.
There are 2 independent parts, one for each index of `grp`. The reference program is written for one: setup_inputs(seed, part) draws one part's arguments, and reference() takes and returns one part's arrays. A program takes and returns all parts, laid end to end along the dimension named above; each array names one. Nothing has to cross between parts.
Inputs may be any that keep to these rules, and one draw needn't show every extreme that they name: `inverse_diag`: Nonnegative. `down_block`: Nonnegative. `up_block`: Nonnegative.
All inputs are finite; a program needn't handle non-finite values.
Results may differ from the reference program's by a relative error of at most 0.00011.
Values sent between devices are 32-bit elements; how exact they have to be, the bound alone decides.
No kernel may reach another device: no remote copies, remote signals or barrier semaphores. Data moves between devices by JAX's collectives and lax.ppermute only.
A program may use at most 64 MiB of HBM per device.

```python
import math
import jax
import jax.numpy as jnp
import numpy as np
from jax import lax

M = 256
K = 64
SWEEPS = 8
LEVELS = 32


mix_local = 0.2


mix_tail = 0.02


up_strength = 3.0


def level_scale(key):
    spread = jax.random.uniform(jax.random.fold_in(key, 17), (LEVELS, 1, 1), jnp.float32, math.log(0.5), math.log(2.0))
    return jnp.exp(spread)


def keep_rate():
    keep_share = 0.3
    return keep_share ** (1.0 / LEVELS)


def local_table():
    offsets = np.abs(np.arange(M)[:, None] - np.arange(M)[None, :])
    weights = np.where((offsets > 0) & (offsets <= 4), 5.0 - offsets, 0.0)
    weights = weights / weights.sum(axis=1, keepdims=True)
    return jnp.asarray(weights, dtype=jnp.float32)


def phase_mixing(key):
    local_low, local_high, tail_low, tail_high = (0.5, 1.5, 0.0, 2.0)
    local_noise = jax.random.uniform(jax.random.fold_in(key, 1), (LEVELS, M, M), jnp.float32, local_low, local_high)
    tail_noise = jax.random.uniform(jax.random.fold_in(key, 2), (LEVELS, M, M), jnp.float32, tail_low, tail_high)
    diag_noise = jax.random.uniform(jax.random.fold_in(key, 3), (LEVELS, M), jnp.float32, 0.9, 1.1)
    identity_mat = jnp.eye(M, dtype=jnp.float32)
    own_part = (1.0 - mix_local - mix_tail) * diag_noise[:, :, None] * identity_mat[None, :, :]
    near_part = mix_local * local_noise * local_table()[None, :, :]
    far_part = mix_tail / M * tail_noise
    return own_part + near_part + far_part


def draw_inverse_diag(key, part):
    return phase_mixing(jax.random.fold_in(key, 101)) * (keep_rate() / level_scale(key))


def draw_down_block(key, part):
    return phase_mixing(jax.random.fold_in(key, 202)) * level_scale(key)


def draw_up_block(key, part):
    return phase_mixing(jax.random.fold_in(key, 303)) * level_scale(key) * (up_strength / max(LEVELS, 32))


def level_of(rng, dims, pieces, smallest, top_value):
    gain = 1.0
    for position, parts in pieces:
        draws = jax.random.uniform(jax.random.fold_in(jax.random.fold_in(rng, 6), position), (parts,), jnp.float32, smallest / len(pieces), top_value / len(pieces))
        gain = gain * jnp.repeat(jnp.exp(draws), dims[position] // parts).reshape((-1,) + (1,) * (len(dims) - 1 - position))
    return gain


def gaussian(own_key, shape, scale, most, split=(), held_as=jnp.bfloat16):
    result = jax.random.normal(own_key, shape, jnp.float32) * scale
    if len(split) > 0:
        result = level_of(own_key, shape, split, -0.22, 0.18) * result
    return jnp.clip(result, min=-most, max=most).astype(held_as)


def setup_inputs(seed: int = 0, part: int = 0) -> dict:
    key_list = jax.random.split(jax.random.key(seed), 5)
    part_keys = jax.random.split(jax.random.fold_in(key_list[4], part), 5)
    return {
        "inverse_diag": draw_inverse_diag(jax.random.fold_in(jax.random.fold_in(key_list[4], part), 71), part),
        "down_block": draw_down_block(jax.random.fold_in(jax.random.fold_in(key_list[4], part), 71), part),
        "up_block": draw_up_block(jax.random.fold_in(jax.random.fold_in(key_list[4], part), 71), part),
        "reward": gaussian(part_keys[3], (LEVELS, K, M), 1.0, 6.0, ((0, 4), (1, 4)), jnp.float32),
    }


PRECISE = lax.Precision.HIGHEST


def apply_right(vector, matrix):
    return jnp.einsum("km,pm->kp", vector, matrix, precision=PRECISE)


def one_sweep(estimate, inverse_diag, down_block, up_block, reward):
    shifted = jnp.concatenate([estimate[1:], jnp.zeros_like(estimate[:1])], axis=0)

    def level_step(carried, inputs):
        inv_here, down_here, up_here, pay_here, next_old = inputs
        updated = apply_right(pay_here + apply_right(carried, down_here) + apply_right(next_old, up_here), inv_here)
        return updated, updated

    _, stacked = lax.scan(level_step, jnp.zeros_like(estimate[0]), (inverse_diag, down_block, up_block, reward, shifted))
    return stacked


def reference(inverse_diag, down_block, up_block, reward):
    estimate = jnp.zeros_like(reward)
    for repeat in range(SWEEPS):
        estimate = one_sweep(estimate, inverse_diag, down_block, up_block, reward)
    return estimate
```

```python
import functools

import jax
import jax.numpy as jnp
from jax import lax
from jax.experimental import pallas as pl
from jax.experimental.pallas import tpu as pltpu
from jax.sharding import PartitionSpec as P

SWEEPS = 8
CHUNK = 4
CHUNKS = SWEEPS // CHUNK
AHEAD = SWEEPS - 1
F32 = jnp.float32
BF16 = jnp.bfloat16


def resident(shape, dtype):
    return pltpu.VMEM(shape, dtype)


def pin(x, memory=pltpu.VMEM):
    return pltpu.with_memory_space_constraint(x, memory)


def split(x):
    high = x.astype(BF16)
    return high, (x - high.astype(F32)).astype(BF16)


def dot(a, b):
    return jnp.dot(a, b, preferred_element_type=F32)


def dot_parts(a, b):
    return dot(a[0], b[0]) + (dot(a[0], b[1]) + dot(a[1], b[0]))


def prepare_kernel(
    inv_hbm, down_hbm, up_hbm, reward,
    a_high, a_low, b_high, b_low, base, kept,
    inv, down, up, x_high, x_low, sems,
):
    levels = inv.shape[0]
    phases = inv.shape[1]
    columns = reward.shape[1]

    def copies(i):
        return [
            pltpu.make_async_copy(source.at[i], target.at[i], sems.at[n, i])
            for n, (source, target) in enumerate(((inv_hbm, inv), (down_hbm, down), (up_hbm, up)))
        ]

    for i in range(levels):
        for copy in copies(i):
            copy.start()

    def products(i, _):
        for copy in copies(i):
            copy.wait()
        here = split(inv[i])
        a_high[i], a_low[i] = split(dot_parts(here, split(down[i])).T)
        b_high[i], b_low[i] = split(dot_parts(here, split(up[i])).T)
        pay = split(reward[i])
        base[i] = dot_nt(pay[0], here[0]) + (dot_nt(pay[0], here[1]) + dot_nt(pay[1], here[0]))
        return 0

    lax.fori_loop(0, levels, products, 0)

    rows = lax.broadcasted_iota(jnp.int32, (phases, phases), 0)
    lanes = lax.broadcasted_iota(jnp.int32, (phases, phases), 1)
    x_high[...] = jnp.zeros_like(x_high)
    x_low[...] = jnp.zeros_like(x_low)
    x_high[0, 0:phases] = jnp.where(rows == lanes, 1.0, 0.0).astype(BF16)

    def sweep(n, _):
        def level(i, _):
            below = (x_high[i], x_low[i])
            above = (x_high[i + 2], x_low[i + 2])
            new = dot_parts(below, (a_high[i], a_low[i])) + dot_parts(above, (b_high[i], b_low[i]))
            first = new[0:phases]
            second = new[phases : phases + columns] + base[i]
            x_high[i + 1, 0:phases], x_low[i + 1, 0:phases] = split(first)
            x_high[i + 1, phases : phases + columns], x_low[i + 1, phases : phases + columns] = split(second)

            @pl.when(i == 0)
            def _():
                kept[n, 0:phases] = first
                kept[n, phases : phases + columns] = second

            return 0

        lax.fori_loop(0, AHEAD - n, level, 0)

        @pl.when(n == 0)
        def _():
            x_high[0] = jnp.zeros_like(x_high[0])

        return 0

    lax.fori_loop(0, AHEAD, sweep, 0)


def dot_nt(a, b):
    return lax.dot_general(a, b, (((1,), (1,)), ((), ())), preferred_element_type=F32)


def prepare(inverse_diag, down_block, up_block, reward):
    levels, phases, _ = inverse_diag.shape
    columns = reward.shape[1]
    matrix = (levels, phases, phases)
    assert levels >= AHEAD
    vmem = pl.BlockSpec(memory_space=pltpu.VMEM)
    return pl.pallas_call(
        prepare_kernel,
        out_shape=[resident(matrix, BF16)] * 4
        + [
            resident((levels, columns, phases), F32),
            jax.ShapeDtypeStruct((AHEAD, phases + columns, phases), F32),
        ],
        in_specs=[pl.BlockSpec(memory_space=pltpu.HBM)] * 3 + [vmem],
        out_specs=[vmem] * 6,
        scratch_shapes=[pltpu.VMEM(matrix, F32)] * 3
        + [pltpu.VMEM((levels + 2, phases + columns, phases), BF16)] * 2
        + [pltpu.SemaphoreType.DMA((3, levels))],
        compiler_params=pltpu.CompilerParams(vmem_limit_bytes=30 * 2**20),
        name="prepare",
    )(*[pin(x, pltpu.HBM) for x in (inverse_diag, down_block, up_block)], reward)


def stack(x):
    high = x.astype(BF16).astype(F32)
    return jnp.concatenate([high, x - high], axis=0).astype(BF16)


def fold(total):
    half = total.shape[0] // 2
    return total[:half] + total[half:]


def stage_kernel(choices, place, a_high, a_low, b_high, b_low, base, kept, state, entering, earlier, new_state, leaving):
    levels, columns, phases = state.shape

    def apply(x, high, low):
        return dot(x, high) + dot(x, low)

    def chunk_of(chunk):
        first = chunk * CHUNK
        feedback = {j: split(kept[j, 0:phases]) for j in range(first + CHUNK - 1)}
        above = {}
        for n in range(first, first + CHUNK):
            above[n] = jnp.zeros((columns, phases), F32) if n == 0 else kept[n - 1, phases : phases + columns]
        past = {n: stack(earlier[n - first + CHUNK - 1]) for n in range(1, first + 1)}
        for j in range(first + CHUNK - 1) if first else ():
            pairs = [(n, n - j) for n in above if n - j in past]
            if pairs:
                total = apply(jnp.concatenate([past[m] for _, m in pairs], axis=0), *feedback[j])
                for p, (n, _) in enumerate(pairs):
                    above[n] += fold(total[p * 2 * columns : (p + 1) * 2 * columns])

        now = {}
        for i in range(levels):
            now[i, first] = stack(state[i]) if first else None
        for k in range(CHUNK):
            now[-1, first + 1 + k] = stack(entering[k])
        for step in range(levels + 2 * (CHUNK - 1)):
            for k in range(CHUNK):
                i = step - 2 * k
                if not 0 <= i < levels:
                    continue
                n = first + 1 + k
                total = apply(now[i - 1, n], a_high[i], a_low[i])
                if n > 1:
                    over = stack(above[n - 1]) if i == levels - 1 else now[i + 1, n - 1]
                    total += apply(over, b_high[i], b_low[i])
                value = base[i] + fold(total)
                now[i, n] = stack(value)
                if k == CHUNK - 1:
                    new_state[i] = value
                if i == levels - 1:
                    leaving[k] = value
                    for later in range(n, first + CHUNK):
                        above[later] += fold(apply(now[i, n], *feedback[later - n]))

    chunk = place[0]
    for choice in choices:
        pl.when(chunk == choice)(functools.partial(chunk_of, choice))

    @pl.when(functools.reduce(jnp.logical_and, [chunk != choice for choice in choices]))
    def _():
        new_state[...] = state[...]
        leaving[...] = jnp.zeros_like(leaving)


def stage(choices, chunk, weights, kept, state, entering, earlier):
    vmem = pl.BlockSpec(memory_space=pltpu.VMEM)
    weights = [pin(w) for w in weights]
    return pl.pallas_call(
        functools.partial(stage_kernel, choices),
        out_shape=[
            jax.ShapeDtypeStruct(state.shape, F32),
            jax.ShapeDtypeStruct(entering.shape, F32),
        ],
        in_specs=[pl.BlockSpec(memory_space=pltpu.SMEM)] + [vmem] * 9,
        out_specs=[vmem] * 2,
        compiler_params=pltpu.CompilerParams(vmem_limit_bytes=24 * 2**20),
        name="stage",
    )(chunk, *weights, kept, state, entering, earlier)


def local(inverse_diag, down_block, up_block, reward):
    levels, given, phases = reward.shape
    columns = -(-given // 16) * 16
    reward = jnp.pad(reward, ((0, 0), (0, columns - given), (0, 0)))
    count = lax.axis_size("lvl")
    place = lax.axis_index("lvl")
    *weights, kept = prepare(inverse_diag, down_block, up_block, reward)
    kept = lax.ppermute(kept, "lvl", [(d + 1, d) for d in range(count - 1)])
    state = jnp.zeros_like(reward)
    entering = jnp.zeros((CHUNK, columns, phases), F32)
    leaving = entering
    stages = count + CHUNKS - 1
    for step in range(stages):
        choices = [c for c in range(CHUNKS) if 0 <= step - c < count]
        chunk = jnp.reshape(step - place, (1,)).astype(jnp.int32)
        state, leaving_now = stage(choices, chunk, weights, kept, state, entering, leaving)
        leaving = leaving_now
        if step < stages - 1:
            entering = lax.ppermute(leaving, "lvl", [(d, d + 1) for d in range(count - 1)])
    return state[:, :given]


def solution(mesh):
    placed = (
        P(("grp", "lvl"), None, None),
        P(("grp", "lvl"), None, None),
        P(("grp", "lvl"), None, None),
        P(("grp", "lvl"), "col", None),
    )
    return jax.shard_map(
        local, mesh=mesh, in_specs=placed, out_specs=P(("grp", "lvl"), "col", None), check_vma=False
    )
```

```python
import functools

import jax
import jax.numpy as jnp
from jax import lax
from jax.experimental import pallas as pl
from jax.experimental.pallas import tpu as pltpu
from jax.sharding import PartitionSpec as P

SWEEPS = 8
CHUNK = 4
CHUNKS = SWEEPS // CHUNK
AHEAD = SWEEPS - 1
SOON = CHUNK - 1
F32 = jnp.float32
BF16 = jnp.bfloat16


def resident(shape, dtype):
    return pltpu.VMEM(shape, dtype)


def pin(x, memory=pltpu.VMEM):
    return pltpu.with_memory_space_constraint(x, memory)


def split(x):
    high = x.astype(BF16)
    return high, (x - high.astype(F32)).astype(BF16)


def dot(a, b):
    return jnp.dot(a, b, preferred_element_type=F32)


def dot_nt(a, b):
    return lax.dot_general(a, b, (((1,), (1,)), ((), ())), preferred_element_type=F32)


def dot_parts(a, b, dot=dot):
    return dot(a[0], b[0]) + (dot(a[0], b[1]) + dot(a[1], b[0]))


def response(first, last, x_high, x_low, a_high, a_low, b_high, b_low, base, kept):
    phases = base.shape[2]
    columns = base.shape[1]
    rows = phases + columns

    def store(i, new):
        top = new[0:phases]
        end = new[phases:rows] + base[i]
        x_high[i, 0:phases], x_low[i, 0:phases] = split(top)
        x_high[i, phases:rows], x_low[i, phases:rows] = split(end)
        return top, end

    def from_below(i):
        return dot_parts((x_high[i - 1], x_low[i - 1]), (a_high[i], a_low[i]))

    def from_above(i):
        return dot_parts((x_high[i + 1], x_low[i + 1]), (b_high[i], b_low[i]))

    for n in range(first, last):
        if n == 0:
            x_high[0, 0:phases], x_low[0, 0:phases] = a_high[0], a_low[0]
            x_high[0, phases:rows], x_low[0, phases:rows] = split(base[0])
            kept[0, 0:phases] = a_high[0].astype(F32) + a_low[0].astype(F32)
            kept[0, phases:rows] = base[0]
        else:
            kept[n - first, 0:phases], kept[n - first, phases:rows] = store(0, from_above(0))

        def level(i, _, n=n):
            store(i, from_below(i) if n == 0 else from_below(i) + from_above(i))
            return 0

        lax.fori_loop(1, AHEAD - n, level, 0)


def prepare_kernel(
    inv_hbm, down_hbm, up_hbm, reward,
    a_high, a_low, b_high, b_low, base, x_high, x_low, kept,
    inv, down, up, sems,
):
    levels = inv.shape[0]

    def copies(i):
        return [
            pltpu.make_async_copy(source.at[i], target.at[i], sems.at[n, i])
            for n, (source, target) in enumerate(((inv_hbm, inv), (down_hbm, down), (up_hbm, up)))
        ]

    for i in range(levels):
        for copy in copies(i):
            copy.start()

    def products(i, _):
        for copy in copies(i):
            copy.wait()
        here = split(inv[i])
        a_high[i], a_low[i] = split(dot_parts(here, split(down[i])).T)
        b_high[i], b_low[i] = split(dot_parts(here, split(up[i])).T)
        base[i] = dot_parts(split(reward[i]), here, dot_nt)
        return 0

    lax.fori_loop(0, levels, products, 0, unroll=2)
    response(0, SOON, x_high, x_low, a_high, a_low, b_high, b_low, base, kept)


VMEM = pl.BlockSpec(memory_space=pltpu.VMEM)


def prepare(inverse_diag, down_block, up_block, reward):
    levels, phases, _ = inverse_diag.shape
    columns = reward.shape[1]
    matrix = (levels, phases, phases)
    assert levels >= AHEAD
    return pl.pallas_call(
        prepare_kernel,
        out_shape=[resident(matrix, BF16)] * 4
        + [resident((levels, columns, phases), F32)]
        + [resident((AHEAD, phases + columns, phases), BF16)] * 2
        + [resident((SOON, phases + columns, phases), F32)],
        in_specs=[pl.BlockSpec(memory_space=pltpu.HBM)] * 3 + [VMEM],
        out_specs=[VMEM] * 8,
        scratch_shapes=[pltpu.VMEM(matrix, F32)] * 3 + [pltpu.SemaphoreType.DMA((3, levels))],
        compiler_params=pltpu.CompilerParams(vmem_limit_bytes=24 * 2**20),
        name="prepare",
    )(*[pin(x, pltpu.HBM) for x in (inverse_diag, down_block, up_block)], reward)


def prepare_rest_kernel(a_high, a_low, b_high, b_low, base, given_high, given_low, kept, x_high, x_low):
    x_high[...] = given_high[...]
    x_low[...] = given_low[...]
    response(SOON, AHEAD, x_high, x_low, a_high, a_low, b_high, b_low, base, kept)


def prepare_rest(weights, x_high, x_low):
    _, rows, phases = x_high.shape
    return pl.pallas_call(
        prepare_rest_kernel,
        out_shape=resident((AHEAD - SOON, rows, phases), F32),
        in_specs=[VMEM] * 7,
        out_specs=VMEM,
        scratch_shapes=[pltpu.VMEM(x_high.shape, BF16)] * 2,
        compiler_params=pltpu.CompilerParams(vmem_limit_bytes=16 * 2**20),
        cost_estimate=pl.CostEstimate(flops=10**10, bytes_accessed=2**24, transcendentals=0),
        name="prepare_rest",
    )(*[pin(w) for w in (*weights, x_high, x_low)])


def stack(x):
    high = x.astype(BF16).astype(F32)
    return jnp.concatenate([high, x - high], axis=0).astype(BF16)


def fold(total):
    half = total.shape[0] // 2
    return total[:half] + total[half:]


def apply(x, high, low):
    return dot(x, high) + dot(x, low)


def stage_kernel(step, choices, has_past, has_soon, has_late, *refs):
    a_high, a_low, b_high, b_low, base, kept_soon = refs[:6]
    rest = list(refs[6:])
    kept_late = rest.pop(0) if has_late else None
    state, earlier = (rest.pop(0), rest.pop(0)) if has_past else (None, None)
    entering = rest.pop(0) if has_soon else None
    new_state, leaving = rest
    levels, columns, phases = base.shape

    def kept(j):
        return kept_soon.at[j] if j < SOON else kept_late.at[j - SOON]

    def chunk_of(chunk):
        first = chunk * CHUNK
        feedback = {j: split(kept(j)[0:phases]) for j in range(first + CHUNK - 1)}
        above = {}
        for n in range(max(first, 1), first + CHUNK):
            above[n] = kept(n - 1)[phases : phases + columns]
        past = {n: stack(earlier[n - first + CHUNK - 1]) for n in range(1, first + 1)}
        for j in range(first + CHUNK - 1) if first else ():
            pairs = [(n, n - j) for n in above if n - j in past]
            if pairs:
                total = apply(jnp.concatenate([past[m] for _, m in pairs], axis=0), *feedback[j])
                for p, (n, _) in enumerate(pairs):
                    above[n] += fold(total[p * 2 * columns : (p + 1) * 2 * columns])

        now = {}
        if first:
            for i in range(levels):
                now[i, first] = stack(state[i])
        if has_soon:
            for k in range(CHUNK):
                now[-1, first + 1 + k] = stack(entering[k])
        for turn in range(levels + 2 * (CHUNK - 1)):
            for k in range(CHUNK):
                i = turn - 2 * k
                if not 0 <= i < levels:
                    continue
                n = first + 1 + k
                value = base[i]
                if (i - 1, n) in now:
                    value += fold(apply(now[i - 1, n], a_high[i], a_low[i]))
                if n > 1:
                    over = stack(above[n - 1]) if i == levels - 1 else now[i + 1, n - 1]
                    value += fold(apply(over, b_high[i], b_low[i]))
                now[i, n] = stack(value)
                if k == CHUNK - 1:
                    new_state[i] = value
                if i == levels - 1:
                    leaving[k] = value
                    for later in range(n, first + CHUNK):
                        above[later] += fold(apply(now[i, n], *feedback[later - n]))

    chunk = step - lax.axis_index("lvl")
    for choice in choices:
        pl.when(chunk == choice)(functools.partial(chunk_of, choice))

    @pl.when(functools.reduce(jnp.logical_and, [chunk != choice for choice in choices]))
    def _():
        new_state[...] = state[...] if has_past else jnp.zeros_like(new_state)
        leaving[...] = jnp.zeros_like(leaving)


def stage(step, choices, weights, kept_soon, kept_late, past, entering, last):
    levels, columns, phases = weights[-1].shape
    operands = [*weights, kept_soon]
    if kept_late is not None:
        operands.append(kept_late)
    if past is not None:
        operands.extend(past)
    if entering is not None:
        operands.append(entering)
    return pl.pallas_call(
        functools.partial(
            stage_kernel, step, choices, past is not None, entering is not None, kept_late is not None
        ),
        out_shape=[
            (jax.ShapeDtypeStruct if last else resident)((levels, columns, phases), F32),
            resident((CHUNK, columns, phases), F32),
        ],
        in_specs=[VMEM] * len(operands),
        out_specs=[VMEM] * 2,
        compiler_params=pltpu.CompilerParams(vmem_limit_bytes=16 * 2**20),
        name="stage",
    )(*[pin(x) for x in operands])


def local(inverse_diag, down_block, up_block, reward):
    given = reward.shape[1]
    columns = -(-given // 16) * 16
    if columns != given:
        reward = jnp.pad(reward, ((0, 0), (0, columns - given), (0, 0)))
    count = lax.axis_size("lvl")
    downward = [(d + 1, d) for d in range(count - 1)]
    upward = [(d, d + 1) for d in range(count - 1)]
    *weights, x_high, x_low, kept_soon = prepare(inverse_diag, down_block, up_block, reward)
    kept_soon = lax.ppermute(kept_soon, "lvl", downward)
    late_here = prepare_rest(weights, x_high, x_low)
    kept_soon, late_here = lax.optimization_barrier((kept_soon, late_here))
    kept_late = lax.ppermute(late_here, "lvl", downward)
    past = entering = None
    stages = count + CHUNKS - 1
    for step in range(stages):
        choices = [c for c in range(CHUNKS) if 0 <= step - c < count]
        late = kept_late if step else None
        state, leaving = past = stage(step, choices, weights, kept_soon, late, past, entering, step == stages - 1)
        if step < stages - 1:
            entering = lax.ppermute(leaving, "lvl", upward)
    return state[:, :given] if columns != given else state


def solution(mesh):
    placed = (
        P(("grp", "lvl"), None, None),
        P(("grp", "lvl"), None, None),
        P(("grp", "lvl"), None, None),
        P(("grp", "lvl"), "col", None),
    )
    return jax.shard_map(
        local, mesh=mesh, in_specs=placed, out_specs=P(("grp", "lvl"), "col", None), check_vma=False
    )
```

```python
import functools

import jax
import jax.numpy as jnp
from jax import lax
from jax.experimental import pallas as pl
from jax.experimental.pallas import tpu as pltpu
from jax.sharding import PartitionSpec as P

SWEEPS = 8
CHUNK = 4
CHUNKS = SWEEPS // CHUNK
AHEAD = SWEEPS - 1
SOON = CHUNK - 1
F32 = jnp.float32
BF16 = jnp.bfloat16


def resident(shape, dtype):
    return pltpu.VMEM(shape, dtype)


def pin(x, memory=pltpu.VMEM):
    return pltpu.with_memory_space_constraint(x, memory)


def split(x):
    high = x.astype(BF16)
    return high, (x - high.astype(F32)).astype(BF16)


def dot(a, b):
    return jnp.dot(a, b, preferred_element_type=F32)


def dot_nt(a, b):
    return lax.dot_general(a, b, (((1,), (1,)), ((), ())), preferred_element_type=F32)


def dot_parts(a, b, dot=dot):
    return dot(a[0], b[0]) + (dot(a[0], b[1]) + dot(a[1], b[0]))


def response(first, last, x_high, x_low, a_high, a_low, b_high, b_low, base, kept):
    _, columns, phases = base.shape
    rows = phases + columns

    def store(i, new):
        top = new[0:phases]
        end = new[phases:rows] + base[i]
        x_high[i, 0:phases], x_low[i, 0:phases] = split(top)
        x_high[i, phases:rows], x_low[i, phases:rows] = split(end)
        return top, end

    def from_below(i):
        return dot_parts((x_high[i - 1], x_low[i - 1]), (a_high[i], a_low[i]))

    def from_above(i):
        return dot_parts((x_high[i + 1], x_low[i + 1]), (b_high[i], b_low[i]))

    for d in range(first, last):
        if d == 0:
            x_high[0, 0:phases], x_low[0, 0:phases] = a_high[0], a_low[0]
            x_high[0, phases:rows], x_low[0, phases:rows] = split(base[0])
            kept[0, 0:phases] = a_high[0].astype(F32) + a_low[0].astype(F32)
            kept[0, phases:rows] = base[0]
            continue
        store(d, from_below(d))

        def level(k, _, d=d):
            i = d - k
            store(i, from_below(i) + from_above(i))
            return 0

        lax.fori_loop(1, d, level, 0)
        kept[d - first, 0:phases], kept[d - first, phases:rows] = store(0, from_above(0))


def products(levels, hbm, reward, a_high, a_low, b_high, b_low, base, buffers, sems):
    def copies(i):
        return [
            pltpu.make_async_copy(source.at[i], target.at[i - levels[0]], sems.at[n, i - levels[0]])
            for n, (source, target) in enumerate(zip(hbm, buffers))
        ]

    for i in levels:
        for copy in copies(i):
            copy.start()

    inv, down, up = buffers
    for i in levels:
        for copy in copies(i):
            copy.wait()
        at = i - levels[0]
        here = split(inv[at])
        a_high[i], a_low[i] = split(dot_parts(here, split(down[at])).T)
        b_high[i], b_low[i] = split(dot_parts(here, split(up[at])).T)
        base[i] = dot_parts(split(reward[i]), here, dot_nt)


def prepare_kernel(
    inv, down, up, reward, a_high, a_low, b_high, b_low, base, x_high, x_low, kept, *scratch
):
    *buffers, sems = scratch
    products(range(SOON), (inv, down, up), reward, a_high, a_low, b_high, b_low, base, buffers, sems)
    response(0, SOON, x_high, x_low, a_high, a_low, b_high, b_low, base, kept)


def prepare_rest_kernel(
    inv, down, up, reward, a_high_soon, a_low_soon, b_high_soon, b_low_soon, base_soon, x_high_soon, x_low_soon,
    a_high, a_low, b_high, b_low, base, kept, x_high, x_low, *scratch
):
    *buffers, sems = scratch
    levels = reward.shape[0]
    for target, source in (
        (a_high, a_high_soon), (a_low, a_low_soon), (b_high, b_high_soon), (b_low, b_low_soon),
        (base, base_soon), (x_high, x_high_soon), (x_low, x_low_soon),
    ):
        target[0:SOON] = source[...]
    products(range(SOON, levels), (inv, down, up), reward, a_high, a_low, b_high, b_low, base, buffers, sems)
    response(SOON, AHEAD, x_high, x_low, a_high, a_low, b_high, b_low, base, kept)


VMEM = pl.BlockSpec(memory_space=pltpu.VMEM)
HBM = pl.BlockSpec(memory_space=pltpu.HBM)


def operators(levels, columns, phases):
    matrix = (levels, phases, phases)
    return [resident(matrix, BF16)] * 4 + [resident((levels, columns, phases), F32)]


def buffers(levels, phases):
    return [pltpu.VMEM((levels, phases, phases), F32)] * 3 + [pltpu.SemaphoreType.DMA((3, levels))]


def prepare(inverse_diag, down_block, up_block, reward):
    levels, columns, phases = reward.shape
    assert levels >= AHEAD
    rows = phases + columns
    given = [pin(x, pltpu.HBM) for x in (inverse_diag, down_block, up_block)] + [pin(reward)]
    *soon, kept_soon = pl.pallas_call(
        prepare_kernel,
        out_shape=operators(SOON, columns, phases)
        + [resident((SOON, rows, phases), BF16)] * 2
        + [resident((SOON, rows, phases), F32)],
        in_specs=[HBM] * 3 + [VMEM],
        out_specs=[VMEM] * 8,
        scratch_shapes=buffers(SOON, phases),
        compiler_params=pltpu.CompilerParams(vmem_limit_bytes=16 * 2**20),
        name="prepare",
    )(*given)
    *weights, kept_late = pl.pallas_call(
        prepare_rest_kernel,
        out_shape=operators(levels, columns, phases) + [resident((AHEAD - SOON, rows, phases), F32)],
        in_specs=[HBM] * 3 + [VMEM] * 8,
        out_specs=[VMEM] * 6,
        scratch_shapes=[pltpu.VMEM((AHEAD, rows, phases), BF16)] * 2 + buffers(levels - SOON, phases),
        compiler_params=pltpu.CompilerParams(vmem_limit_bytes=24 * 2**20),
        cost_estimate=pl.CostEstimate(flops=10**10, bytes_accessed=2**24, transcendentals=0),
        name="prepare_rest",
    )(*given, *[pin(x) for x in soon])
    return weights, kept_soon, kept_late


def stack(x):
    high = x.astype(BF16).astype(F32)
    return jnp.concatenate([high, x - high], axis=0).astype(BF16)


def fold(total):
    half = total.shape[0] // 2
    return total[:half] + total[half:]


def apply(x, high, low):
    return dot(x, high) + dot(x, low)


def kept_at(soon, late, j):
    return soon[j] if j < SOON else late[j - SOON]


def carried(soon, late, past, first, last):
    phases = soon.shape[2]
    above = {n: kept_at(soon, late, n - 1)[phases:] for n in range(max(first, 1), last + 1)}
    columns = soon.shape[1] - phases
    for j in range(last) if past else ():
        pairs = [(n, n - j) for n in above if n - j in past]
        if pairs:
            total = apply(
                jnp.concatenate([past[m] for _, m in pairs], axis=0), *split(kept_at(soon, late, j)[0:phases])
            )
            for p, (n, _) in enumerate(pairs):
                above[n] += fold(total[p * 2 * columns : (p + 1) * 2 * columns])
    return above


def stage_kernel(step, choices, names, *refs):
    a_high, a_low, b_high, b_low, base = refs[:5]
    given = dict(zip(names, refs[5:]))
    new_state, leaving = refs[5 + len(names) :]
    levels, columns, phases = base.shape
    soon = given["soon"]

    def chunk_of(chunk):
        first = chunk * CHUNK
        feedback = [split(soon[j, 0:phases]) for j in range(SOON)]
        if not first:
            above = carried(soon, None, {}, first, first + CHUNK - 1)
        elif "late" in given:
            past = {n + 1: stack(given["earlier"][n]) for n in range(first)}
            above = carried(soon, given["late"], past, first, first + CHUNK - 1)
        else:
            above = {first + k: given["returned"][k] if "returned" in given else 0.0 for k in range(CHUNK)}

        now = {}
        if first:
            for i in range(levels):
                now[i, first] = stack(given["state"][i])
        if "entering" in given:
            for k in range(CHUNK):
                now[-1, first + 1 + k] = stack(given["entering"][k])
        for turn in range(levels + 2 * (CHUNK - 1)):
            for k in range(CHUNK):
                i = turn - 2 * k
                if not 0 <= i < levels:
                    continue
                n = first + 1 + k
                value = base[i]
                if (i - 1, n) in now:
                    value += fold(apply(now[i - 1, n], a_high[i], a_low[i]))
                if n > 1:
                    over = stack(above[n - 1] + jnp.zeros_like(value)) if i == levels - 1 else now[i + 1, n - 1]
                    value += fold(apply(over, b_high[i], b_low[i]))
                now[i, n] = stack(value)
                if k == CHUNK - 1:
                    new_state[i] = value
                if i == levels - 1:
                    leaving[k] = value
                    for later in range(n, first + CHUNK):
                        above[later] += fold(apply(now[i, n], *feedback[later - n]))

    chunk = step - lax.axis_index("lvl")
    for choice in choices:
        pl.when(chunk == choice)(functools.partial(chunk_of, choice))

    @pl.when(functools.reduce(jnp.logical_and, [chunk != choice for choice in choices]))
    def _():
        new_state[...] = given["state"][...] if "state" in given else jnp.zeros_like(new_state)
        leaving[...] = jnp.zeros_like(leaving)


def stage(step, choices, weights, given, last):
    levels, columns, phases = weights[-1].shape
    given = {name: x for name, x in given.items() if x is not None}
    return pl.pallas_call(
        functools.partial(stage_kernel, step, choices, tuple(given)),
        out_shape=[
            (jax.ShapeDtypeStruct if last else resident)((levels, columns, phases), F32),
            resident((CHUNK, columns, phases), F32),
        ],
        in_specs=[VMEM] * (len(weights) + len(given)),
        out_specs=[VMEM] * 2,
        compiler_params=pltpu.CompilerParams(vmem_limit_bytes=16 * 2**20),
        name="stage",
    )(*[pin(x) for x in (*weights, *given.values())])


def answer_kernel(step, soon, late, entering, returned):
    @pl.when(lax.axis_index("lvl") == step)
    def _():
        past = {n + 1: stack(entering[n]) for n in range(CHUNK)}
        above = carried(soon, late, past, CHUNK, 2 * CHUNK - 1)
        for k in range(CHUNK):
            returned[k] = above[CHUNK + k]

    @pl.when(lax.axis_index("lvl") != step)
    def _():
        returned[...] = jnp.zeros_like(returned)


def answer(step, soon, late, entering):
    return pl.pallas_call(
        functools.partial(answer_kernel, step),
        out_shape=resident(entering.shape, F32),
        in_specs=[VMEM] * 3,
        out_specs=VMEM,
        compiler_params=pltpu.CompilerParams(vmem_limit_bytes=8 * 2**20),
        name="answer",
    )(*[pin(x) for x in (soon, late, entering)])


def local(inverse_diag, down_block, up_block, reward):
    given = reward.shape[1]
    columns = -(-given // 16) * 16
    if columns != given:
        reward = jnp.pad(reward, ((0, 0), (0, columns - given), (0, 0)))
    count = lax.axis_size("lvl")
    assert CHUNKS == 2
    weights, soon_here, late_here = prepare(inverse_diag, down_block, up_block, reward)
    soon = lax.ppermute(soon_here, "lvl", [(d + 1, d) for d in range(count - 1)])
    soon, late_sent = lax.optimization_barrier((soon, late_here))
    late = lax.ppermute(late_sent, "lvl", [(d + 1, d) for d in range(0, count - 1, 2)])
    state = leaving = entering = None
    stages = count + CHUNKS - 1
    for step in range(stages):
        returned = None
        if step % 2 == 0 and 0 < step < count:
            returned = lax.ppermute(answer(step, soon_here, late_here, entering), "lvl", [(step, step - 1)])
        choices = [c for c in range(CHUNKS) if 0 <= step - c < count]
        state, leaving = stage(
            step,
            choices,
            weights,
            {
                "soon": soon,
                "late": late if step % 2 else None,
                "returned": returned,
                "state": state,
                "earlier": leaving if step % 2 else None,
                "entering": entering,
            },
            step == stages - 1,
        )
        if step < stages - 1:
            entering = lax.ppermute(leaving, "lvl", [(d, d + 1) for d in range(count - 1)])
    return state[:, :given] if columns != given else state


def solution(mesh):
    placed = (
        P(("grp", "lvl"), None, None),
        P(("grp", "lvl"), None, None),
        P(("grp", "lvl"), None, None),
        P(("grp", "lvl"), "col", None),
    )
    return jax.shard_map(
        local, mesh=mesh, in_specs=placed, out_specs=P(("grp", "lvl"), "col", None), check_vma=False
    )
```

```python
import functools

import jax
import jax.numpy as jnp
from jax import lax
from jax.experimental import pallas as pl
from jax.experimental.pallas import tpu as pltpu
from jax.sharding import PartitionSpec as P

SWEEPS = 8
CHUNK = 4
CHUNKS = SWEEPS // CHUNK
AHEAD = SWEEPS - 1
SOON = CHUNK - 1
F32 = jnp.float32
BF16 = jnp.bfloat16


def resident(shape, dtype):
    return pltpu.VMEM(shape, dtype)


def pin(x, memory=pltpu.VMEM):
    return pltpu.with_memory_space_constraint(x, memory)


def split(x):
    high = x.astype(BF16)
    return high, (x - high.astype(F32)).astype(BF16)


def dot(a, b):
    return jnp.dot(a, b, preferred_element_type=F32)


def dot_nt(a, b):
    return lax.dot_general(a, b, (((1,), (1,)), ((), ())), preferred_element_type=F32)


def dot_parts(a, b):
    return dot(jnp.concatenate([a[0], a[0], a[1]], axis=1), jnp.concatenate([b[0], b[1], b[0]], axis=0))


def place_operators(weight, i, down, up):
    phases = down.shape[0]
    for k, part in enumerate((*split(down.T), *split(up.T))):
        weight[i, k * phases : (k + 1) * phases] = part


def response(first, last, x_high, x_low, weight, base, kept):
    _, columns, phases = base.shape
    rows = phases + columns

    def store(i, new):
        top = new[0:phases]
        end = new[phases:rows] + base[i]
        x_high[i, 0:phases], x_low[i, 0:phases] = split(top)
        x_high[i, phases:rows], x_low[i, phases:rows] = split(end)
        return top, end

    def operator(i, k):
        high = weight[i, 2 * k * phases : (2 * k + 1) * phases]
        low = weight[i, (2 * k + 1) * phases : (2 * k + 2) * phases]
        return [high, low, high]

    def value(i):
        return [x_high[i], x_high[i], x_low[i]]

    def product(values, operators):
        return dot(jnp.concatenate(values, axis=1), jnp.concatenate(operators, axis=0))

    for d in range(first, last):
        if d == 0:
            high, low = weight[0, 0:phases], weight[0, phases : 2 * phases]
            x_high[0, 0:phases], x_low[0, 0:phases] = high, low
            x_high[0, phases:rows], x_low[0, phases:rows] = split(base[0])
            kept[0, 0:phases] = high.astype(F32) + low.astype(F32)
            kept[0, phases:rows] = base[0]
            continue
        store(d, product(value(d - 1), operator(d, 0)))

        def level(k, _, d=d):
            i = d - k
            store(i, product(value(i - 1) + value(i + 1), operator(i, 0) + operator(i, 1)))
            return 0

        lax.fori_loop(1, d, level, 0)
        kept[d - first, 0:phases], kept[d - first, phases:rows] = store(0, product(value(1), operator(0, 1)))


def products(levels, given, weight, base, buffers, sems):
    first = levels[0]

    def copies(i):
        return [
            pltpu.make_async_copy(source.at[i], target.at[i - first], sems.at[n, i - first])
            for n, (source, target) in enumerate(zip(given, buffers))
        ]

    for i in levels:
        for copy in copies(i):
            copy.start()

    inv, down, up, pay = buffers
    for i in levels:
        for copy in copies(i):
            copy.wait()
        at = i - first
        here = split(inv[at])
        place_operators(weight, i, dot_parts(here, split(down[at])), dot_parts(here, split(up[at])))
        high, low = split(pay[at])
        base[i] = dot_nt(high, here[0]) + (dot_nt(high, here[1]) + dot_nt(low, here[0]))


def prepare_kernel(inv, down, up, reward, weight, base, x_high, x_low, kept, *scratch):
    *buffers, sems = scratch
    products(range(SOON), (inv, down, up, reward), weight, base, buffers, sems)
    response(0, SOON, x_high, x_low, weight, base, kept)


def prepare_rest_kernel(inv, down, up, reward, weight_soon, base_soon, weight, base, *scratch):
    *buffers, sems = scratch
    levels = reward.shape[0]
    weight[0:SOON] = weight_soon[...]
    base[0:SOON] = base_soon[...]
    products(range(SOON, levels), (inv, down, up, reward), weight, base, buffers, sems)


def respond_kernel(weight, base, x_high_soon, x_low_soon, kept, x_high, x_low):
    @pl.when(lax.axis_index("lvl") > 0)
    def _():
        x_high[0:SOON] = x_high_soon[...]
        x_low[0:SOON] = x_low_soon[...]
        response(SOON, AHEAD, x_high, x_low, weight, base, kept)


VMEM = pl.BlockSpec(memory_space=pltpu.VMEM)
HBM = pl.BlockSpec(memory_space=pltpu.HBM)


def operators(levels, columns, phases):
    return [resident((levels, 4 * phases, phases), BF16), resident((levels, columns, phases), F32)]


def buffers(levels, columns, phases):
    return (
        [pltpu.VMEM((levels, phases, phases), F32)] * 3
        + [pltpu.VMEM((levels, columns, phases), F32)]
        + [pltpu.SemaphoreType.DMA((4, levels))]
    )


def prepare(inverse_diag, down_block, up_block, reward):
    levels, columns, phases = reward.shape
    assert levels >= AHEAD
    rows = phases + columns
    given = [pin(x, pltpu.HBM) for x in (inverse_diag, down_block, up_block, reward)]
    *soon, kept_soon = pl.pallas_call(
        prepare_kernel,
        out_shape=operators(SOON, columns, phases)
        + [resident((SOON, rows, phases), BF16)] * 2
        + [resident((SOON, rows, phases), F32)],
        in_specs=[HBM] * 4,
        out_specs=[VMEM] * 5,
        scratch_shapes=buffers(SOON, columns, phases),
        compiler_params=pltpu.CompilerParams(vmem_limit_bytes=16 * 2**20),
        name="prepare",
    )(*given)
    weights = pl.pallas_call(
        prepare_rest_kernel,
        out_shape=operators(levels, columns, phases),
        in_specs=[HBM] * 4 + [VMEM] * 2,
        out_specs=[VMEM] * 2,
        scratch_shapes=buffers(levels - SOON, columns, phases),
        compiler_params=pltpu.CompilerParams(vmem_limit_bytes=16 * 2**20),
        name="prepare_rest",
    )(*given, *[pin(x) for x in soon[:2]])
    return weights, soon[2:], kept_soon


def respond(weights, started):
    _, rows, phases = started[0].shape
    return pl.pallas_call(
        respond_kernel,
        out_shape=resident((AHEAD - SOON, rows, phases), F32),
        in_specs=[VMEM] * 4,
        out_specs=VMEM,
        scratch_shapes=[pltpu.VMEM((AHEAD, rows, phases), BF16)] * 2,
        compiler_params=pltpu.CompilerParams(vmem_limit_bytes=16 * 2**20),
        name="respond",
    )(*[pin(x) for x in (*weights, *started)])


def stack(x):
    high = x.astype(BF16).astype(F32)
    return jnp.concatenate([high, x - high], axis=0).astype(BF16)


def fold(total):
    half = total.shape[0] // 2
    return total[:half] + total[half:]


def apply(terms):
    values = jnp.concatenate([x for x, _ in terms for _ in range(2)], axis=1)
    return fold(dot(values, jnp.concatenate([operator for _, operator in terms], axis=0)))


def whole(operator):
    return jnp.concatenate(split(operator), axis=0)


def kept_at(soon, late, j):
    return soon[j] if j < SOON else late[j - SOON]


def carried(soon, late, past, first, last):
    phases = soon.shape[2]
    above = {n: kept_at(soon, late, n - 1)[phases:] for n in range(max(first, 1), last + 1)}
    for j in range(last) if past else ():
        pairs = [(n, n - j) for n in above if n - j in past]
        for n, m in pairs:
            above[n] += apply([(past[m], whole(kept_at(soon, late, j)[0:phases]))])
    return above


def chunk_kernel(chunk, place, names, *refs):
    given = dict(zip(names, refs))
    new_state, leaving = refs[len(names) :]
    weight, base, soon = given["weight"], given["base"], given["soon"]
    levels, columns, phases = base.shape
    first = chunk * CHUNK

    @pl.when(lax.axis_index("lvl") != place)
    def _():
        for name, target in (("state", new_state), ("leaving", leaving)):
            target[...] = given[name][...] if name in given else jnp.zeros_like(target)

    @pl.when(lax.axis_index("lvl") == place)
    def _():
        feedback = [whole(soon[j, 0:phases]) for j in range(SOON)]
        if not first:
            above = carried(soon, None, {}, first, first + CHUNK - 1)
        elif "late" in given:
            past = {n + 1: stack(given["earlier"][n]) for n in range(first)}
            above = carried(soon, given["late"], past, first, first + CHUNK - 1)
        else:
            zero = jnp.zeros((columns, phases), F32)
            above = {first + k: given["returned"][k] if "returned" in given else zero for k in range(CHUNK)}

        now = {}
        if first:
            for i in range(levels):
                now[i, first] = stack(given["state"][i])
        if "entering" in given:
            for k in range(CHUNK):
                now[-1, first + 1 + k] = stack(given["entering"][k])
        for turn in range(levels + 2 * (CHUNK - 1)):
            for k in range(CHUNK):
                i = turn - 2 * k
                if not 0 <= i < levels:
                    continue
                n = first + 1 + k
                terms = []
                if (i - 1, n) in now:
                    terms.append((now[i - 1, n], weight[i, 0 : 2 * phases]))
                if n > 1:
                    over = stack(above[n - 1]) if i == levels - 1 else now[i + 1, n - 1]
                    terms.append((over, weight[i, 2 * phases : 4 * phases]))
                value = base[i] + apply(terms) if terms else base[i]
                now[i, n] = stack(value)
                if k == CHUNK - 1:
                    new_state[i] = value
                if i == levels - 1:
                    leaving[k] = value
                    for later in range(n, first + CHUNK):
                        above[later] += apply([(now[i, n], feedback[later - n])])


def run_chunk(chunk, place, given, last=False):
    given = {name: x for name, x in given.items() if x is not None}
    names = tuple(given)
    levels, columns, phases = given["base"].shape
    return pl.pallas_call(
        functools.partial(chunk_kernel, chunk, place, names),
        out_shape=[
            (jax.ShapeDtypeStruct if last else resident)((levels, columns, phases), F32),
            resident((CHUNK, columns, phases), F32),
        ],
        in_specs=[VMEM] * len(given),
        out_specs=[VMEM] * 2,
        compiler_params=pltpu.CompilerParams(vmem_limit_bytes=16 * 2**20),
        name="chunk",
    )(*[pin(x) for x in given.values()])


def answer_kernel(step, soon, late, entering, returned):
    @pl.when(lax.axis_index("lvl") == step)
    def _():
        past = {n + 1: stack(entering[n]) for n in range(CHUNK)}
        above = carried(soon, late, past, CHUNK, 2 * CHUNK - 1)
        for k in range(CHUNK):
            returned[k] = above[CHUNK + k]


def answer(step, soon, late, entering):
    return pl.pallas_call(
        functools.partial(answer_kernel, step),
        out_shape=resident(entering.shape, F32),
        in_specs=[VMEM] * 3,
        out_specs=VMEM,
        compiler_params=pltpu.CompilerParams(vmem_limit_bytes=8 * 2**20),
        name="answer",
    )(*[pin(x) for x in (soon, late, entering)])


def local(inverse_diag, down_block, up_block, reward):
    given = reward.shape[1]
    columns = -(-given // 16) * 16
    if columns != given:
        reward = jnp.pad(reward, ((0, 0), (0, columns - given), (0, 0)))
    count = lax.axis_size("lvl")
    assert CHUNKS == 2
    weights, started, soon_here = prepare(inverse_diag, down_block, up_block, reward)
    late_here = respond(weights, started)
    upward = [(d, d + 1) for d in range(count - 1)]
    from_odd = [(d + 1, d) for d in range(0, count - 1, 2)]
    soon = lax.ppermute(soon_here, "lvl", [(d + 1, d) for d in range(count - 1)])
    soon, late_here = lax.optimization_barrier((soon, late_here))
    late = returned = entering = leaving = state = None
    for step in range(count + 1):
        earlier = leaving
        shared = {"weight": weights[0], "base": weights[1], "entering": entering}
        if step % 2 == 0 and 0 < step < count:
            returned = lax.ppermute(answer(step, soon_here, late_here, entering), "lvl", [(step, step - 1)])
        if step < count:
            own = {**shared, "soon": soon, "state": state}
            state, leaving = run_chunk(0, step, own)
        if step == 1:
            late_sent, entering = lax.optimization_barrier((late_here, entering))
            late = lax.ppermute(late_sent, "lvl", from_odd)
        if step > 0:
            own = {**shared, "soon": soon, "state": state, "leaving": leaving}
            if step % 2:
                own.update(late=late, earlier=earlier)
            elif step < count:
                own.update(returned=returned)
            state, leaving = run_chunk(1, step - 1, own, last=step == count)
        if step < count:
            entering = lax.ppermute(leaving, "lvl", upward)
    return state[:, :given] if columns != given else state


def solution(mesh):
    placed = (
        P(("grp", "lvl"), None, None),
        P(("grp", "lvl"), None, None),
        P(("grp", "lvl"), None, None),
        P(("grp", "lvl"), "col", None),
    )
    return jax.shard_map(
        local, mesh=mesh, in_specs=placed, out_specs=P(("grp", "lvl"), "col", None), check_vma=False
    )
```

```python
import functools

import jax
import jax.numpy as jnp
from jax import lax
from jax.experimental import pallas as pl
from jax.experimental.pallas import tpu as pltpu
from jax.sharding import PartitionSpec as P

SWEEPS = 8
CHUNK = 4
CHUNKS = SWEEPS // CHUNK
AHEAD = SWEEPS - 1
SOON = CHUNK - 1
F32 = jnp.float32
BF16 = jnp.bfloat16


def resident(shape, dtype):
    return pltpu.VMEM(shape, dtype)


def pin(x, memory=pltpu.VMEM):
    return pltpu.with_memory_space_constraint(x, memory)


def split(x):
    high = x.astype(BF16)
    return high, (x - high.astype(F32)).astype(BF16)


def dot(a, b):
    return jnp.dot(a, b, preferred_element_type=F32)


def dot_nt(a, b):
    return lax.dot_general(a, b, (((1,), (1,)), ((), ())), preferred_element_type=F32)


def dot_parts(a, b, dot=dot):
    return dot(a[0], b[0]) + (dot(a[0], b[1]) + dot(a[1], b[0]))


def place_operators(weight, i, down, up):
    phases = down.shape[0]
    for k, part in enumerate((*split(down.T), *split(up.T))):
        weight[i, k * phases : (k + 1) * phases] = part


def operator(weight, i, k):
    phases = weight.shape[2]
    at = 2 * k * phases
    return weight[i, at : at + phases], weight[i, at + phases : at + 2 * phases]


def response(first, last, x_high, x_low, weight, base, kept):
    _, columns, phases = base.shape
    rows = phases + columns

    def store(i, new):
        top = new[0:phases]
        end = new[phases:rows] + base[i]
        x_high[i, 0:phases], x_low[i, 0:phases] = split(top)
        x_high[i, phases:rows], x_low[i, phases:rows] = split(end)
        return top, end

    def from_below(i):
        return dot_parts((x_high[i - 1], x_low[i - 1]), operator(weight, i, 0))

    def from_above(i):
        return dot_parts((x_high[i + 1], x_low[i + 1]), operator(weight, i, 1))

    for d in range(first, last):
        if d == 0:
            high, low = weight[0, 0:phases], weight[0, phases : 2 * phases]
            x_high[0, 0:phases], x_low[0, 0:phases] = high, low
            x_high[0, phases:rows], x_low[0, phases:rows] = split(base[0])
            kept[0, 0:phases] = high.astype(F32) + low.astype(F32)
            kept[0, phases:rows] = base[0]
            continue
        store(d, from_below(d))

        def level(k, _, d=d):
            i = d - k
            store(i, from_below(i) + from_above(i))
            return 0

        lax.fori_loop(1, d, level, 0)
        kept[d - first, 0:phases], kept[d - first, phases:rows] = store(0, from_above(0))


def products(levels, given, weight, base, buffers, sems):
    first = levels[0]

    def copies(i):
        return [
            pltpu.make_async_copy(source.at[i], target.at[i - first], sems.at[n, i - first])
            for n, (source, target) in enumerate(zip(given, buffers))
        ]

    for i in levels:
        for copy in copies(i):
            copy.start()

    inv, down, up, pay = buffers
    for i in levels:
        for copy in copies(i):
            copy.wait()
        at = i - first
        here = split(inv[at])
        place_operators(weight, i, dot_parts(here, split(down[at])), dot_parts(here, split(up[at])))
        base[i] = dot_parts(split(pay[at]), here, dot_nt)


def prepare_kernel(inv, down, up, reward, weight, base, x_high, x_low, kept, *scratch):
    *buffers, sems = scratch
    products(range(SOON), (inv, down, up, reward), weight, base, buffers, sems)
    response(0, SOON, x_high, x_low, weight, base, kept)


def prepare_rest_kernel(inv, down, up, reward, weight_soon, base_soon, weight, base, *scratch):
    *buffers, sems = scratch
    levels = reward.shape[0]
    weight[0:SOON] = weight_soon[...]
    base[0:SOON] = base_soon[...]
    products(range(SOON, levels), (inv, down, up, reward), weight, base, buffers, sems)


def respond_kernel(weight, base, x_high_soon, x_low_soon, kept, x_high, x_low):
    @pl.when(lax.axis_index("lvl") > 0)
    def _():
        x_high[0:SOON] = x_high_soon[...]
        x_low[0:SOON] = x_low_soon[...]
        response(SOON, AHEAD, x_high, x_low, weight, base, kept)


VMEM = pl.BlockSpec(memory_space=pltpu.VMEM)
HBM = pl.BlockSpec(memory_space=pltpu.HBM)


def operators(levels, columns, phases):
    return [resident((levels, 4 * phases, phases), BF16), resident((levels, columns, phases), F32)]


def buffers(levels, columns, phases):
    return (
        [pltpu.VMEM((levels, phases, phases), F32)] * 3
        + [pltpu.VMEM((levels, columns, phases), F32)]
        + [pltpu.SemaphoreType.DMA((4, levels))]
    )


def prepare(inverse_diag, down_block, up_block, reward):
    levels, columns, phases = reward.shape
    assert levels >= AHEAD
    rows = phases + columns
    given = [pin(x, pltpu.HBM) for x in (inverse_diag, down_block, up_block, reward)]
    *soon, kept_soon = pl.pallas_call(
        prepare_kernel,
        out_shape=operators(SOON, columns, phases)
        + [resident((SOON, rows, phases), BF16)] * 2
        + [resident((SOON, rows, phases), F32)],
        in_specs=[HBM] * 4,
        out_specs=[VMEM] * 5,
        scratch_shapes=buffers(SOON, columns, phases),
        compiler_params=pltpu.CompilerParams(vmem_limit_bytes=16 * 2**20),
        name="prepare",
    )(*given)
    weights = pl.pallas_call(
        prepare_rest_kernel,
        out_shape=operators(levels, columns, phases),
        in_specs=[HBM] * 4 + [VMEM] * 2,
        out_specs=[VMEM] * 2,
        scratch_shapes=buffers(levels - SOON, columns, phases),
        compiler_params=pltpu.CompilerParams(vmem_limit_bytes=16 * 2**20),
        name="prepare_rest",
    )(*given, *[pin(x) for x in soon[:2]])
    return weights, soon[2:], kept_soon


def respond(weights, started):
    _, rows, phases = started[0].shape
    return pl.pallas_call(
        respond_kernel,
        out_shape=resident((AHEAD - SOON, rows, phases), F32),
        in_specs=[VMEM] * 4,
        out_specs=VMEM,
        scratch_shapes=[pltpu.VMEM((AHEAD, rows, phases), BF16)] * 2,
        compiler_params=pltpu.CompilerParams(vmem_limit_bytes=16 * 2**20),
        name="respond",
    )(*[pin(x) for x in (*weights, *started)])


def stack(x):
    high = x.astype(BF16).astype(F32)
    return jnp.concatenate([high, x - high], axis=0).astype(BF16)


def fold(total):
    half = total.shape[0] // 2
    return total[:half] + total[half:]


def apply(terms):
    values = jnp.concatenate([x for x, _ in terms for _ in range(2)], axis=1)
    return fold(dot(values, jnp.concatenate([operator for _, operator in terms], axis=0)))


def apply_each(values, operator, columns):
    phases = operator.shape[1]
    values = jnp.concatenate(values, axis=0) if len(values) > 1 else values[0]
    total = dot(values, operator[0:phases]) + dot(values, operator[phases:])
    return [fold(total[at : at + 2 * columns]) for at in range(0, total.shape[0], 2 * columns)]


def whole(operator):
    return jnp.concatenate(split(operator), axis=0)


def kept_at(soon, late, j):
    return soon[j] if j < SOON else late[j - SOON]


def carried(soon, late, past, first, last):
    phases = soon.shape[2]
    above = {n: kept_at(soon, late, n - 1)[phases:] for n in range(max(first, 1), last + 1)}
    columns = soon.shape[1] - phases
    for j in range(last) if past else ():
        pairs = [(n, n - j) for n in above if n - j in past]
        if pairs:
            terms = [past[m] for _, m in pairs]
            for (n, _), term in zip(pairs, apply_each(terms, whole(kept_at(soon, late, j)[0:phases]), columns)):
                above[n] += term
    return above


def wave(first, weight, base, now, above, feedback, due, emit):
    levels, _, phases = base.shape
    for turn in range(levels + 2 * (CHUNK - 1)):
        for k in range(CHUNK):
            i = turn - 2 * k
            if not (0 <= i < levels and due(i, k)):
                continue
            n = first + 1 + k
            terms = []
            if (i - 1, n) in now:
                terms.append((now[i - 1, n], weight[i, 0 : 2 * phases]))
            if n > 1:
                over = stack(above[n - 1]) if i == levels - 1 else now[i + 1, n - 1]
                terms.append((over, weight[i, 2 * phases : 4 * phases]))
            value = base[i] + apply(terms) if terms else base[i]
            now[i, n] = stack(value)
            emit(i, k, value)
            if i == levels - 1:
                for later in range(n, first + CHUNK):
                    above[later] += apply([(now[i, n], feedback[later - n])])


def edge_level(levels, k):
    return levels - 2 - k


def chunk_kernel(chunk, place, part, names, *refs):
    given = dict(zip(names, refs))
    new_state, leaving = refs[len(names) :]
    weight, base = given["weight"], given["base"]
    levels, columns, phases = base.shape
    first = chunk * CHUNK

    @pl.when(lax.axis_index("lvl") != place)
    def _():
        for name, target in (("state", new_state), ("leaving", leaving)):
            target[...] = given[name][...] if name in given else jnp.zeros_like(target)

    @pl.when(lax.axis_index("lvl") == place)
    def _():
        zero = jnp.zeros((columns, phases), F32)
        above, feedback = {first + k: zero for k in range(CHUNK)}, []
        if part != "early":
            soon = given["soon"]
            feedback = [whole(soon[j, 0:phases]) for j in range(SOON)]
            if not first:
                above = carried(soon, None, {}, first, first + CHUNK - 1)
            elif "late" in given:
                past = {n + 1: stack(given["earlier"][n]) for n in range(first)}
                above = carried(soon, given["late"], past, first, first + CHUNK - 1)
            elif "returned" in given:
                above = {first + k: given["returned"][k] for k in range(CHUNK)}

        now = {}
        if part == "late":
            for k in range(CHUNK):
                now[edge_level(levels, k), first + 1 + k] = stack(given["edge"][k])
            new_state[...] = given["state"][...]
        elif first:
            for i in range(levels):
                now[i, first] = stack(given["state"][i])
        if part != "late" and "entering" in given:
            for k in range(CHUNK):
                now[-1, first + 1 + k] = stack(given["entering"][k])

        def due(i, k):
            return part == "all" or (i <= edge_level(levels, k)) == (part == "early")

        def emit(i, k, value):
            if k == CHUNK - 1:
                new_state[i] = value
            if i == (edge_level(levels, k) if part == "early" else levels - 1):
                leaving[k] = value

        wave(first, weight, base, now, above, feedback, due, emit)


def run_chunk(chunk, place, given, part="all"):
    given = {name: x for name, x in given.items() if x is not None}
    levels, columns, phases = given["base"].shape
    return pl.pallas_call(
        functools.partial(chunk_kernel, chunk, place, part, tuple(given)),
        out_shape=[resident((levels, columns, phases), F32), resident((CHUNK, columns, phases), F32)],
        in_specs=[VMEM] * len(given),
        out_specs=[VMEM] * 2,
        compiler_params=pltpu.CompilerParams(vmem_limit_bytes=16 * 2**20),
        name="chunk",
    )(*[pin(x) for x in given.values()])


def among(places):
    return functools.reduce(jnp.logical_or, [lax.axis_index("lvl") == place for place in places])


def spread_kernel(places, weight, soon, out):
    levels, _, phases = weight.shape

    def get(at):
        return out[at, 0:phases], out[at, phases : 2 * phases]

    def put(at, value):
        out[at, 0:phases], out[at, phases : 2 * phases] = split(value)

    @pl.when(among(places))
    def _():
        out[0] = weight[0, 0 : 2 * phases]

        def up(i, _):
            put(i, dot_parts(get(i - 1), operator(weight, i, 0)))
            return 0

        lax.fori_loop(1, levels, up, 0)
        feedback = [split(soon[j, 0:phases]) for j in range(CHUNK - 1)]
        for a in range(1, CHUNK):
            at, old = a * levels, (a - 1) * levels
            put(at, dot_parts(get(old + 1), operator(weight, 0, 1)))

            def both(i, _, at=at, old=old):
                below = dot_parts(get(at + i - 1), operator(weight, i, 0))
                put(at + i, below + dot_parts(get(old + i + 1), operator(weight, i, 1)))
                return 0

            lax.fori_loop(1, levels - 1, both, 0)
            back = sum(dot_parts(get((a - 1 - j) * levels + levels - 1), feedback[j]) for j in range(a))
            top = levels - 1
            below = dot_parts(get(at + top - 1), operator(weight, top, 0))
            put(at + top, below + dot_parts(split(back), operator(weight, top, 1)))


def spread(places, weight, soon):
    levels, _, phases = weight.shape
    return pl.pallas_call(
        functools.partial(spread_kernel, places),
        out_shape=resident((CHUNK * levels, 2 * phases, phases), BF16),
        in_specs=[VMEM] * 2,
        out_specs=VMEM,
        compiler_params=pltpu.CompilerParams(vmem_limit_bytes=16 * 2**20),
        name="spread",
    )(*[pin(x) for x in (weight, soon)])


def finish_leaving_kernel(place, ways, entering, leaving, before, new):
    levels = ways.shape[0] // CHUNK
    columns = entering.shape[1]

    @pl.when(lax.axis_index("lvl") != place)
    def _():
        new[...] = before[...]

    @pl.when(lax.axis_index("lvl") == place)
    def _():
        values = [stack(entering[k]) for k in range(CHUNK)]
        total = [leaving[k] for k in range(CHUNK)]
        for a in range(CHUNK):
            for k, term in enumerate(apply_each(values[: CHUNK - a], ways[a * levels + levels - 1], columns)):
                total[a + k] += term
        for k in range(CHUNK):
            new[k] = total[k]


def finish_leaving(place, ways, entering, leaving, before):
    return pl.pallas_call(
        functools.partial(finish_leaving_kernel, place),
        out_shape=resident(leaving.shape, F32),
        in_specs=[VMEM] * 4,
        out_specs=VMEM,
        compiler_params=pltpu.CompilerParams(vmem_limit_bytes=8 * 2**20),
        name="finish_leaving",
    )(*[pin(x) for x in (ways, entering, leaving, before)])


def finish_state_kernel(place, ways, entering, state, new):
    levels = state.shape[0]

    @pl.when(lax.axis_index("lvl") != place)
    def _():
        new[...] = state[...]

    @pl.when(lax.axis_index("lvl") == place)
    def _():
        values = [stack(entering[CHUNK - 1 - a]) for a in range(CHUNK)]
        for i in range(levels):
            new[i] = state[i] + apply([(values[a], ways[a * levels + i]) for a in range(CHUNK)])


def finish_state(place, ways, entering, state, last):
    return pl.pallas_call(
        functools.partial(finish_state_kernel, place),
        out_shape=(jax.ShapeDtypeStruct if last else resident)(state.shape, F32),
        in_specs=[VMEM] * 3,
        out_specs=VMEM,
        compiler_params=pltpu.CompilerParams(vmem_limit_bytes=8 * 2**20),
        name="finish_state",
    )(*[pin(x) for x in (ways, entering, state)])


def answer_kernel(step, soon, late, entering, returned):
    @pl.when(lax.axis_index("lvl") == step)
    def _():
        past = {n + 1: stack(entering[n]) for n in range(CHUNK)}
        above = carried(soon, late, past, CHUNK, 2 * CHUNK - 1)
        for k in range(CHUNK):
            returned[k] = above[CHUNK + k]


def answer(step, soon, late, entering):
    return pl.pallas_call(
        functools.partial(answer_kernel, step),
        out_shape=resident(entering.shape, F32),
        in_specs=[VMEM] * 3,
        out_specs=VMEM,
        compiler_params=pltpu.CompilerParams(vmem_limit_bytes=8 * 2**20),
        name="answer",
    )(*[pin(x) for x in (soon, late, entering)])


def local(inverse_diag, down_block, up_block, reward):
    given = reward.shape[1]
    columns = -(-given // 16) * 16
    if columns != given:
        reward = jnp.pad(reward, ((0, 0), (0, columns - given), (0, 0)))
    count = lax.axis_size("lvl")
    weights, started, soon_here = prepare(inverse_diag, down_block, up_block, reward)
    late_here = respond(weights, started)
    assert CHUNKS == 2 and count > 1
    top = count - 1
    from_odd = [(d + 1, d) for d in range(0, top, 2)]
    soon = lax.ppermute(soon_here, "lvl", [(d + 1, d) for d in range(top)])
    soon, late_here = lax.optimization_barrier((soon, late_here))
    weight, base = weights
    own = {"weight": weight, "base": base, "soon": soon}
    ready = [d for d in range(1, count) if d % 2 == 0 or d == top]
    state = leaving = entering = late = ways = parted = None
    for step in range(count + 1):
        place = step - 1
        earlier = leaving
        returned = edge = None
        if step % 2 == 0 and 0 < step < count:
            returned = lax.ppermute(answer(step, soon_here, late_here, entering), "lvl", [(step, place)])
            state, edge = run_chunk(
                1, place, {"weight": weight, "base": base, "entering": entering, "state": state}, "early"
            )
        if place in ready and place < top:
            leaving = finish_leaving(place, ways, entering, parted, leaving)
        if step < count:
            state, leaving = run_chunk(0, step, {**own, "entering": entering, "state": state, "leaving": leaving})
        if step == 1:
            late_sent, entering = lax.optimization_barrier((late_here, entering))
            late = lax.ppermute(late_sent, "lvl", from_odd)
            state, leaving = run_chunk(
                1, 0, {**own, "late": late, "earlier": earlier, "state": state, "leaving": leaving}
            )
        if returned is not None:
            state, leaving = run_chunk(
                1, place, {**own, "returned": returned, "edge": edge, "state": state, "leaving": leaving}, "late"
            )
        came = entering
        if step < count:
            pairs = [(d, d + 1) for d in (place, step) if 0 <= d < top]
            entering = lax.ppermute(leaving, "lvl", pairs) if pairs else None
        if step == 0:
            ways, entering = lax.optimization_barrier((spread(ready, weight, soon), entering))
        if place in ready:
            state = finish_state(place, ways, came, state, step == count)
        if step in ready:
            extra = {} if step == top else {"late": late, "earlier": leaving}
            state, parted = run_chunk(1, step, {**own, **extra, "state": state})
    return state[:, :given] if columns != given else state


def solution(mesh):
    placed = (
        P(("grp", "lvl"), None, None),
        P(("grp", "lvl"), None, None),
        P(("grp", "lvl"), None, None),
        P(("grp", "lvl"), "col", None),
    )
    return jax.shard_map(
        local, mesh=mesh, in_specs=placed, out_specs=P(("grp", "lvl"), "col", None), check_vma=False
    )
```

```python
import functools

import jax
import jax.numpy as jnp
from jax import lax
from jax.experimental import pallas as pl
from jax.experimental.pallas import tpu as pltpu
from jax.sharding import PartitionSpec as P

SWEEPS = 8
CHUNK = 4
CHUNKS = SWEEPS // CHUNK
AHEAD = SWEEPS - 1
SOON = CHUNK - 1
F32 = jnp.float32
BF16 = jnp.bfloat16


def resident(shape, dtype):
    return pltpu.VMEM(shape, dtype)


def pin(x, memory=pltpu.VMEM):
    return pltpu.with_memory_space_constraint(x, memory)


def split(x):
    high = x.astype(BF16)
    return high, (x - high.astype(F32)).astype(BF16)


def dot(a, b):
    return jnp.dot(a, b, preferred_element_type=F32)


def dot_nt(a, b):
    return lax.dot_general(a, b, (((1,), (1,)), ((), ())), preferred_element_type=F32)


def dot_parts(a, b, dot=dot):
    return dot(a[0], b[0]) + (dot(a[0], b[1]) + dot(a[1], b[0]))


BLOCK = 64


def blocks(rows):
    cuts = list(range(0, rows - BLOCK + 1, BLOCK)) + [rows]
    return list(zip(cuts, cuts[1:]))


def sum_products(terms, at, end):
    return sum(dot_parts((high(at, end), low(at, end)), b()) for (high, low), b in terms)


def place_operators(weight, i, inv, down, up):
    phases = inv[0].shape[0]
    half = 128
    for k, block in enumerate((down, up)):
        for column in range(0, phases, half):
            turned = split(block[:, column : column + half].T)
            for at in range(0, half, BLOCK):
                rows = [part[at : at + BLOCK] for part in turned]
                high, low = split(dot_parts(rows, inv, dot_nt))
                start = 2 * k * phases + column + at
                weight[i, start : start + BLOCK] = high
                weight[i, start + phases : start + phases + BLOCK] = low


def operator(weight, i, k):
    phases = weight.shape[2]
    at = 2 * k * phases
    return weight[i, at : at + phases], weight[i, at + phases : at + 2 * phases]


def response(first, last, x_high, x_low, weight, base, kept):
    _, columns, phases = base.shape
    rows = phases + columns

    def step(i, terms, n=None):
        done = []
        for at, end in blocks(rows):
            new = sum_products(terms, at, end)
            if end == rows:
                new = jnp.concatenate([new[: phases - at], new[phases - at :] + base[i]], axis=0)
            if n is not None:
                kept[n, at:end] = new
            done.append((at, end, *split(new)))
        for at, end, high, low in done:
            x_high[i, at:end], x_low[i, at:end] = high, low

    def term(j, i, k):
        return (lambda at, end: x_high[j, at:end], lambda at, end: x_low[j, at:end]), lambda: operator(weight, i, k)

    for d in range(first, last):
        if d == 0:
            high, low = operator(weight, 0, 0)
            x_high[0, 0:phases], x_low[0, 0:phases] = high, low
            x_high[0, phases:rows], x_low[0, phases:rows] = split(base[0])
            kept[0, 0:phases] = high.astype(F32) + low.astype(F32)
            kept[0, phases:rows] = base[0]
            continue
        step(d, [term(d - 1, d, 0)])

        def level(k, _, d=d):
            step(d - k, [term(d - k - 1, d - k, 0), term(d - k + 1, d - k, 1)])
            return 0

        lax.fori_loop(1, d, level, 0)
        step(0, [term(1, 0, 1)], d - first)


def products(levels, given, weight, base, buffers, sems):
    first = levels[0]

    def copies(i):
        return [
            pltpu.make_async_copy(source.at[i], target.at[i - first], sems.at[n, i - first])
            for n, (source, target) in enumerate(zip(given, buffers))
        ]

    for i in levels:
        for copy in copies(i):
            copy.start()

    inv, down, up, pay = buffers
    for i in levels:
        for copy in copies(i):
            copy.wait()
        at = i - first
        here = split(inv[at])
        place_operators(weight, i, here, down[at], up[at])
        base[i] = dot_parts(split(pay[at]), here, dot_nt)


def prepare_kernel(inv, down, up, reward, weight, base, x_high, x_low, kept, *scratch):
    *buffers, sems = scratch
    products(range(SOON), (inv, down, up, reward), weight, base, buffers, sems)
    response(0, SOON, x_high, x_low, weight, base, kept)


def prepare_rest_kernel(inv, down, up, reward, weight_soon, base_soon, weight, base, *scratch):
    *buffers, sems = scratch
    levels = reward.shape[0]
    weight[0:SOON] = weight_soon[...]
    base[0:SOON] = base_soon[...]
    products(range(SOON, levels), (inv, down, up, reward), weight, base, buffers, sems)


def respond_kernel(weight, base, x_high_soon, x_low_soon, kept, x_high, x_low):
    @pl.when(lax.axis_index("lvl") > 0)
    def _():
        x_high[0:SOON] = x_high_soon[...]
        x_low[0:SOON] = x_low_soon[...]
        response(SOON, AHEAD, x_high, x_low, weight, base, kept)


VMEM = pl.BlockSpec(memory_space=pltpu.VMEM)
HBM = pl.BlockSpec(memory_space=pltpu.HBM)


def operators(levels, columns, phases):
    return [resident((levels, 4 * phases, phases), BF16), resident((levels, columns, phases), F32)]


def buffers(levels, columns, phases):
    return (
        [pltpu.VMEM((levels, phases, phases), F32)] * 3
        + [pltpu.VMEM((levels, columns, phases), F32)]
        + [pltpu.SemaphoreType.DMA((4, levels))]
    )


def prepare(inverse_diag, down_block, up_block, reward):
    levels, columns, phases = reward.shape
    assert levels >= AHEAD
    rows = phases + columns
    given = [pin(x, pltpu.HBM) for x in (inverse_diag, down_block, up_block, reward)]
    *soon, kept_soon = pl.pallas_call(
        prepare_kernel,
        out_shape=operators(SOON, columns, phases)
        + [resident((SOON, rows, phases), BF16)] * 2
        + [resident((SOON, rows, phases), F32)],
        in_specs=[HBM] * 4,
        out_specs=[VMEM] * 5,
        scratch_shapes=buffers(SOON, columns, phases),
        compiler_params=pltpu.CompilerParams(vmem_limit_bytes=16 * 2**20),
        name="prepare",
    )(*given)
    weights = pl.pallas_call(
        prepare_rest_kernel,
        out_shape=operators(levels, columns, phases),
        in_specs=[HBM] * 4 + [VMEM] * 2,
        out_specs=[VMEM] * 2,
        scratch_shapes=buffers(levels - SOON, columns, phases),
        compiler_params=pltpu.CompilerParams(vmem_limit_bytes=16 * 2**20),
        name="prepare_rest",
    )(*given, *[pin(x) for x in soon[:2]])
    return weights, soon[2:], kept_soon


def respond(weights, started):
    _, rows, phases = started[0].shape
    return pl.pallas_call(
        respond_kernel,
        out_shape=resident((AHEAD - SOON, rows, phases), F32),
        in_specs=[VMEM] * 4,
        out_specs=VMEM,
        scratch_shapes=[pltpu.VMEM((AHEAD, rows, phases), BF16)] * 2,
        compiler_params=pltpu.CompilerParams(vmem_limit_bytes=16 * 2**20),
        name="respond",
    )(*[pin(x) for x in (*weights, *started)])


def stack(x):
    high = x.astype(BF16).astype(F32)
    return jnp.concatenate([high, x - high], axis=0).astype(BF16)


def fold(total):
    half = total.shape[0] // 2
    return total[:half] + total[half:]


def apply(terms):
    values = jnp.concatenate([x for x, _ in terms for _ in range(2)], axis=1)
    return fold(dot(values, jnp.concatenate([operator for _, operator in terms], axis=0)))


def apply_each(values, operator, columns):
    phases = operator.shape[1]
    values = jnp.concatenate(values, axis=0) if len(values) > 1 else values[0]
    total = dot(values, operator[0:phases]) + dot(values, operator[phases:])
    return [fold(total[at : at + 2 * columns]) for at in range(0, total.shape[0], 2 * columns)]


def whole(operator):
    return jnp.concatenate(split(operator), axis=0)


def kept_at(soon, late, j):
    return soon[j] if j < SOON else late[j - SOON]


def carried(soon, late, past, first, last):
    phases = soon.shape[2]
    above = {n: kept_at(soon, late, n - 1)[phases:] for n in range(max(first, 1), last + 1)}
    columns = soon.shape[1] - phases
    for j in range(last) if past else ():
        pairs = [(n, n - j) for n in above if n - j in past]
        if pairs:
            terms = [past[m] for _, m in pairs]
            for (n, _), term in zip(pairs, apply_each(terms, whole(kept_at(soon, late, j)[0:phases]), columns)):
                above[n] += term
    return above


def wave(first, weight, base, now, above, feedback, due, emit):
    levels, _, phases = base.shape
    for turn in range(levels + 2 * (CHUNK - 1)):
        for k in range(CHUNK):
            i = turn - 2 * k
            if not (0 <= i < levels and due(i, k)):
                continue
            n = first + 1 + k
            terms = []
            if (i - 1, n) in now:
                terms.append((now[i - 1, n], weight[i, 0 : 2 * phases]))
            if n > 1:
                over = stack(above[n - 1]) if i == levels - 1 else now[i + 1, n - 1]
                terms.append((over, weight[i, 2 * phases : 4 * phases]))
            value = base[i] + apply(terms) if terms else base[i]
            now[i, n] = stack(value)
            emit(i, k, value)
            if i == levels - 1:
                for later in range(n, first + CHUNK):
                    above[later] += apply([(now[i, n], feedback[later - n])])


def edge_level(levels, k):
    return levels - 2 - k


def chunk_kernel(chunk, place, part, names, *refs):
    given = dict(zip(names, refs))
    new_state, leaving = refs[len(names) :]
    weight, base = given["weight"], given["base"]
    levels, columns, phases = base.shape
    first = chunk * CHUNK

    @pl.when(lax.axis_index("lvl") != place)
    def _():
        for name, target in (("state", new_state), ("leaving", leaving)):
            target[...] = given[name][...] if name in given else jnp.zeros_like(target)

    @pl.when(lax.axis_index("lvl") == place)
    def _():
        zero = jnp.zeros((columns, phases), F32)
        above, feedback = {first + k: zero for k in range(CHUNK)}, []
        if part != "early":
            soon = given["soon"]
            feedback = [whole(soon[j, 0:phases]) for j in range(SOON)]
            if not first:
                above = carried(soon, None, {}, first, first + CHUNK - 1)
            elif "late" in given:
                past = {n + 1: stack(given["earlier"][n]) for n in range(first)}
                above = carried(soon, given["late"], past, first, first + CHUNK - 1)
            elif "returned" in given:
                above = {first + k: given["returned"][k] for k in range(CHUNK)}

        now = {}
        if part == "late":
            for k in range(CHUNK):
                now[edge_level(levels, k), first + 1 + k] = stack(given["edge"][k])
            new_state[...] = given["state"][...]
        elif first:
            for i in range(levels):
                now[i, first] = stack(given["state"][i])
        if part != "late" and "entering" in given:
            for k in range(CHUNK):
                now[-1, first + 1 + k] = stack(given["entering"][k])

        def due(i, k):
            return part == "all" or (i <= edge_level(levels, k)) == (part == "early")

        def emit(i, k, value):
            if k == CHUNK - 1:
                new_state[i] = value
            if i == (edge_level(levels, k) if part == "early" else levels - 1):
                leaving[k] = value

        wave(first, weight, base, now, above, feedback, due, emit)


def run_chunk(chunk, place, given, part="all"):
    given = {name: x for name, x in given.items() if x is not None}
    levels, columns, phases = given["base"].shape
    return pl.pallas_call(
        functools.partial(chunk_kernel, chunk, place, part, tuple(given)),
        out_shape=[resident((levels, columns, phases), F32), resident((CHUNK, columns, phases), F32)],
        in_specs=[VMEM] * len(given),
        out_specs=[VMEM] * 2,
        compiler_params=pltpu.CompilerParams(vmem_limit_bytes=16 * 2**20),
        name="chunk",
    )(*[pin(x) for x in given.values()])


def among(places):
    return functools.reduce(jnp.logical_or, [lax.axis_index("lvl") == place for place in places])


def spread_kernel(places, weight, soon, out, feedback_high, feedback_low, back_high, back_low):
    levels, _, phases = weight.shape

    def step(i, a, terms):
        done = [(at, end, *split(sum_products(terms, at, end))) for at, end in blocks(phases)]
        for at, end, high, low in done:
            out[a * levels + i, at:end] = high
            out[a * levels + i, phases + at : phases + end] = low

    def parts(a, i):
        slot = a * levels + i
        return lambda at, end: out[slot, at:end], lambda at, end: out[slot, phases + at : phases + end]

    def term(a, j, i, k):
        return parts(a, j), lambda: operator(weight, i, k)

    @pl.when(among(places))
    def _():
        top = levels - 1
        out[0] = weight[0, 0 : 2 * phases]

        def up(i, _):
            step(i, 0, [term(0, i - 1, i, 0)])
            return 0

        lax.fori_loop(1, levels, up, 0)
        for j in range(CHUNK - 1):
            feedback_high[j], feedback_low[j] = split(soon[j, 0:phases])
        for a in range(1, CHUNK):
            step(0, a, [term(a - 1, 1, 0, 1)])

            def both(i, _, a=a):
                step(i, a, [term(a, i - 1, i, 0), term(a - 1, i + 1, i, 1)])
                return 0

            lax.fori_loop(1, top, both, 0)
            returns = [
                (parts(a - 1 - j, top), lambda j=j: (feedback_high[j], feedback_low[j])) for j in range(a)
            ]
            for at, end in blocks(phases):
                back_high[at:end], back_low[at:end] = split(sum_products(returns, at, end))
            back = lambda at, end: back_high[at:end], lambda at, end: back_low[at:end]
            step(top, a, [term(a, top - 1, top, 0), (back, lambda: operator(weight, top, 1))])


def spread(places, weight, soon):
    levels, _, phases = weight.shape
    return pl.pallas_call(
        functools.partial(spread_kernel, places),
        out_shape=resident((CHUNK * levels, 2 * phases, phases), BF16),
        in_specs=[VMEM] * 2,
        out_specs=VMEM,
        scratch_shapes=[pltpu.VMEM((CHUNK - 1, phases, phases), BF16)] * 2 + [pltpu.VMEM((phases, phases), BF16)] * 2,
        compiler_params=pltpu.CompilerParams(vmem_limit_bytes=16 * 2**20),
        name="spread",
    )(*[pin(x) for x in (weight, soon)])


def finish_leaving_kernel(place, ways, entering, leaving, before, new):
    levels = ways.shape[0] // CHUNK
    columns = entering.shape[1]

    @pl.when(lax.axis_index("lvl") != place)
    def _():
        new[...] = before[...]

    @pl.when(lax.axis_index("lvl") == place)
    def _():
        values = [stack(entering[k]) for k in range(CHUNK)]
        total = [leaving[k] for k in range(CHUNK)]
        for a in range(CHUNK):
            for k, term in enumerate(apply_each(values[: CHUNK - a], ways[a * levels + levels - 1], columns)):
                total[a + k] += term
        for k in range(CHUNK):
            new[k] = total[k]


def finish_leaving(place, ways, entering, leaving, before):
    return pl.pallas_call(
        functools.partial(finish_leaving_kernel, place),
        out_shape=resident(leaving.shape, F32),
        in_specs=[VMEM] * 4,
        out_specs=VMEM,
        compiler_params=pltpu.CompilerParams(vmem_limit_bytes=8 * 2**20),
        name="finish_leaving",
    )(*[pin(x) for x in (ways, entering, leaving, before)])


def finish_state_kernel(place, ways, entering, state, new):
    levels = state.shape[0]

    @pl.when(lax.axis_index("lvl") != place)
    def _():
        new[...] = state[...]

    @pl.when(lax.axis_index("lvl") == place)
    def _():
        values = [stack(entering[CHUNK - 1 - a]) for a in range(CHUNK)]
        for i in range(levels):
            new[i] = state[i] + apply([(values[a], ways[a * levels + i]) for a in range(CHUNK)])


def finish_state(place, ways, entering, state, last):
    return pl.pallas_call(
        functools.partial(finish_state_kernel, place),
        out_shape=(jax.ShapeDtypeStruct if last else resident)(state.shape, F32),
        in_specs=[VMEM] * 3,
        out_specs=VMEM,
        compiler_params=pltpu.CompilerParams(vmem_limit_bytes=8 * 2**20),
        name="finish_state",
    )(*[pin(x) for x in (ways, entering, state)])


def answer_kernel(step, soon, late, entering, returned):
    @pl.when(lax.axis_index("lvl") == step)
    def _():
        past = {n + 1: stack(entering[n]) for n in range(CHUNK)}
        above = carried(soon, late, past, CHUNK, 2 * CHUNK - 1)
        for k in range(CHUNK):
            returned[k] = above[CHUNK + k]


def answer(step, soon, late, entering):
    return pl.pallas_call(
        functools.partial(answer_kernel, step),
        out_shape=resident(entering.shape, F32),
        in_specs=[VMEM] * 3,
        out_specs=VMEM,
        compiler_params=pltpu.CompilerParams(vmem_limit_bytes=8 * 2**20),
        name="answer",
    )(*[pin(x) for x in (soon, late, entering)])


def local(inverse_diag, down_block, up_block, reward):
    given = reward.shape[1]
    columns = -(-given // 16) * 16
    if columns != given:
        reward = jnp.pad(reward, ((0, 0), (0, columns - given), (0, 0)))
    count = lax.axis_size("lvl")
    weights, started, soon_here = prepare(inverse_diag, down_block, up_block, reward)
    late_here = respond(weights, started)
    assert CHUNKS == 2 and count > 1
    top = count - 1
    from_odd = [(d + 1, d) for d in range(0, top, 2)]
    soon = lax.ppermute(soon_here, "lvl", [(d + 1, d) for d in range(top)])
    soon, late_here = lax.optimization_barrier((soon, late_here))
    weight, base = weights
    own = {"weight": weight, "base": base, "soon": soon}
    ready = [d for d in range(1, count) if d % 2 == 0 or d == top]
    state = leaving = entering = late = ways = parted = None
    for step in range(count + 1):
        place = step - 1
        earlier = leaving
        returned = edge = None
        if step % 2 == 0 and 0 < step < count:
            returned = lax.ppermute(answer(step, soon_here, late_here, entering), "lvl", [(step, place)])
            state, edge = run_chunk(
                1, place, {"weight": weight, "base": base, "entering": entering, "state": state}, "early"
            )
        if place in ready and place < top:
            leaving = finish_leaving(place, ways, entering, parted, leaving)
        if step < count:
            state, leaving = run_chunk(0, step, {**own, "entering": entering, "state": state, "leaving": leaving})
        if step == 1:
            late_sent, entering = lax.optimization_barrier((late_here, entering))
            late = lax.ppermute(late_sent, "lvl", from_odd)
            state, leaving = run_chunk(
                1, 0, {**own, "late": late, "earlier": earlier, "state": state, "leaving": leaving}
            )
        if returned is not None:
            state, leaving = run_chunk(
                1, place, {**own, "returned": returned, "edge": edge, "state": state, "leaving": leaving}, "late"
            )
        came = entering
        if step < count:
            pairs = [(d, d + 1) for d in (place, step) if 0 <= d < top]
            entering = lax.ppermute(leaving, "lvl", pairs) if pairs else None
        if step == 0:
            ways, entering = lax.optimization_barrier((spread(ready, weight, soon), entering))
        if place in ready:
            state = finish_state(place, ways, came, state, step == count)
        if step in ready:
            extra = {} if step == top else {"late": late, "earlier": leaving}
            state, parted = run_chunk(1, step, {**own, **extra, "state": state})
    return state[:, :given] if columns != given else state


def solution(mesh):
    placed = (
        P(("grp", "lvl"), None, None),
        P(("grp", "lvl"), None, None),
        P(("grp", "lvl"), None, None),
        P(("grp", "lvl"), "col", None),
    )
    return jax.shard_map(
        local, mesh=mesh, in_specs=placed, out_specs=P(("grp", "lvl"), "col", None), check_vma=False
    )
```

```python
import functools

import jax
import jax.numpy as jnp
from jax import lax
from jax.experimental import pallas as pl
from jax.experimental.pallas import tpu as pltpu
from jax.sharding import PartitionSpec as P

SWEEPS = 8
CHUNK = 4
CHUNKS = SWEEPS // CHUNK
AHEAD = SWEEPS - 1
SOON = CHUNK - 1
F32 = jnp.float32
BF16 = jnp.bfloat16


def resident(shape, dtype):
    return pltpu.VMEM(shape, dtype)


def pin(x, memory=pltpu.VMEM):
    return pltpu.with_memory_space_constraint(x, memory)


def split(x):
    high = x.astype(BF16)
    return high, (x - high.astype(F32)).astype(BF16)


def dot(a, b):
    return jnp.dot(a, b, preferred_element_type=F32)


def dot_nt(a, b):
    return lax.dot_general(a, b, (((1,), (1,)), ((), ())), preferred_element_type=F32)


def dot_parts(a, b, dot=dot):
    return dot(a[0], b[0]) + (dot(a[0], b[1]) + dot(a[1], b[0]))


def place_operators(weight, i, down, up):
    phases = down.shape[0]
    for k, part in enumerate((*split(down.T), *split(up.T))):
        weight[i, k * phases : (k + 1) * phases] = part


def operator(weight, i, k):
    phases = weight.shape[2]
    at = 2 * k * phases
    return weight[i, at : at + phases], weight[i, at + phases : at + 2 * phases]


def response(first, last, x_high, x_low, weight, base, kept):
    _, columns, phases = base.shape
    rows = phases + columns

    def store(i, new):
        top = new[0:phases]
        end = new[phases:rows] + base[i]
        x_high[i, 0:phases], x_low[i, 0:phases] = split(top)
        x_high[i, phases:rows], x_low[i, phases:rows] = split(end)
        return top, end

    def from_below(i):
        return dot_parts((x_high[i - 1], x_low[i - 1]), operator(weight, i, 0))

    def from_above(i):
        return dot_parts((x_high[i + 1], x_low[i + 1]), operator(weight, i, 1))

    for d in range(first, last):
        if d == 0:
            high, low = weight[0, 0:phases], weight[0, phases : 2 * phases]
            x_high[0, 0:phases], x_low[0, 0:phases] = high, low
            x_high[0, phases:rows], x_low[0, phases:rows] = split(base[0])
            kept[0, 0:phases] = high.astype(F32) + low.astype(F32)
            kept[0, phases:rows] = base[0]
            continue
        store(d, from_below(d))

        def level(k, _, d=d):
            i = d - k
            store(i, from_below(i) + from_above(i))
            return 0

        lax.fori_loop(1, d, level, 0)
        kept[d - first, 0:phases], kept[d - first, phases:rows] = store(0, from_above(0))


def products(levels, given, weight, base, buffers, sems):
    first = levels[0]

    def copies(i):
        return [
            pltpu.make_async_copy(source.at[i], target.at[i - first], sems.at[n, i - first])
            for n, (source, target) in enumerate(zip(given, buffers))
        ]

    for i in levels:
        for copy in copies(i):
            copy.start()

    inv, down, up, pay = buffers
    for i in levels:
        for copy in copies(i):
            copy.wait()
        at = i - first
        here = split(inv[at])
        place_operators(weight, i, dot_parts(here, split(down[at])), dot_parts(here, split(up[at])))
        base[i] = dot_parts(split(pay[at]), here, dot_nt)


def prepare_kernel(inv, down, up, reward, weight, base, x_high, x_low, kept, *scratch):
    *buffers, sems = scratch
    products(range(SOON), (inv, down, up, reward), weight, base, buffers, sems)
    response(0, SOON, x_high, x_low, weight, base, kept)


def prepare_rest_kernel(inv, down, up, reward, weight_soon, base_soon, weight, base, *scratch):
    *buffers, sems = scratch
    levels = reward.shape[0]
    weight[0:SOON] = weight_soon[...]
    base[0:SOON] = base_soon[...]
    products(range(SOON, levels), (inv, down, up, reward), weight, base, buffers, sems)


def respond_kernel(weight, base, x_high_soon, x_low_soon, kept, x_high, x_low):
    @pl.when(lax.axis_index("lvl") > 0)
    def _():
        x_high[0:SOON] = x_high_soon[...]
        x_low[0:SOON] = x_low_soon[...]
        response(SOON, AHEAD, x_high, x_low, weight, base, kept)


VMEM = pl.BlockSpec(memory_space=pltpu.VMEM)
HBM = pl.BlockSpec(memory_space=pltpu.HBM)


def operators(levels, columns, phases):
    return [resident((levels, 4 * phases, phases), BF16), resident((levels, columns, phases), F32)]


def buffers(levels, columns, phases):
    return (
        [pltpu.VMEM((levels, phases, phases), F32)] * 3
        + [pltpu.VMEM((levels, columns, phases), F32)]
        + [pltpu.SemaphoreType.DMA((4, levels))]
    )


def prepare(inverse_diag, down_block, up_block, reward):
    levels, columns, phases = reward.shape
    assert levels >= AHEAD
    rows = phases + columns
    given = [pin(x, pltpu.HBM) for x in (inverse_diag, down_block, up_block, reward)]
    *soon, kept_soon = pl.pallas_call(
        prepare_kernel,
        out_shape=operators(SOON, columns, phases)
        + [resident((SOON, rows, phases), BF16)] * 2
        + [resident((SOON, rows, phases), F32)],
        in_specs=[HBM] * 4,
        out_specs=[VMEM] * 5,
        scratch_shapes=buffers(SOON, columns, phases),
        compiler_params=pltpu.CompilerParams(vmem_limit_bytes=16 * 2**20),
        name="prepare",
    )(*given)
    weights = pl.pallas_call(
        prepare_rest_kernel,
        out_shape=operators(levels, columns, phases),
        in_specs=[HBM] * 4 + [VMEM] * 2,
        out_specs=[VMEM] * 2,
        scratch_shapes=buffers(levels - SOON, columns, phases),
        compiler_params=pltpu.CompilerParams(vmem_limit_bytes=16 * 2**20),
        name="prepare_rest",
    )(*given, *[pin(x) for x in soon[:2]])
    return weights, soon[2:], kept_soon


def respond(weights, started):
    _, rows, phases = started[0].shape
    return pl.pallas_call(
        respond_kernel,
        out_shape=resident((AHEAD - SOON, rows, phases), F32),
        in_specs=[VMEM] * 4,
        out_specs=VMEM,
        scratch_shapes=[pltpu.VMEM((AHEAD, rows, phases), BF16)] * 2,
        compiler_params=pltpu.CompilerParams(vmem_limit_bytes=16 * 2**20),
        name="respond",
    )(*[pin(x) for x in (*weights, *started)])


def stack(x):
    high = x.astype(BF16).astype(F32)
    return jnp.concatenate([high, x - high], axis=0).astype(BF16)


def fold(total):
    half = total.shape[0] // 2
    return total[:half] + total[half:]


def apply(terms):
    values = jnp.concatenate([x for x, _ in terms for _ in range(2)], axis=1)
    return fold(dot(values, jnp.concatenate([operator for _, operator in terms], axis=0)))


def apply_each(values, operator, columns):
    phases = operator.shape[1]
    values = jnp.concatenate(values, axis=0) if len(values) > 1 else values[0]
    total = dot(values, operator[0:phases]) + dot(values, operator[phases:])
    return [fold(total[at : at + 2 * columns]) for at in range(0, total.shape[0], 2 * columns)]


def whole(operator):
    return jnp.concatenate(split(operator), axis=0)


def kept_at(soon, late, j):
    return soon[j] if j < SOON else late[j - SOON]


def carried(soon, late, past, first, last):
    phases = soon.shape[2]
    above = {n: kept_at(soon, late, n - 1)[phases:] for n in range(max(first, 1), last + 1)}
    columns = soon.shape[1] - phases
    for j in range(last) if past else ():
        pairs = [(n, n - j) for n in above if n - j in past]
        if pairs:
            terms = [past[m] for _, m in pairs]
            for (n, _), term in zip(pairs, apply_each(terms, whole(kept_at(soon, late, j)[0:phases]), columns)):
                above[n] += term
    return above


def wave(first, weight, base, now, above, feedback, due, emit):
    levels, _, phases = base.shape
    for turn in range(levels + 2 * (CHUNK - 1)):
        for k in range(CHUNK):
            i = turn - 2 * k
            if not (0 <= i < levels and due(i, k)):
                continue
            n = first + 1 + k
            terms = []
            if (i - 1, n) in now:
                terms.append((now[i - 1, n], weight[i, 0 : 2 * phases]))
            if n > 1:
                over = stack(above[n - 1]) if i == levels - 1 else now[i + 1, n - 1]
                terms.append((over, weight[i, 2 * phases : 4 * phases]))
            value = base[i] + apply(terms) if terms else base[i]
            now[i, n] = stack(value)
            emit(i, k, value)
            if i == levels - 1:
                for later in range(n, first + CHUNK):
                    above[later] += apply([(now[i, n], feedback[later - n])])


def edge_level(levels, k):
    return levels - 2 - k


def chunk_kernel(chunk, places, part, names, *refs):
    given = dict(zip(names, refs))
    new_state, leaving = refs[len(names) :]
    weight, base = given["weight"], given["base"]
    levels, columns, phases = base.shape
    first = chunk * CHUNK

    @pl.when(jnp.logical_not(among(places)))
    def _():
        for name, target in (("state", new_state), ("leaving", leaving)):
            target[...] = given[name][...] if name in given else jnp.zeros_like(target)

    @pl.when(among(places))
    def _():
        zero = jnp.zeros((columns, phases), F32)
        above, feedback = {first + k: zero for k in range(CHUNK)}, []
        if part != "early":
            soon = given["soon"]
            feedback = [whole(soon[j, 0:phases]) for j in range(SOON)]
            if not first:
                above = carried(soon, None, {}, first, first + CHUNK - 1)
            elif "late" in given:
                past = {n + 1: stack(given["earlier"][n]) for n in range(first)}
                above = carried(soon, given["late"], past, first, first + CHUNK - 1)
            elif "returned" in given:
                above = {first + k: given["returned"][k] for k in range(CHUNK)}

        now = {}
        if part == "late":
            for k in range(CHUNK):
                now[edge_level(levels, k), first + 1 + k] = stack(given["edge"][k])
            new_state[...] = given["state"][...]
        elif first:
            for i in range(levels):
                now[i, first] = stack(given["state"][i])
        if part != "late" and "entering" in given:
            for k in range(CHUNK):
                now[-1, first + 1 + k] = stack(given["entering"][k])

        def due(i, k):
            return part == "all" or (i <= edge_level(levels, k)) == (part == "early")

        def emit(i, k, value):
            if k == CHUNK - 1:
                new_state[i] = value
            if i == (edge_level(levels, k) if part == "early" else levels - 1):
                leaving[k] = value

        wave(first, weight, base, now, above, feedback, due, emit)


def run_chunk(chunk, places, given, part="all"):
    given = {name: x for name, x in given.items() if x is not None}
    levels, columns, phases = given["base"].shape
    return pl.pallas_call(
        functools.partial(chunk_kernel, chunk, tuple(places), part, tuple(given)),
        out_shape=[resident((levels, columns, phases), F32), resident((CHUNK, columns, phases), F32)],
        in_specs=[VMEM] * len(given),
        out_specs=[VMEM] * 2,
        compiler_params=pltpu.CompilerParams(vmem_limit_bytes=16 * 2**20),
        name="chunk",
    )(*[pin(x) for x in given.values()])


def among(places):
    return functools.reduce(jnp.logical_or, [lax.axis_index("lvl") == place for place in places])


def spread_kernel(places, weight, soon, out):
    levels, _, phases = weight.shape

    def get(at):
        return out[at, 0:phases], out[at, phases : 2 * phases]

    def put(at, value):
        out[at, 0:phases], out[at, phases : 2 * phases] = split(value)

    @pl.when(among(places))
    def _():
        out[0] = weight[0, 0 : 2 * phases]

        def up(i, _):
            put(i, dot_parts(get(i - 1), operator(weight, i, 0)))
            return 0

        lax.fori_loop(1, levels, up, 0)
        feedback = [split(soon[j, 0:phases]) for j in range(CHUNK - 1)]
        for a in range(1, CHUNK):
            at, old = a * levels, (a - 1) * levels
            put(at, dot_parts(get(old + 1), operator(weight, 0, 1)))

            def both(i, _, at=at, old=old):
                below = dot_parts(get(at + i - 1), operator(weight, i, 0))
                put(at + i, below + dot_parts(get(old + i + 1), operator(weight, i, 1)))
                return 0

            lax.fori_loop(1, levels - 1, both, 0)
            back = sum(dot_parts(get((a - 1 - j) * levels + levels - 1), feedback[j]) for j in range(a))
            top = levels - 1
            below = dot_parts(get(at + top - 1), operator(weight, top, 0))
            put(at + top, below + dot_parts(split(back), operator(weight, top, 1)))


def spread(places, weight, soon):
    levels, _, phases = weight.shape
    return pl.pallas_call(
        functools.partial(spread_kernel, places),
        out_shape=resident((CHUNK * levels, 2 * phases, phases), BF16),
        in_specs=[VMEM] * 2,
        out_specs=VMEM,
        compiler_params=pltpu.CompilerParams(vmem_limit_bytes=16 * 2**20),
        name="spread",
    )(*[pin(x) for x in (weight, soon)])


def finish_leaving_kernel(place, ways, entering, leaving, before, new):
    levels = ways.shape[0] // CHUNK
    columns = entering.shape[1]

    @pl.when(lax.axis_index("lvl") != place)
    def _():
        new[...] = before[...]

    @pl.when(lax.axis_index("lvl") == place)
    def _():
        values = [stack(entering[k]) for k in range(CHUNK)]
        total = [leaving[k] for k in range(CHUNK)]
        for a in range(CHUNK):
            for k, term in enumerate(apply_each(values[: CHUNK - a], ways[a * levels + levels - 1], columns)):
                total[a + k] += term
        for k in range(CHUNK):
            new[k] = total[k]


def finish_leaving(place, ways, entering, leaving, before):
    return pl.pallas_call(
        functools.partial(finish_leaving_kernel, place),
        out_shape=resident(leaving.shape, F32),
        in_specs=[VMEM] * 4,
        out_specs=VMEM,
        compiler_params=pltpu.CompilerParams(vmem_limit_bytes=8 * 2**20),
        name="finish_leaving",
    )(*[pin(x) for x in (ways, entering, leaving, before)])


def finish_state_kernel(place, ways, entering, state, new):
    levels = state.shape[0]

    @pl.when(lax.axis_index("lvl") != place)
    def _():
        new[...] = state[...]

    @pl.when(lax.axis_index("lvl") == place)
    def _():
        values = [stack(entering[CHUNK - 1 - a]) for a in range(CHUNK)]
        for i in range(levels):
            new[i] = state[i] + apply([(values[a], ways[a * levels + i]) for a in range(CHUNK)])


def finish_state(place, ways, entering, state, last):
    return pl.pallas_call(
        functools.partial(finish_state_kernel, place),
        out_shape=(jax.ShapeDtypeStruct if last else resident)(state.shape, F32),
        in_specs=[VMEM] * 3,
        out_specs=VMEM,
        compiler_params=pltpu.CompilerParams(vmem_limit_bytes=8 * 2**20),
        name="finish_state",
    )(*[pin(x) for x in (ways, entering, state)])


def answer_kernel(step, soon, late, entering, returned):
    @pl.when(lax.axis_index("lvl") == step)
    def _():
        past = {n + 1: stack(entering[n]) for n in range(CHUNK)}
        above = carried(soon, late, past, CHUNK, 2 * CHUNK - 1)
        for k in range(CHUNK):
            returned[k] = above[CHUNK + k]


def answer(step, soon, late, entering):
    return pl.pallas_call(
        functools.partial(answer_kernel, step),
        out_shape=resident(entering.shape, F32),
        in_specs=[VMEM] * 3,
        out_specs=VMEM,
        compiler_params=pltpu.CompilerParams(vmem_limit_bytes=8 * 2**20),
        name="answer",
    )(*[pin(x) for x in (soon, late, entering)])


def local(inverse_diag, down_block, up_block, reward):
    given = reward.shape[1]
    columns = -(-given // 16) * 16
    if columns != given:
        reward = jnp.pad(reward, ((0, 0), (0, columns - given), (0, 0)))
    count = lax.axis_size("lvl")
    weights, started, soon_here = prepare(inverse_diag, down_block, up_block, reward)
    late_here = respond(weights, started)
    assert CHUNKS == 2 and count > 1
    top = count - 1
    from_odd = [(d + 1, d) for d in range(0, top, 2)]
    soon = lax.ppermute(soon_here, "lvl", [(d + 1, d) for d in range(top)])
    soon, late_here = lax.optimization_barrier((soon, late_here))
    weight, base = weights
    own = {"weight": weight, "base": base, "soon": soon}
    assert count > 1
    top = count - 1
    soon = lax.ppermute(soon_here, "lvl", [(d + 1, d) for d in range(top)])
    late = lax.ppermute(late_here, "lvl", [(d + 1, d) for d in range(0, top, 2)])
    soon, late_here = lax.optimization_barrier((soon, late_here))
    weight, base = weights
    own = {"weight": weight, "base": base, "soon": soon}
    ready = [d for d in range(1, count) if d % 2 == 0 or d == top]
    state = leaving = entering = ways = parted = None
    for step in range(count + 1):
        place = step - 1
        earlier = leaving
        returned = edge = None
        if step % 2 == 0 and 0 < step < count:
            returned = lax.ppermute(answer(step, soon_here, late_here, entering), "lvl", [(step, place)])
            given_early = {"weight": weight, "base": base, "entering": entering, "state": state}
            state, edge = run_chunk(1, [place], given_early, "early")
        if place in ready and place < top:
            leaving = finish_leaving(place, ways, entering, parted, leaving)
        if step == 0:
            state, leaving = started = run_chunk(0, [0, *ready], own)
        elif step in ready:
            if step < top:
                leaving = finish_leaving(step, ways, entering, started[1], leaving)
        elif step < count:
            state, leaving = run_chunk(0, [step], {**own, "entering": entering, "state": state, "leaving": leaving})
        if step == 1:
            given_first = {**own, "late": late, "earlier": earlier, "state": state, "leaving": leaving}
            state, leaving = run_chunk(1, [0], given_first)
        if returned is not None:
            given_rest = {**own, "returned": returned, "edge": edge, "state": state, "leaving": leaving}
            state, leaving = run_chunk(1, [place], given_rest, "late")
        came = entering
        if step < count:
            pairs = [(d, d + 1) for d in (place, step) if 0 <= d < top]
            entering = lax.ppermute(leaving, "lvl", pairs) if pairs else None
        if step == 1:
            soon_then, leaving = lax.optimization_barrier((soon, leaving))
            ways, entering = lax.optimization_barrier((spread(ready, weight, soon_then), entering))
        if place in ready:
            state = finish_state(place, ways, came, state, step == count)
        if step in ready:
            state = finish_state(step, ways, came, state, False)
            extra = {} if step == top else {"late": late, "earlier": leaving}
            state, parted = run_chunk(1, [step], {**own, **extra, "state": state})
    return state[:, :given] if columns != given else state


def solution(mesh):
    placed = (
        P(("grp", "lvl"), None, None),
        P(("grp", "lvl"), None, None),
        P(("grp", "lvl"), None, None),
        P(("grp", "lvl"), "col", None),
    )
    return jax.shard_map(
        local, mesh=mesh, in_specs=placed, out_specs=P(("grp", "lvl"), "col", None), check_vma=False
    )
```

```python
import functools

import jax
import jax.numpy as jnp
from jax import lax
from jax.experimental import pallas as pl
from jax.experimental.pallas import tpu as pltpu
from jax.sharding import PartitionSpec as P

SWEEPS = 8
CHUNK = 4
CHUNKS = SWEEPS // CHUNK
AHEAD = SWEEPS - 1
SOON = CHUNK - 1
F32 = jnp.float32
BF16 = jnp.bfloat16


def resident(shape, dtype):
    return pltpu.VMEM(shape, dtype)


def pin(x, memory=pltpu.VMEM):
    return pltpu.with_memory_space_constraint(x, memory)


def split(x):
    high = x.astype(BF16)
    return high, (x - high.astype(F32)).astype(BF16)


def dot(a, b):
    return jnp.dot(a, b, preferred_element_type=F32)


def dot_nt(a, b):
    return lax.dot_general(a, b, (((1,), (1,)), ((), ())), preferred_element_type=F32)


def dot_parts(a, b, dot=dot):
    return dot(a[0], b[0]) + (dot(a[0], b[1]) + dot(a[1], b[0]))


def place_operator(weight, i, k, value):
    phases = value.shape[0]
    for n, part in enumerate(split(value.T)):
        weight[i, (2 * k + n) * phases : (2 * k + n + 1) * phases] = part


def operator(weight, i, k):
    phases = weight.shape[2]
    at = 2 * k * phases
    return weight[i, at : at + phases], weight[i, at + phases : at + 2 * phases]


def response(first, last, x_high, x_low, weight, base, kept):
    _, columns, phases = base.shape
    rows = phases + columns

    def store(i, new):
        top = new[0:phases]
        end = new[phases:rows] + base[i]
        x_high[i, 0:phases], x_low[i, 0:phases] = split(top)
        x_high[i, phases:rows], x_low[i, phases:rows] = split(end)
        return top, end

    def from_below(i):
        return dot_parts((x_high[i - 1], x_low[i - 1]), operator(weight, i, 0))

    def from_above(i):
        return dot_parts((x_high[i + 1], x_low[i + 1]), operator(weight, i, 1))

    for d in range(first, last):
        if d == 0:
            high, low = weight[0, 0:phases], weight[0, phases : 2 * phases]
            x_high[0, 0:phases], x_low[0, 0:phases] = high, low
            x_high[0, phases:rows], x_low[0, phases:rows] = split(base[0])
            kept[0, 0:phases] = high.astype(F32) + low.astype(F32)
            kept[0, phases:rows] = base[0]
            continue
        store(d, from_below(d))

        def level(k, _, d=d):
            i = d - k
            store(i, from_below(i) + from_above(i))
            return 0

        lax.fori_loop(1, d, level, 0)
        kept[d - first, 0:phases], kept[d - first, phases:rows] = store(0, from_above(0))


def products(wanted, given, weight, base, buffers, sems):
    first = min(wanted)
    names = {i: [0] + [n for n in (1, 2, 3) if n - 1 in wanted[i]] for i in wanted}

    def copies(i):
        return [
            pltpu.make_async_copy(given[n].at[i], buffers[n].at[i - first], sems.at[n, i - first]) for n in names[i]
        ]

    for i in wanted:
        for copy in copies(i):
            copy.start()

    inv, down, up, pay = buffers
    for i in wanted:
        for copy in copies(i):
            copy.wait()
        at = i - first
        here = split(inv[at])
        for k, block in ((0, down), (1, up)):
            if k in wanted[i]:
                place_operator(weight, i, k, dot_parts(here, split(block[at])))
        if 2 in wanted[i]:
            base[i] = dot_parts(split(pay[at]), here, dot_nt)


def prepare_kernel(inv, down, up, reward, weight, base, x_high, x_low, kept, *scratch):
    *buffers, sems = scratch
    wanted = {i: (0, 1, 2) if i < SOON - 1 else (0, 2) for i in range(SOON)}
    products(wanted, (inv, down, up, reward), weight, base, buffers, sems)
    response(0, SOON, x_high, x_low, weight, base, kept)


def prepare_rest_kernel(inv, down, up, reward, weight_soon, base_soon, weight, base, *scratch):
    *buffers, sems = scratch
    levels, phases = reward.shape[0], reward.shape[2]
    for i in range(SOON):
        rows = (4 if i < SOON - 1 else 2) * phases
        weight[i, 0:rows] = weight_soon[i, 0:rows]
    base[0:SOON] = base_soon[...]
    wanted = {i: (0, 1, 2) if i >= SOON else (1,) for i in range(SOON - 1, levels)}
    products(wanted, (inv, down, up, reward), weight, base, buffers, sems)


def respond_kernel(places, weight, base, x_high_soon, x_low_soon, kept, x_high, x_low):
    @pl.when(among(places))
    def _():
        x_high[0:SOON] = x_high_soon[...]
        x_low[0:SOON] = x_low_soon[...]
        response(SOON, AHEAD, x_high, x_low, weight, base, kept)


VMEM = pl.BlockSpec(memory_space=pltpu.VMEM)
HBM = pl.BlockSpec(memory_space=pltpu.HBM)


def operators(levels, columns, phases):
    return [resident((levels, 4 * phases, phases), BF16), resident((levels, columns, phases), F32)]


def buffers(levels, columns, phases):
    return (
        [pltpu.VMEM((levels, phases, phases), F32)] * 3
        + [pltpu.VMEM((levels, columns, phases), F32)]
        + [pltpu.SemaphoreType.DMA((4, levels))]
    )


def prepare(inverse_diag, down_block, up_block, reward):
    levels, columns, phases = reward.shape
    assert levels >= AHEAD
    rows = phases + columns
    given = [pin(x, pltpu.HBM) for x in (inverse_diag, down_block, up_block, reward)]
    *soon, kept_soon = pl.pallas_call(
        prepare_kernel,
        out_shape=operators(SOON, columns, phases)
        + [resident((SOON, rows, phases), BF16)] * 2
        + [resident((SOON, rows, phases), F32)],
        in_specs=[HBM] * 4,
        out_specs=[VMEM] * 5,
        scratch_shapes=buffers(SOON, columns, phases),
        compiler_params=pltpu.CompilerParams(vmem_limit_bytes=16 * 2**20),
        name="prepare",
    )(*given)
    weights = pl.pallas_call(
        prepare_rest_kernel,
        out_shape=operators(levels, columns, phases),
        in_specs=[HBM] * 4 + [VMEM] * 2,
        out_specs=[VMEM] * 2,
        scratch_shapes=buffers(levels - SOON + 1, columns, phases),
        compiler_params=pltpu.CompilerParams(vmem_limit_bytes=16 * 2**20),
        name="prepare_rest",
    )(*given, *[pin(x) for x in soon[:2]])
    return weights, soon[2:], kept_soon


def respond(places, weights, started):
    _, rows, phases = started[0].shape
    return pl.pallas_call(
        functools.partial(respond_kernel, tuple(places)),
        out_shape=resident((AHEAD - SOON, rows, phases), F32),
        in_specs=[VMEM] * 4,
        out_specs=VMEM,
        scratch_shapes=[pltpu.VMEM((AHEAD, rows, phases), BF16)] * 2,
        compiler_params=pltpu.CompilerParams(vmem_limit_bytes=16 * 2**20),
        name="respond",
    )(*[pin(x) for x in (*weights, *started)])


def stack(x):
    high = x.astype(BF16).astype(F32)
    return jnp.concatenate([high, x - high], axis=0).astype(BF16)


def fold(total):
    half = total.shape[0] // 2
    return total[:half] + total[half:]


def apply(terms):
    values = jnp.concatenate([x for x, _ in terms for _ in range(2)], axis=1)
    return fold(dot(values, jnp.concatenate([operator for _, operator in terms], axis=0)))


def apply_each(values, operator, columns):
    phases = operator.shape[1]
    values = jnp.concatenate(values, axis=0) if len(values) > 1 else values[0]
    total = dot(values, operator[0:phases]) + dot(values, operator[phases:])
    return [fold(total[at : at + 2 * columns]) for at in range(0, total.shape[0], 2 * columns)]


def whole(operator):
    return jnp.concatenate(split(operator), axis=0)


def kept_at(soon, late, j):
    return soon[j] if j < SOON else late[j - SOON]


def carried(soon, late, past, first, last):
    phases = soon.shape[2]
    above = {n: kept_at(soon, late, n - 1)[phases:] for n in range(max(first, 1), last + 1)}
    columns = soon.shape[1] - phases
    for j in range(last) if past else ():
        pairs = [(n, n - j) for n in above if n - j in past]
        if pairs:
            terms = [past[m] for _, m in pairs]
            for (n, _), term in zip(pairs, apply_each(terms, whole(kept_at(soon, late, j)[0:phases]), columns)):
                above[n] += term
    return above


def wave(first, weight, base, now, above, feedback, due, emit):
    levels, _, phases = base.shape
    for turn in range(levels + 2 * (CHUNK - 1)):
        for k in range(CHUNK):
            i = turn - 2 * k
            if not (0 <= i < levels and due(i, k)):
                continue
            n = first + 1 + k
            terms = []
            if (i - 1, n) in now:
                terms.append((now[i - 1, n], weight[i, 0 : 2 * phases]))
            if n > 1:
                over = stack(above[n - 1]) if i == levels - 1 else now[i + 1, n - 1]
                terms.append((over, weight[i, 2 * phases : 4 * phases]))
            value = base[i] + apply(terms) if terms else base[i]
            now[i, n] = stack(value)
            emit(i, k, value)
            if i == levels - 1:
                for later in range(n, first + CHUNK):
                    above[later] += apply([(now[i, n], feedback[later - n])])


def edge_level(levels, k):
    return levels - 2 - k


def chunk_kernel(chunk, places, part, names, *refs):
    given = dict(zip(names, refs))
    new_state, leaving = refs[len(names) :]
    weight, base = given["weight"], given["base"]
    levels, columns, phases = base.shape
    first = chunk * CHUNK

    @pl.when(jnp.logical_not(among(places)))
    def _():
        for name, target in (("state", new_state), ("leaving", leaving)):
            target[...] = given[name][...] if name in given else jnp.zeros_like(target)

    @pl.when(among(places))
    def _():
        zero = jnp.zeros((columns, phases), F32)
        above, feedback = {first + k: zero for k in range(CHUNK)}, []
        if part != "early":
            soon = given["soon"]
            feedback = [whole(soon[j, 0:phases]) for j in range(SOON)]
            if not first:
                above = carried(soon, None, {}, first, first + CHUNK - 1)
            elif "late" in given:
                past = {n + 1: stack(given["earlier"][n]) for n in range(first)}
                above = carried(soon, given["late"], past, first, first + CHUNK - 1)
            elif "returned" in given:
                above = {first + k: given["returned"][k] for k in range(CHUNK)}

        now = {}
        if part == "late":
            for k in range(CHUNK):
                now[edge_level(levels, k), first + 1 + k] = stack(given["edge"][k])
            new_state[...] = given["state"][...]
        elif first:
            for i in range(levels):
                now[i, first] = stack(given["state"][i])
        if part != "late" and "entering" in given:
            for k in range(CHUNK):
                now[-1, first + 1 + k] = stack(given["entering"][k])

        def due(i, k):
            return part == "all" or (i <= edge_level(levels, k)) == (part == "early")

        def emit(i, k, value):
            if k == CHUNK - 1:
                new_state[i] = value
            if i == (edge_level(levels, k) if part == "early" else levels - 1):
                leaving[k] = value

        wave(first, weight, base, now, above, feedback, due, emit)


def run_chunk(chunk, places, given, part="all"):
    given = {name: x for name, x in given.items() if x is not None}
    levels, columns, phases = given["base"].shape
    return pl.pallas_call(
        functools.partial(chunk_kernel, chunk, tuple(places), part, tuple(given)),
        out_shape=[resident((levels, columns, phases), F32), resident((CHUNK, columns, phases), F32)],
        in_specs=[VMEM] * len(given),
        out_specs=[VMEM] * 2,
        compiler_params=pltpu.CompilerParams(vmem_limit_bytes=16 * 2**20),
        name="chunk",
    )(*[pin(x) for x in given.values()])


def among(places):
    return functools.reduce(jnp.logical_or, [lax.axis_index("lvl") == place for place in places])


def slot_of(levels, a, i):
    return a * levels + i if a < CHUNK else CHUNK * levels + sum(AHEAD - n for n in range(CHUNK, a)) + i


def spread_kernel(places, weight, base, soon, high, low, kept, state, leaving, back_high, back_low, soon_high, soon_low):
    levels, columns, phases = base.shape
    rows = phases + columns
    top = levels - 1

    def step(a, i, terms, last=False):
        new = sum(dot_parts(x, y) for x, y in terms)
        unit, run = new[0:phases], new[phases:rows] + base[i]
        at = slot_of(levels, a, i)
        high[at, 0:phases], low[at, 0:phases] = split(unit)
        high[at, phases:rows], low[at, phases:rows] = split(run)
        if last and a >= SOON:
            kept[a - SOON, 0:phases], kept[a - SOON, phases:rows] = unit, run
        if a == CHUNK - 1:
            state[i] = run
        return run

    def get(a, i):
        at = slot_of(levels, a, i)
        return high[at], low[at]

    def below(a, i):
        return get(a, i - 1), operator(weight, i, 0)

    def above(a, i):
        return get(a - 1, i + 1), operator(weight, i, 1)

    @pl.when(among(places))
    def _():
        for j in range(CHUNK - 1):
            soon_high[j], soon_low[j] = split(soon[j, 0:phases])
        high[0, 0:phases], low[0, 0:phases] = operator(weight, 0, 0)
        high[0, phases:rows], low[0, phases:rows] = split(base[0])

        def up(i, _):
            step(0, i, [below(0, i)])
            return 0

        lax.fori_loop(1, levels, up, 0)
        leaving[0] = get(0, top)[0][phases:rows].astype(F32) + get(0, top)[1][phases:rows].astype(F32)
        for a in range(1, AHEAD):
            step(a, 0, [above(a, 0)], True)

            def both(i, _, a=a):
                step(a, i, [below(a, i), above(a, i)])
                return 0

            lax.fori_loop(1, top if a < CHUNK else AHEAD - a, both, 0)
            if a < CHUNK:
                back = sum(dot_parts(get(a - 1 - j, top), (soon_high[j], soon_low[j])) for j in range(a))
                back_high[0:phases], back_low[0:phases] = split(back[0:phases])
                back_high[phases:rows], back_low[phases:rows] = split(back[phases:rows] + soon[a - 1, phases:rows])
                terms = [below(a, top), ((back_high[...], back_low[...]), operator(weight, top, 1))]
                leaving[a] = step(a, top, terms)


def spread(places, weight, base, soon):
    levels, columns, phases = base.shape
    rows = phases + columns
    slots = slot_of(levels, AHEAD, 0)
    *ways, kept, state, leaving = pl.pallas_call(
        functools.partial(spread_kernel, tuple(places)),
        out_shape=[resident((slots, rows, phases), BF16)] * 2
        + [
            resident((AHEAD - SOON, rows, phases), F32),
            resident((levels, columns, phases), F32),
            resident((CHUNK, columns, phases), F32),
        ],
        in_specs=[VMEM] * 3,
        out_specs=[VMEM] * 5,
        scratch_shapes=[pltpu.VMEM((rows, phases), BF16)] * 2 + [pltpu.VMEM((CHUNK - 1, phases, phases), BF16)] * 2,
        compiler_params=pltpu.CompilerParams(vmem_limit_bytes=16 * 2**20),
        name="spread",
    )(*[pin(x) for x in (weight, base, soon)])
    return ways, kept, state, leaving


def finish_leaving_kernel(place, high, low, entering, leaving, before, new, *, levels):
    columns, phases = entering.shape[1:]

    @pl.when(lax.axis_index("lvl") != place)
    def _():
        new[...] = before[...]

    @pl.when(lax.axis_index("lvl") == place)
    def _():
        values = [stack(entering[k]) for k in range(CHUNK)]
        total = [leaving[k] for k in range(CHUNK)]
        for a in range(CHUNK):
            at = slot_of(levels, a, levels - 1)
            pair = jnp.concatenate([high[at, 0:phases], low[at, 0:phases]], axis=0)
            for k, term in enumerate(apply_each(values[: CHUNK - a], pair, columns)):
                total[a + k] += term
        for k in range(CHUNK):
            new[k] = total[k]


def finish_leaving(place, ways, entering, leaving, before, levels):
    return pl.pallas_call(
        functools.partial(finish_leaving_kernel, place, levels=levels),
        out_shape=resident(leaving.shape, F32),
        in_specs=[VMEM] * 5,
        out_specs=VMEM,
        compiler_params=pltpu.CompilerParams(vmem_limit_bytes=8 * 2**20),
        name="finish_leaving",
    )(*[pin(x) for x in (*ways, entering, leaving, before)])


def finish_state_kernel(place, high, low, entering, state, new):
    levels, _, phases = state.shape

    @pl.when(lax.axis_index("lvl") != place)
    def _():
        new[...] = state[...]

    @pl.when(lax.axis_index("lvl") == place)
    def _():
        values = [stack(entering[CHUNK - 1 - a]) for a in range(CHUNK)]
        for i in range(levels):
            terms = []
            for a in range(CHUNK):
                at = slot_of(levels, a, i)
                terms.append((values[a], jnp.concatenate([high[at, 0:phases], low[at, 0:phases]], axis=0)))
            new[i] = state[i] + apply(terms)


def finish_state(place, ways, entering, state, last):
    return pl.pallas_call(
        functools.partial(finish_state_kernel, place),
        out_shape=(jax.ShapeDtypeStruct if last else resident)(state.shape, F32),
        in_specs=[VMEM] * 4,
        out_specs=VMEM,
        compiler_params=pltpu.CompilerParams(vmem_limit_bytes=8 * 2**20),
        name="finish_state",
    )(*[pin(x) for x in (*ways, entering, state)])


def answer_kernel(step, soon, late, entering, returned):
    @pl.when(lax.axis_index("lvl") == step)
    def _():
        past = {n + 1: stack(entering[n]) for n in range(CHUNK)}
        above = carried(soon, late, past, CHUNK, 2 * CHUNK - 1)
        for k in range(CHUNK):
            returned[k] = above[CHUNK + k]


def answer(step, soon, late, entering):
    return pl.pallas_call(
        functools.partial(answer_kernel, step),
        out_shape=resident(entering.shape, F32),
        in_specs=[VMEM] * 3,
        out_specs=VMEM,
        compiler_params=pltpu.CompilerParams(vmem_limit_bytes=8 * 2**20),
        name="answer",
    )(*[pin(x) for x in (soon, late, entering)])


def local(inverse_diag, down_block, up_block, reward):
    given = reward.shape[1]
    columns = -(-given // 16) * 16
    if columns != given:
        reward = jnp.pad(reward, ((0, 0), (0, columns - given), (0, 0)))
    count = lax.axis_size("lvl")
    assert CHUNKS == 2 and count > 1
    top = count - 1
    ready = [d for d in range(1, count) if d % 2 == 0 or d == top]
    odd = [d for d in range(1, top, 2)]
    weights, begun, soon_here = prepare(inverse_diag, down_block, up_block, reward)
    weight, base = weights
    late_odd = respond(odd, weights, begun) if odd else None
    soon = lax.ppermute(soon_here, "lvl", [(d + 1, d) for d in range(top)])
    if odd:
        late = lax.ppermute(late_odd, "lvl", [(d, d - 1) for d in odd])
        soon, late_odd = lax.optimization_barrier((soon, late_odd))
    ways, late_here, state, parted_first = spread(ready, weight, base, soon)
    late_top = lax.ppermute(late_here, "lvl", [(top, top - 1)]) if top % 2 else None
    own = {"weight": weight, "base": base, "soon": soon}
    leaving = entering = parted = None
    for step in range(count + 1):
        place = step - 1
        earlier = leaving
        returned = edge = None
        if step % 2 == 0 and 0 < step < count:
            returned = lax.ppermute(answer(step, soon_here, late_here, entering), "lvl", [(step, place)])
            given_early = {"weight": weight, "base": base, "entering": entering, "state": state}
            state, edge = run_chunk(1, [place], given_early, "early")
        if place in ready and place < top:
            leaving = finish_leaving(place, ways, entering, parted, leaving, base.shape[0])
        if step in ready:
            if step < top:
                leaving = finish_leaving(step, ways, entering, parted_first, leaving, base.shape[0])
        elif step < count:
            state, leaving = run_chunk(
                0, [step], {**own, "entering": entering, "state": state, "leaving": leaving}
            )
        if step == 1:
            first_late = late if odd else late_top
            given_first = {**own, "late": first_late, "earlier": earlier, "state": state, "leaving": leaving}
            state, leaving = run_chunk(1, [0], given_first)
        if returned is not None:
            given_rest = {**own, "returned": returned, "edge": edge, "state": state, "leaving": leaving}
            state, leaving = run_chunk(1, [place], given_rest, "late")
        came = entering
        if step < count:
            pairs = [(d, d + 1) for d in (place, step) if 0 <= d < top]
            entering = lax.ppermute(leaving, "lvl", pairs) if pairs else None
        if place in ready:
            state = finish_state(place, ways, came, state, step == count)
        if step in ready:
            state = finish_state(step, ways, came, state, False)
            extra = {} if step == top else {"late": late_top if step == top - 1 else late, "earlier": leaving}
            state, parted = run_chunk(1, [step], {**own, **extra, "state": state})
    return state[:, :given] if columns != given else state


def solution(mesh):
    placed = (
        P(("grp", "lvl"), None, None),
        P(("grp", "lvl"), None, None),
        P(("grp", "lvl"), None, None),
        P(("grp", "lvl"), "col", None),
    )
    return jax.shard_map(
        local, mesh=mesh, in_specs=placed, out_specs=P(("grp", "lvl"), "col", None), check_vma=False
    )
```

```python
import functools

import jax
import jax.numpy as jnp
from jax import lax
from jax.experimental import pallas as pl
from jax.experimental.pallas import tpu as pltpu
from jax.sharding import PartitionSpec as P

SWEEPS = 8
CHUNK = 4
CHUNKS = SWEEPS // CHUNK
AHEAD = SWEEPS - 1
SOON = CHUNK - 1
F32 = jnp.float32
BF16 = jnp.bfloat16


def resident(shape, dtype):
    return pltpu.VMEM(shape, dtype)


def pin(x, memory=pltpu.VMEM):
    return pltpu.with_memory_space_constraint(x, memory)


def split(x):
    high = x.astype(BF16)
    return high, (x - high.astype(F32)).astype(BF16)


def dot(a, b):
    return jnp.dot(a, b, preferred_element_type=F32)


def dot_nt(a, b):
    return lax.dot_general(a, b, (((1,), (1,)), ((), ())), preferred_element_type=F32)


def dot_parts(a, b, dot=dot):
    return dot(a[0], b[0]) + (dot(a[0], b[1]) + dot(a[1], b[0]))


def place_operator(weight, i, k, value):
    phases = value.shape[0]
    for n, part in enumerate(split(value.T)):
        weight[i, (2 * k + n) * phases : (2 * k + n + 1) * phases] = part


def operator(weight, i, k):
    phases = weight.shape[2]
    at = 2 * k * phases
    return weight[i, at : at + phases], weight[i, at + phases : at + 2 * phases]


def response(first, last, x_high, x_low, weight, base, kept):
    _, columns, phases = base.shape
    rows = phases + columns

    def store(i, new):
        top = new[0:phases]
        end = new[phases:rows] + base[i]
        x_high[i, 0:phases], x_low[i, 0:phases] = split(top)
        x_high[i, phases:rows], x_low[i, phases:rows] = split(end)
        return top, end

    def from_below(i):
        return dot_parts((x_high[i - 1], x_low[i - 1]), operator(weight, i, 0))

    def from_above(i):
        return dot_parts((x_high[i + 1], x_low[i + 1]), operator(weight, i, 1))

    for d in range(first, last):
        if d == 0:
            high, low = weight[0, 0:phases], weight[0, phases : 2 * phases]
            x_high[0, 0:phases], x_low[0, 0:phases] = high, low
            x_high[0, phases:rows], x_low[0, phases:rows] = split(base[0])
            kept[0, 0:phases] = high.astype(F32) + low.astype(F32)
            kept[0, phases:rows] = base[0]
            continue
        store(d, from_below(d))

        def level(k, _, d=d):
            i = d - k
            store(i, from_below(i) + from_above(i))
            return 0

        lax.fori_loop(1, d, level, 0)
        kept[d - first, 0:phases], kept[d - first, phases:rows] = store(0, from_above(0))


def products(wanted, given, weight, base, buffers, sems):
    first = min(wanted)
    names = {i: [0] + [n for n in (1, 2, 3) if n - 1 in wanted[i]] for i in wanted}

    def copies(i):
        return [
            pltpu.make_async_copy(given[n].at[i], buffers[n].at[i - first], sems.at[n, i - first]) for n in names[i]
        ]

    for i in wanted:
        for copy in copies(i):
            copy.start()

    inv, down, up, pay = buffers
    for i in wanted:
        for copy in copies(i):
            copy.wait()
        at = i - first
        here = split(inv[at])
        for k, block in ((0, down), (1, up)):
            if k in wanted[i]:
                place_operator(weight, i, k, dot_parts(here, split(block[at])))
        if 2 in wanted[i]:
            base[i] = dot_parts(split(pay[at]), here, dot_nt)


def prepare_kernel(inv, down, up, reward, weight, base, x_high, x_low, kept, *scratch):
    *buffers, sems = scratch
    wanted = {i: (0, 1, 2) if i < SOON - 1 else (0, 2) for i in range(SOON)}
    products(wanted, (inv, down, up, reward), weight, base, buffers, sems)
    response(0, SOON, x_high, x_low, weight, base, kept)


def prepare_rest_kernel(inv, down, up, reward, weight_soon, base_soon, weight, base, *scratch):
    *buffers, sems = scratch
    levels, phases = reward.shape[0], reward.shape[2]
    for i in range(SOON):
        rows = (4 if i < SOON - 1 else 2) * phases
        weight[i, 0:rows] = weight_soon[i, 0:rows]
    base[0:SOON] = base_soon[...]
    wanted = {i: (0, 1, 2) if i >= SOON else (1,) for i in range(SOON - 1, levels)}
    products(wanted, (inv, down, up, reward), weight, base, buffers, sems)


def respond_kernel(places, weight, base, x_high_soon, x_low_soon, kept, x_high, x_low):
    @pl.when(among(places))
    def _():
        x_high[0:SOON] = x_high_soon[...]
        x_low[0:SOON] = x_low_soon[...]
        response(SOON, AHEAD, x_high, x_low, weight, base, kept)


VMEM = pl.BlockSpec(memory_space=pltpu.VMEM)
HBM = pl.BlockSpec(memory_space=pltpu.HBM)


def operators(levels, columns, phases):
    return [resident((levels, 4 * phases, phases), BF16), resident((levels, columns, phases), F32)]


def buffers(levels, columns, phases):
    return (
        [pltpu.VMEM((levels, phases, phases), F32)] * 3
        + [pltpu.VMEM((levels, columns, phases), F32)]
        + [pltpu.SemaphoreType.DMA((4, levels))]
    )


def prepare(inverse_diag, down_block, up_block, reward):
    levels, columns, phases = reward.shape
    assert levels >= AHEAD
    rows = phases + columns
    given = [pin(x, pltpu.HBM) for x in (inverse_diag, down_block, up_block, reward)]
    *soon, kept_soon = pl.pallas_call(
        prepare_kernel,
        out_shape=operators(SOON, columns, phases)
        + [resident((SOON, rows, phases), BF16)] * 2
        + [resident((SOON, rows, phases), F32)],
        in_specs=[HBM] * 4,
        out_specs=[VMEM] * 5,
        scratch_shapes=buffers(SOON, columns, phases),
        compiler_params=pltpu.CompilerParams(vmem_limit_bytes=16 * 2**20),
        name="prepare",
    )(*given)
    weights = pl.pallas_call(
        prepare_rest_kernel,
        out_shape=operators(levels, columns, phases),
        in_specs=[HBM] * 4 + [VMEM] * 2,
        out_specs=[VMEM] * 2,
        scratch_shapes=buffers(levels - SOON + 1, columns, phases),
        compiler_params=pltpu.CompilerParams(vmem_limit_bytes=16 * 2**20),
        name="prepare_rest",
    )(*given, *[pin(x) for x in soon[:2]])
    return weights, soon[2:], kept_soon


def respond(places, weights, started):
    _, rows, phases = started[0].shape
    return pl.pallas_call(
        functools.partial(respond_kernel, tuple(places)),
        out_shape=resident((AHEAD - SOON, rows, phases), F32),
        in_specs=[VMEM] * 4,
        out_specs=VMEM,
        scratch_shapes=[pltpu.VMEM((AHEAD, rows, phases), BF16)] * 2,
        compiler_params=pltpu.CompilerParams(vmem_limit_bytes=16 * 2**20),
        name="respond",
    )(*[pin(x) for x in (*weights, *started)])


def stack(x):
    high = x.astype(BF16).astype(F32)
    return jnp.concatenate([high, x - high], axis=0).astype(BF16)


def fold(total):
    half = total.shape[0] // 2
    return total[:half] + total[half:]


def apply(terms):
    values = jnp.concatenate([x for x, _ in terms for _ in range(2)], axis=1)
    return fold(dot(values, jnp.concatenate([operator for _, operator in terms], axis=0)))


def apply_each(values, operator, columns):
    phases = operator.shape[1]
    values = jnp.concatenate(values, axis=0) if len(values) > 1 else values[0]
    total = dot(values, operator[0:phases]) + dot(values, operator[phases:])
    return [fold(total[at : at + 2 * columns]) for at in range(0, total.shape[0], 2 * columns)]


def whole(operator):
    return jnp.concatenate(split(operator), axis=0)


def kept_at(soon, late, j):
    return soon[j] if j < SOON else late[j - SOON]


def carried(soon, late, past, first, last):
    phases = soon.shape[2]
    above = {n: kept_at(soon, late, n - 1)[phases:] for n in range(max(first, 1), last + 1)}
    columns = soon.shape[1] - phases
    for j in range(last) if past else ():
        pairs = [(n, n - j) for n in above if n - j in past]
        if pairs:
            terms = [past[m] for _, m in pairs]
            for (n, _), term in zip(pairs, apply_each(terms, whole(kept_at(soon, late, j)[0:phases]), columns)):
                above[n] += term
    return above


def wave(first, weight, base, now, above, feedback, due, emit):
    levels, _, phases = base.shape
    for turn in range(levels + 2 * (CHUNK - 1)):
        for k in range(CHUNK):
            i = turn - 2 * k
            if not (0 <= i < levels and due(i, k)):
                continue
            n = first + 1 + k
            terms = []
            if (i - 1, n) in now:
                terms.append((now[i - 1, n], weight[i, 0 : 2 * phases]))
            if n > 1:
                over = stack(above[n - 1]) if i == levels - 1 else now[i + 1, n - 1]
                terms.append((over, weight[i, 2 * phases : 4 * phases]))
            value = base[i] + apply(terms) if terms else base[i]
            now[i, n] = stack(value)
            emit(i, k, value)
            if i == levels - 1:
                for later in range(n, first + CHUNK):
                    above[later] += apply([(now[i, n], feedback[later - n])])


def edge_level(levels, k):
    return levels - 2 - k


def chunk_kernel(chunk, places, part, names, *refs):
    given = dict(zip(names, refs))
    new_state, leaving = refs[len(names) :]
    weight, base = given["weight"], given["base"]
    levels, columns, phases = base.shape
    first = chunk * CHUNK

    @pl.when(jnp.logical_not(among(places)))
    def _():
        for name, target in (("state", new_state), ("leaving", leaving)):
            target[...] = given[name][...] if name in given else jnp.zeros_like(target)

    @pl.when(among(places))
    def _():
        zero = jnp.zeros((columns, phases), F32)
        above, feedback = {first + k: zero for k in range(CHUNK)}, []
        if part != "early":
            soon = given["soon"]
            feedback = [whole(soon[j, 0:phases]) for j in range(SOON)]
            if not first:
                above = carried(soon, None, {}, first, first + CHUNK - 1)
            elif "late" in given:
                past = {n + 1: stack(given["earlier"][n]) for n in range(first)}
                above = carried(soon, given["late"], past, first, first + CHUNK - 1)
            elif "returned" in given:
                above = {first + k: given["returned"][k] for k in range(CHUNK)}

        now = {}
        if part == "late":
            for k in range(CHUNK):
                now[edge_level(levels, k), first + 1 + k] = stack(given["edge"][k])
            new_state[...] = given["state"][...]
        elif first:
            for i in range(levels):
                now[i, first] = stack(given["state"][i])
        if part != "late" and "entering" in given:
            for k in range(CHUNK):
                now[-1, first + 1 + k] = stack(given["entering"][k])

        def due(i, k):
            return part == "all" or (i <= edge_level(levels, k)) == (part == "early")

        def emit(i, k, value):
            if k == CHUNK - 1:
                new_state[i] = value
            if i == (edge_level(levels, k) if part == "early" else levels - 1):
                leaving[k] = value

        wave(first, weight, base, now, above, feedback, due, emit)


def run_chunk(chunk, places, given, part="all"):
    given = {name: x for name, x in given.items() if x is not None}
    levels, columns, phases = given["base"].shape
    return pl.pallas_call(
        functools.partial(chunk_kernel, chunk, tuple(places), part, tuple(given)),
        out_shape=[resident((levels, columns, phases), F32), resident((CHUNK, columns, phases), F32)],
        in_specs=[VMEM] * len(given),
        out_specs=[VMEM] * 2,
        compiler_params=pltpu.CompilerParams(vmem_limit_bytes=16 * 2**20),
        name="chunk",
    )(*[pin(x) for x in given.values()])


def among(places):
    return functools.reduce(jnp.logical_or, [lax.axis_index("lvl") == place for place in places])


def is_open(levels, a, i):
    return i + a < levels


def slot_of(levels, a, i):
    if not is_open(levels, a, i):
        return sum(range(1, a)) + i - (levels - a)
    return sum(levels - n if n < CHUNK else AHEAD - n for n in range(a)) + i


def get_answer(ways, levels, a, i, rows=slice(None)):
    high, low = ways[0:2] if is_open(levels, a, i) else ways[2:4]
    at = slot_of(levels, a, i)
    return high[at, rows], low[at, rows]


def spread_open_kernel(places, weight, base, high, low, kept):
    levels, columns, phases = base.shape
    rows = phases + columns

    def step(at, i, terms, keep=None):
        new = sum(dot_parts((high[x], low[x]), operator(weight, i, k)) for x, k in terms)
        unit, run = new[0:phases], new[phases:rows] + base[i]
        high[at, 0:phases], low[at, 0:phases] = split(unit)
        high[at, phases:rows], low[at, phases:rows] = split(run)
        if keep is not None:
            kept[keep, 0:phases], kept[keep, phases:rows] = unit, run

    @pl.when(among(places))
    def _():
        high[0, 0:phases], low[0, 0:phases] = operator(weight, 0, 0)
        high[0, phases:rows], low[0, phases:rows] = split(base[0])

        def up(i, _):
            step(i, i, [(i - 1, 0)])
            return 0

        lax.fori_loop(1, levels, up, 0)
        for a in range(1, AHEAD):
            first, old = slot_of(levels, a, 0), slot_of(levels, a - 1, 0)
            step(first, 0, [(old + 1, 1)], a - SOON if a >= SOON else None)

            def both(i, _, first=first, old=old):
                step(first + i, i, [(first + i - 1, 0), (old + i + 1, 1)])
                return 0

            lax.fori_loop(1, levels - a if a < CHUNK else AHEAD - a, both, 0)


def spread_close_kernel(
    places, weight, base, soon, open_high, open_low, before, high, low, state, leaving, feed_high, feed_low
):
    levels, columns, phases = base.shape
    rows = phases + columns
    top = levels - 1
    ways = (open_high, open_low, high, low)

    @pl.when(jnp.logical_not(among(places)))
    def _():
        state[...] = before[...]

    @pl.when(among(places))
    def _():
        for j in range(CHUNK - 1):
            feed_high[j], feed_low[j] = split(soon[j, 0:phases])
        for a in range(1, CHUNK):
            for i in range(levels - a, levels):
                new = dot_parts(get_answer(ways, levels, a, i - 1), operator(weight, i, 0))
                if i < top:
                    over = get_answer(ways, levels, a - 1, i + 1)
                else:
                    back = sum(
                        dot_parts(get_answer(ways, levels, a - 1 - j, top), (feed_high[j], feed_low[j])) for j in range(a)
                    )
                    end = back[phases:rows] + soon[a - 1, phases:rows]
                    over = split(jnp.concatenate([back[0:phases], end], axis=0))
                new += dot_parts(over, operator(weight, i, 1))
                at = slot_of(levels, a, i)
                high[at, 0:phases], low[at, 0:phases] = split(new[0:phases])
                high[at, phases:rows], low[at, phases:rows] = split(new[phases:rows] + base[i])

        def run(a, i):
            return sum(part.astype(F32) for part in get_answer(ways, levels, a, i, slice(phases, rows)))

        for i in range(levels):
            state[i] = run(CHUNK - 1, i)
        for a in range(CHUNK):
            leaving[a] = run(a, top)


def spread_open(places, weight, base):
    levels, columns, phases = base.shape
    assert levels > AHEAD and levels >= 2 * CHUNK - 1
    rows = phases + columns
    slots = slot_of(levels, AHEAD, 0)
    *ways, kept = pl.pallas_call(
        functools.partial(spread_open_kernel, tuple(places)),
        out_shape=[resident((slots, rows, phases), BF16)] * 2 + [resident((AHEAD - SOON, rows, phases), F32)],
        in_specs=[VMEM] * 2,
        out_specs=[VMEM] * 3,
        compiler_params=pltpu.CompilerParams(vmem_limit_bytes=16 * 2**20),
        name="spread_open",
    )(*[pin(x) for x in (weight, base)])
    return ways, kept


def spread_close(places, weight, base, soon, ways, state):
    levels, columns, phases = base.shape
    rows = phases + columns
    *more, state, leaving = pl.pallas_call(
        functools.partial(spread_close_kernel, tuple(places)),
        out_shape=[resident((sum(range(CHUNK)), rows, phases), BF16)] * 2
        + [resident((levels, columns, phases), F32), resident((CHUNK, columns, phases), F32)],
        in_specs=[VMEM] * 6,
        out_specs=[VMEM] * 4,
        scratch_shapes=[pltpu.VMEM((CHUNK - 1, phases, phases), BF16)] * 2,
        compiler_params=pltpu.CompilerParams(vmem_limit_bytes=16 * 2**20),
        name="spread_close",
    )(*[pin(x) for x in (weight, base, soon, *ways, state)])
    return [*ways, *more], state, leaving


def finish_leaving_kernel(place, *refs, levels):
    *ways, entering, leaving, before, new = refs
    columns, phases = entering.shape[1:]

    @pl.when(lax.axis_index("lvl") != place)
    def _():
        new[...] = before[...]

    @pl.when(lax.axis_index("lvl") == place)
    def _():
        values = [stack(entering[k]) for k in range(CHUNK)]
        total = [leaving[k] for k in range(CHUNK)]
        for a in range(CHUNK):
            pair = jnp.concatenate(get_answer(ways, levels, a, levels - 1, slice(0, phases)), axis=0)
            for k, term in enumerate(apply_each(values[: CHUNK - a], pair, columns)):
                total[a + k] += term
        for k in range(CHUNK):
            new[k] = total[k]


def finish_leaving(place, ways, entering, leaving, before, levels):
    return pl.pallas_call(
        functools.partial(finish_leaving_kernel, place, levels=levels),
        out_shape=resident(leaving.shape, F32),
        in_specs=[VMEM] * 7,
        out_specs=VMEM,
        compiler_params=pltpu.CompilerParams(vmem_limit_bytes=8 * 2**20),
        name="finish_leaving",
    )(*[pin(x) for x in (*ways, entering, leaving, before)])


def finish_state_kernel(place, *refs):
    *ways, entering, state, new = refs
    levels, _, phases = state.shape

    @pl.when(lax.axis_index("lvl") != place)
    def _():
        new[...] = state[...]

    @pl.when(lax.axis_index("lvl") == place)
    def _():
        values = [stack(entering[CHUNK - 1 - a]) for a in range(CHUNK)]
        for i in range(levels):
            terms = []
            for a in range(CHUNK):
                pair = jnp.concatenate(get_answer(ways, levels, a, i, slice(0, phases)), axis=0)
                terms.append((values[a], pair))
            new[i] = state[i] + apply(terms)


def finish_state(place, ways, entering, state, last):
    return pl.pallas_call(
        functools.partial(finish_state_kernel, place),
        out_shape=(jax.ShapeDtypeStruct if last else resident)(state.shape, F32),
        in_specs=[VMEM] * 6,
        out_specs=VMEM,
        compiler_params=pltpu.CompilerParams(vmem_limit_bytes=8 * 2**20),
        name="finish_state",
    )(*[pin(x) for x in (*ways, entering, state)])


def answer_kernel(step, soon, late, entering, returned):
    @pl.when(lax.axis_index("lvl") == step)
    def _():
        past = {n + 1: stack(entering[n]) for n in range(CHUNK)}
        above = carried(soon, late, past, CHUNK, 2 * CHUNK - 1)
        for k in range(CHUNK):
            returned[k] = above[CHUNK + k]


def answer(step, soon, late, entering):
    return pl.pallas_call(
        functools.partial(answer_kernel, step),
        out_shape=resident(entering.shape, F32),
        in_specs=[VMEM] * 3,
        out_specs=VMEM,
        compiler_params=pltpu.CompilerParams(vmem_limit_bytes=8 * 2**20),
        name="answer",
    )(*[pin(x) for x in (soon, late, entering)])


def local(inverse_diag, down_block, up_block, reward):
    given = reward.shape[1]
    columns = -(-given // 16) * 16
    if columns != given:
        reward = jnp.pad(reward, ((0, 0), (0, columns - given), (0, 0)))
    count = lax.axis_size("lvl")
    assert CHUNKS == 2 and count > 1
    top = count - 1
    ready = [d for d in range(1, count) if d % 2 == 0 or d == top]
    odd = [d for d in range(1, top, 2)]
    weights, begun, soon_here = prepare(inverse_diag, down_block, up_block, reward)
    weight, base = weights
    late_odd = respond(odd, weights, begun) if odd else None
    ways, late_here = spread_open(ready, weight, base)
    soon = lax.ppermute(soon_here, "lvl", [(d + 1, d) for d in range(top)])
    late = lax.ppermute(late_odd, "lvl", [(d, d - 1) for d in odd]) if odd else None
    soon, late_here, late_odd = lax.optimization_barrier((soon, late_here, late_odd))
    late_top = lax.ppermute(late_here, "lvl", [(top, top - 1)]) if top % 2 else None
    own = {"weight": weight, "base": base, "soon": soon}
    state = leaving = entering = parted = None
    for step in range(count + 1):
        place = step - 1
        earlier = leaving
        returned = edge = None
        if step % 2 == 0 and 0 < step < count:
            returned = lax.ppermute(answer(step, soon_here, late_here, entering), "lvl", [(step, place)])
            given_early = {"weight": weight, "base": base, "entering": entering, "state": state}
            state, edge = run_chunk(1, [place], given_early, "early")
        if place in ready and place < top:
            leaving = finish_leaving(place, ways, entering, parted, leaving, base.shape[0])
        if step in ready:
            if step < top:
                leaving = finish_leaving(step, ways, entering, parted_first, leaving, base.shape[0])
        elif step < count:
            state, leaving = run_chunk(
                0, [step], {**own, "entering": entering, "state": state, "leaving": leaving}
            )
        if step == 1:
            first_late = late if odd else late_top
            given_first = {**own, "late": first_late, "earlier": earlier, "state": state, "leaving": leaving}
            state, leaving = run_chunk(1, [0], given_first)
        if returned is not None:
            given_rest = {**own, "returned": returned, "edge": edge, "state": state, "leaving": leaving}
            state, leaving = run_chunk(1, [place], given_rest, "late")
        came = entering
        if step < count:
            pairs = [(d, d + 1) for d in (place, step) if 0 <= d < top]
            entering = lax.ppermute(leaving, "lvl", pairs) if pairs else None
        if step == 1:
            ways_then, leaving = lax.optimization_barrier((ways, leaving))
            ways, state, parted_first = spread_close(ready, weight, base, soon, ways_then, state)
            if entering is not None:
                entering, state = lax.optimization_barrier((entering, state))
        if place in ready:
            state = finish_state(place, ways, came, state, step == count)
        if step in ready:
            state = finish_state(step, ways, came, state, False)
            extra = {} if step == top else {"late": late_top if step == top - 1 else late, "earlier": leaving}
            state, parted = run_chunk(1, [step], {**own, **extra, "state": state})
    return state[:, :given] if columns != given else state


def solution(mesh):
    placed = (
        P(("grp", "lvl"), None, None),
        P(("grp", "lvl"), None, None),
        P(("grp", "lvl"), None, None),
        P(("grp", "lvl"), "col", None),
    )
    return jax.shard_map(
        local, mesh=mesh, in_specs=placed, out_specs=P(("grp", "lvl"), "col", None), check_vma=False
    )
```

```python
import functools

import jax
import jax.numpy as jnp
from jax import lax
from jax.experimental import pallas as pl
from jax.experimental.pallas import tpu as pltpu
from jax.sharding import PartitionSpec as P

SWEEPS = 8
CHUNK = 4
CHUNKS = SWEEPS // CHUNK
AHEAD = SWEEPS - 1
SOON = CHUNK - 1
F32 = jnp.float32
BF16 = jnp.bfloat16


def resident(shape, dtype):
    return pltpu.VMEM(shape, dtype)


def pin(x, memory=pltpu.VMEM):
    return pltpu.with_memory_space_constraint(x, memory)


def split(x):
    high = x.astype(BF16)
    return high, (x - high.astype(F32)).astype(BF16)


def dot(a, b):
    return jnp.dot(a, b, preferred_element_type=F32)


def dot_nt(a, b):
    return lax.dot_general(a, b, (((1,), (1,)), ((), ())), preferred_element_type=F32)


def dot_parts(a, b, dot=dot):
    return dot(a[0], b[0]) + (dot(a[0], b[1]) + dot(a[1], b[0]))


def place_operator(weight, i, k, value):
    phases = value.shape[0]
    for n, part in enumerate(split(value.T)):
        weight[i, (2 * k + n) * phases : (2 * k + n + 1) * phases] = part


def operator(weight, i, k):
    phases = weight.shape[2]
    at = 2 * k * phases
    return weight[i, at : at + phases], weight[i, at + phases : at + 2 * phases]


def response(first, last, x_high, x_low, weight, base, kept):
    _, columns, phases = base.shape
    rows = phases + columns

    def store(i, new):
        top = new[0:phases]
        end = new[phases:rows] + base[i]
        x_high[i, 0:phases], x_low[i, 0:phases] = split(top)
        x_high[i, phases:rows], x_low[i, phases:rows] = split(end)
        return top, end

    def from_below(i):
        return dot_parts((x_high[i - 1], x_low[i - 1]), operator(weight, i, 0))

    def from_above(i):
        return dot_parts((x_high[i + 1], x_low[i + 1]), operator(weight, i, 1))

    for d in range(first, last):
        if d == 0:
            high, low = weight[0, 0:phases], weight[0, phases : 2 * phases]
            x_high[0, 0:phases], x_low[0, 0:phases] = high, low
            x_high[0, phases:rows], x_low[0, phases:rows] = split(base[0])
            kept[0, 0:phases] = high.astype(F32) + low.astype(F32)
            kept[0, phases:rows] = base[0]
            continue
        store(d, from_below(d))

        def level(k, _, d=d):
            i = d - k
            store(i, from_below(i) + from_above(i))
            return 0

        lax.fori_loop(1, d, level, 0)
        kept[d - first, 0:phases], kept[d - first, phases:rows] = store(0, from_above(0))


def products(wanted, here_from, weight, base, inv, down, up, pay):
    for i in wanted:
        here_from(i)
        here = split(inv[i])
        for k, block in ((0, down), (1, up)):
            if k in wanted[i]:
                place_operator(weight, i, k, dot_parts(here, split(block[i])))
        if 2 in wanted[i]:
            base[i] = dot_parts(split(pay[i]), here, dot_nt)


def prepare_kernel(inv_far, down_far, up_far, pay_far, weight, base, x_high, x_low, kept, inv, down, up, pay, sems):
    levels = pay.shape[0]

    def copies(i):
        pairs = ((inv_far, inv), (down_far, down), (pay_far, pay), (up_far, up))
        return [pltpu.make_async_copy(far.at[i], near.at[i], sems.at[n, i]) for n, (far, near) in enumerate(pairs)]

    def wait(i):
        for copy in copies(i):
            copy.wait()

    for i in range(levels):
        for copy in copies(i):
            copy.start()
    wanted = {i: (0, 1, 2) if i < SOON - 1 else (0, 2) for i in range(SOON)}
    products(wanted, wait, weight, base, inv, down, up, pay)
    response(0, SOON, x_high, x_low, weight, base, kept)
    for i in range(SOON, levels):
        wait(i)


def prepare_rest_kernel(weight_soon, base_soon, inv, down, up, pay, weight, base):
    levels, _, phases = pay.shape
    for i in range(SOON):
        rows = (4 if i < SOON - 1 else 2) * phases
        weight[i, 0:rows] = weight_soon[i, 0:rows]
    base[0:SOON] = base_soon[...]
    wanted = {i: (0, 1, 2) if i >= SOON else (1,) for i in range(SOON - 1, levels)}
    products(wanted, lambda i: None, weight, base, inv, down, up, pay)


def respond_kernel(places, weight, base, x_high_soon, x_low_soon, kept, x_high, x_low):
    @pl.when(among(places))
    def _():
        x_high[0:SOON] = x_high_soon[...]
        x_low[0:SOON] = x_low_soon[...]
        response(SOON, AHEAD, x_high, x_low, weight, base, kept)


VMEM = pl.BlockSpec(memory_space=pltpu.VMEM)
HBM = pl.BlockSpec(memory_space=pltpu.HBM)


def operators(levels, columns, phases):
    return [resident((levels, 4 * phases, phases), BF16), resident((levels, columns, phases), F32)]


def prepare(inverse_diag, down_block, up_block, reward):
    levels, columns, phases = reward.shape
    rows = phases + columns
    matrix = resident((levels, phases, phases), F32)
    *soon, x_high, x_low, kept_soon, inv, down, up, pay = pl.pallas_call(
        prepare_kernel,
        out_shape=operators(SOON, columns, phases)
        + [resident((SOON, rows, phases), BF16)] * 2
        + [resident((SOON, rows, phases), F32)]
        + [matrix] * 3
        + [resident((levels, columns, phases), F32)],
        in_specs=[HBM] * 4,
        out_specs=[VMEM] * 9,
        scratch_shapes=[pltpu.SemaphoreType.DMA((4, levels))],
        compiler_params=pltpu.CompilerParams(vmem_limit_bytes=16 * 2**20),
        name="prepare",
    )(*[pin(x, pltpu.HBM) for x in (inverse_diag, down_block, up_block, reward)])
    weights = pl.pallas_call(
        prepare_rest_kernel,
        out_shape=operators(levels, columns, phases),
        in_specs=[VMEM] * 6,
        out_specs=[VMEM] * 2,
        compiler_params=pltpu.CompilerParams(vmem_limit_bytes=16 * 2**20),
        name="prepare_rest",
    )(*[pin(x) for x in (*soon, inv, down, up, pay)])
    return weights, (x_high, x_low), kept_soon


def respond(places, weights, started):
    _, rows, phases = started[0].shape
    return pl.pallas_call(
        functools.partial(respond_kernel, tuple(places)),
        out_shape=resident((AHEAD - SOON, rows, phases), F32),
        in_specs=[VMEM] * 4,
        out_specs=VMEM,
        scratch_shapes=[pltpu.VMEM((AHEAD, rows, phases), BF16)] * 2,
        compiler_params=pltpu.CompilerParams(vmem_limit_bytes=16 * 2**20),
        name="respond",
    )(*[pin(x) for x in (*weights, *started)])


def stack(x):
    high = x.astype(BF16).astype(F32)
    return jnp.concatenate([high, x - high], axis=0).astype(BF16)


def fold(total):
    half = total.shape[0] // 2
    return total[:half] + total[half:]


def apply(terms):
    values = jnp.concatenate([x for x, _ in terms for _ in range(2)], axis=1)
    return fold(dot(values, jnp.concatenate([operator for _, operator in terms], axis=0)))


def apply_each(values, operator, columns):
    phases = operator.shape[1]
    values = jnp.concatenate(values, axis=0) if len(values) > 1 else values[0]
    total = dot(values, operator[0:phases]) + dot(values, operator[phases:])
    return [fold(total[at : at + 2 * columns]) for at in range(0, total.shape[0], 2 * columns)]


def whole(operator):
    return jnp.concatenate(split(operator), axis=0)


def kept_at(soon, late, j):
    return soon[j] if j < SOON else late[j - SOON]


def carried(soon, late, past, first, last):
    phases = soon.shape[2]
    above = {n: kept_at(soon, late, n - 1)[phases:] for n in range(max(first, 1), last + 1)}
    columns = soon.shape[1] - phases
    for j in range(last) if past else ():
        pairs = [(n, n - j) for n in above if n - j in past]
        if pairs:
            terms = [past[m] for _, m in pairs]
            for (n, _), term in zip(pairs, apply_each(terms, whole(kept_at(soon, late, j)[0:phases]), columns)):
                above[n] += term
    return above


def wave(first, weight, base, now, above, feedback, due, emit):
    levels, _, phases = base.shape
    for turn in range(levels + 2 * (CHUNK - 1)):
        for k in range(CHUNK):
            i = turn - 2 * k
            if not (0 <= i < levels and due(i, k)):
                continue
            n = first + 1 + k
            terms = []
            if (i - 1, n) in now:
                terms.append((now[i - 1, n], weight[i, 0 : 2 * phases]))
            if n > 1:
                over = stack(above[n - 1]) if i == levels - 1 else now[i + 1, n - 1]
                terms.append((over, weight[i, 2 * phases : 4 * phases]))
            value = base[i] + apply(terms) if terms else base[i]
            now[i, n] = stack(value)
            emit(i, k, value)
            if i == levels - 1:
                for later in range(n, first + CHUNK):
                    above[later] += apply([(now[i, n], feedback[later - n])])


def edge_level(levels, k):
    return levels - 2 - k


def chunk_kernel(chunk, places, part, names, *refs):
    given = dict(zip(names, refs))
    new_state, leaving = refs[len(names) :]
    weight, base = given["weight"], given["base"]
    levels, columns, phases = base.shape
    first = chunk * CHUNK

    @pl.when(jnp.logical_not(among(places)))
    def _():
        for name, target in (("state", new_state), ("leaving", leaving)):
            target[...] = given[name][...] if name in given else jnp.zeros_like(target)

    @pl.when(among(places))
    def _():
        zero = jnp.zeros((columns, phases), F32)
        above, feedback = {first + k: zero for k in range(CHUNK)}, []
        if part != "early":
            soon = given["soon"]
            feedback = [whole(soon[j, 0:phases]) for j in range(SOON)]
            if not first:
                above = carried(soon, None, {}, first, first + CHUNK - 1)
            elif "late" in given:
                past = {n + 1: stack(given["earlier"][n]) for n in range(first)}
                above = carried(soon, given["late"], past, first, first + CHUNK - 1)
            elif "returned" in given:
                above = {first + k: given["returned"][k] for k in range(CHUNK)}

        now = {}
        if part == "late":
            for k in range(CHUNK):
                now[edge_level(levels, k), first + 1 + k] = stack(given["edge"][k])
            new_state[...] = given["state"][...]
        elif first:
            for i in range(levels):
                now[i, first] = stack(given["state"][i])
        if part != "late" and "entering" in given:
            for k in range(CHUNK):
                now[-1, first + 1 + k] = stack(given["entering"][k])

        def due(i, k):
            return part == "all" or (i <= edge_level(levels, k)) == (part == "early")

        def emit(i, k, value):
            if k == CHUNK - 1:
                new_state[i] = value
            if i == (edge_level(levels, k) if part == "early" else levels - 1):
                leaving[k] = value

        wave(first, weight, base, now, above, feedback, due, emit)


def run_chunk(chunk, places, given, part="all"):
    given = {name: x for name, x in given.items() if x is not None}
    levels, columns, phases = given["base"].shape
    return pl.pallas_call(
        functools.partial(chunk_kernel, chunk, tuple(places), part, tuple(given)),
        out_shape=[resident((levels, columns, phases), F32), resident((CHUNK, columns, phases), F32)],
        in_specs=[VMEM] * len(given),
        out_specs=[VMEM] * 2,
        compiler_params=pltpu.CompilerParams(vmem_limit_bytes=16 * 2**20),
        name="chunk",
    )(*[pin(x) for x in given.values()])


def among(places):
    return functools.reduce(jnp.logical_or, [lax.axis_index("lvl") == place for place in places])


def is_open(levels, a, i):
    return i + a < levels


def slot_of(levels, a, i):
    if not is_open(levels, a, i):
        return sum(range(1, a)) + i - (levels - a)
    return sum(levels - n if n < CHUNK else AHEAD - n for n in range(a)) + i


def get_answer(ways, levels, a, i, rows=slice(None)):
    high, low = ways[0:2] if is_open(levels, a, i) else ways[2:4]
    at = slot_of(levels, a, i)
    return high[at, rows], low[at, rows]


def spread_open_kernel(places, weight, base, high, low, kept):
    levels, columns, phases = base.shape
    rows = phases + columns

    def step(at, i, terms, keep=None):
        new = sum(dot_parts((high[x], low[x]), operator(weight, i, k)) for x, k in terms)
        unit, run = new[0:phases], new[phases:rows] + base[i]
        high[at, 0:phases], low[at, 0:phases] = split(unit)
        high[at, phases:rows], low[at, phases:rows] = split(run)
        if keep is not None:
            kept[keep, 0:phases], kept[keep, phases:rows] = unit, run

    @pl.when(among(places))
    def _():
        high[0, 0:phases], low[0, 0:phases] = operator(weight, 0, 0)
        high[0, phases:rows], low[0, phases:rows] = split(base[0])

        def up(i, _):
            step(i, i, [(i - 1, 0)])
            return 0

        lax.fori_loop(1, levels, up, 0)
        for a in range(1, AHEAD):
            first, old = slot_of(levels, a, 0), slot_of(levels, a - 1, 0)
            step(first, 0, [(old + 1, 1)], a - SOON if a >= SOON else None)

            def both(i, _, first=first, old=old):
                step(first + i, i, [(first + i - 1, 0), (old + i + 1, 1)])
                return 0

            lax.fori_loop(1, levels - a if a < CHUNK else AHEAD - a, both, 0)


def spread_close_kernel(
    places, weight, base, soon, open_high, open_low, before, high, low, state, leaving, feed_high, feed_low
):
    levels, columns, phases = base.shape
    rows = phases + columns
    top = levels - 1
    ways = (open_high, open_low, high, low)

    @pl.when(jnp.logical_not(among(places)))
    def _():
        state[...] = before[...]

    @pl.when(among(places))
    def _():
        for j in range(CHUNK - 1):
            feed_high[j], feed_low[j] = split(soon[j, 0:phases])
        for a in range(1, CHUNK):
            for i in range(levels - a, levels):
                new = dot_parts(get_answer(ways, levels, a, i - 1), operator(weight, i, 0))
                if i < top:
                    over = get_answer(ways, levels, a - 1, i + 1)
                else:
                    back = sum(
                        dot_parts(get_answer(ways, levels, a - 1 - j, top), (feed_high[j], feed_low[j])) for j in range(a)
                    )
                    end = back[phases:rows] + soon[a - 1, phases:rows]
                    over = split(jnp.concatenate([back[0:phases], end], axis=0))
                new += dot_parts(over, operator(weight, i, 1))
                at = slot_of(levels, a, i)
                high[at, 0:phases], low[at, 0:phases] = split(new[0:phases])
                high[at, phases:rows], low[at, phases:rows] = split(new[phases:rows] + base[i])

        def run(a, i):
            return sum(part.astype(F32) for part in get_answer(ways, levels, a, i, slice(phases, rows)))

        for i in range(levels):
            state[i] = run(CHUNK - 1, i)
        for a in range(CHUNK):
            leaving[a] = run(a, top)


def spread_open(places, weight, base):
    levels, columns, phases = base.shape
    assert levels > AHEAD and levels >= 2 * CHUNK - 1
    rows = phases + columns
    slots = slot_of(levels, AHEAD, 0)
    *ways, kept = pl.pallas_call(
        functools.partial(spread_open_kernel, tuple(places)),
        out_shape=[resident((slots, rows, phases), BF16)] * 2 + [resident((AHEAD - SOON, rows, phases), F32)],
        in_specs=[VMEM] * 2,
        out_specs=[VMEM] * 3,
        compiler_params=pltpu.CompilerParams(vmem_limit_bytes=16 * 2**20),
        name="spread_open",
    )(*[pin(x) for x in (weight, base)])
    return ways, kept


def spread_close(places, weight, base, soon, ways, state):
    levels, columns, phases = base.shape
    rows = phases + columns
    *more, state, leaving = pl.pallas_call(
        functools.partial(spread_close_kernel, tuple(places)),
        out_shape=[resident((sum(range(CHUNK)), rows, phases), BF16)] * 2
        + [resident((levels, columns, phases), F32), resident((CHUNK, columns, phases), F32)],
        in_specs=[VMEM] * 6,
        out_specs=[VMEM] * 4,
        scratch_shapes=[pltpu.VMEM((CHUNK - 1, phases, phases), BF16)] * 2,
        compiler_params=pltpu.CompilerParams(vmem_limit_bytes=16 * 2**20),
        name="spread_close",
    )(*[pin(x) for x in (weight, base, soon, *ways, state)])
    return [*ways, *more], state, leaving


def finish_leaving_kernel(place, *refs, levels):
    *ways, entering, leaving, before, new = refs
    columns, phases = entering.shape[1:]

    @pl.when(lax.axis_index("lvl") != place)
    def _():
        new[...] = before[...]

    @pl.when(lax.axis_index("lvl") == place)
    def _():
        values = [stack(entering[k]) for k in range(CHUNK)]
        total = [leaving[k] for k in range(CHUNK)]
        for a in range(CHUNK):
            pair = jnp.concatenate(get_answer(ways, levels, a, levels - 1, slice(0, phases)), axis=0)
            for k, term in enumerate(apply_each(values[: CHUNK - a], pair, columns)):
                total[a + k] += term
        for k in range(CHUNK):
            new[k] = total[k]


def finish_leaving(place, ways, entering, leaving, before, levels):
    return pl.pallas_call(
        functools.partial(finish_leaving_kernel, place, levels=levels),
        out_shape=resident(leaving.shape, F32),
        in_specs=[VMEM] * 7,
        out_specs=VMEM,
        compiler_params=pltpu.CompilerParams(vmem_limit_bytes=8 * 2**20),
        name="finish_leaving",
    )(*[pin(x) for x in (*ways, entering, leaving, before)])


def finish_state_kernel(place, *refs):
    *ways, entering, state, new = refs
    levels, _, phases = state.shape

    @pl.when(lax.axis_index("lvl") != place)
    def _():
        new[...] = state[...]

    @pl.when(lax.axis_index("lvl") == place)
    def _():
        values = [stack(entering[CHUNK - 1 - a]) for a in range(CHUNK)]
        for i in range(levels):
            terms = []
            for a in range(CHUNK):
                pair = jnp.concatenate(get_answer(ways, levels, a, i, slice(0, phases)), axis=0)
                terms.append((values[a], pair))
            new[i] = state[i] + apply(terms)


def finish_state(place, ways, entering, state, last):
    return pl.pallas_call(
        functools.partial(finish_state_kernel, place),
        out_shape=(jax.ShapeDtypeStruct if last else resident)(state.shape, F32),
        in_specs=[VMEM] * 6,
        out_specs=VMEM,
        compiler_params=pltpu.CompilerParams(vmem_limit_bytes=8 * 2**20),
        name="finish_state",
    )(*[pin(x) for x in (*ways, entering, state)])


def answer_kernel(step, soon, late, entering, returned):
    @pl.when(lax.axis_index("lvl") == step)
    def _():
        past = {n + 1: stack(entering[n]) for n in range(CHUNK)}
        above = carried(soon, late, past, CHUNK, 2 * CHUNK - 1)
        for k in range(CHUNK):
            returned[k] = above[CHUNK + k]


def answer(step, soon, late, entering):
    return pl.pallas_call(
        functools.partial(answer_kernel, step),
        out_shape=resident(entering.shape, F32),
        in_specs=[VMEM] * 3,
        out_specs=VMEM,
        compiler_params=pltpu.CompilerParams(vmem_limit_bytes=8 * 2**20),
        name="answer",
    )(*[pin(x) for x in (soon, late, entering)])


def local(inverse_diag, down_block, up_block, reward):
    given = reward.shape[1]
    columns = -(-given // 16) * 16
    if columns != given:
        reward = jnp.pad(reward, ((0, 0), (0, columns - given), (0, 0)))
    count = lax.axis_size("lvl")
    assert CHUNKS == 2 and count > 1
    top = count - 1
    ready = [d for d in range(1, count) if d % 2 == 0 or d == top]
    odd = [d for d in range(1, top, 2)]
    weights, begun, soon_here = prepare(inverse_diag, down_block, up_block, reward)
    weight, base = weights
    late_odd = respond(odd, weights, begun) if odd else None
    ways, late_here = spread_open(ready, weight, base)
    soon = lax.ppermute(soon_here, "lvl", [(d + 1, d) for d in range(top)])
    late = lax.ppermute(late_odd, "lvl", [(d, d - 1) for d in odd]) if odd else None
    soon, late_here, late_odd = lax.optimization_barrier((soon, late_here, late_odd))
    late_top = lax.ppermute(late_here, "lvl", [(top, top - 1)]) if top % 2 else None
    own = {"weight": weight, "base": base, "soon": soon}
    state = leaving = entering = parted = None
    for step in range(count + 1):
        place = step - 1
        earlier = leaving
        returned = edge = None
        if step % 2 == 0 and 0 < step < count:
            returned = lax.ppermute(answer(step, soon_here, late_here, entering), "lvl", [(step, place)])
            given_early = {"weight": weight, "base": base, "entering": entering, "state": state}
            state, edge = run_chunk(1, [place], given_early, "early")
        if place in ready and place < top:
            leaving = finish_leaving(place, ways, entering, parted, leaving, base.shape[0])
        if step in ready:
            if step < top:
                leaving = finish_leaving(step, ways, entering, parted_first, leaving, base.shape[0])
        elif step < count:
            state, leaving = run_chunk(
                0, [step], {**own, "entering": entering, "state": state, "leaving": leaving}
            )
        if step == 1:
            first_late = late if odd else late_top
            given_first = {**own, "late": first_late, "earlier": earlier, "state": state, "leaving": leaving}
            state, leaving = run_chunk(1, [0], given_first)
        if returned is not None:
            given_rest = {**own, "returned": returned, "edge": edge, "state": state, "leaving": leaving}
            state, leaving = run_chunk(1, [place], given_rest, "late")
        came = entering
        if step < count:
            pairs = [(d, d + 1) for d in (place, step) if 0 <= d < top]
            entering = lax.ppermute(leaving, "lvl", pairs) if pairs else None
        if step == 1:
            ways_then, leaving = lax.optimization_barrier((ways, leaving))
            ways, state, parted_first = spread_close(ready, weight, base, soon, ways_then, state)
            if entering is not None:
                entering, state = lax.optimization_barrier((entering, state))
        if place in ready:
            state = finish_state(place, ways, came, state, step == count)
        if step in ready:
            state = finish_state(step, ways, came, state, False)
            extra = {} if step == top else {"late": late_top if step == top - 1 else late, "earlier": leaving}
            state, parted = run_chunk(1, [step], {**own, **extra, "state": state})
    return state[:, :given] if columns != given else state


def solution(mesh):
    placed = (
        P(("grp", "lvl"), None, None),
        P(("grp", "lvl"), None, None),
        P(("grp", "lvl"), None, None),
        P(("grp", "lvl"), "col", None),
    )
    return jax.shard_map(
        local, mesh=mesh, in_specs=placed, out_specs=P(("grp", "lvl"), "col", None), check_vma=False
    )
```

```python
import functools

import jax
import jax.numpy as jnp
from jax import lax
from jax.experimental import pallas as pl
from jax.experimental.pallas import tpu as pltpu
from jax.sharding import PartitionSpec as P

SWEEPS = 8
CHUNK = 4
CHUNKS = SWEEPS // CHUNK
AHEAD = SWEEPS - 1
SOON = CHUNK - 1
F32 = jnp.float32
BF16 = jnp.bfloat16


def resident(shape, dtype):
    return pltpu.VMEM(shape, dtype)


def pin(x, memory=pltpu.VMEM):
    return pltpu.with_memory_space_constraint(x, memory)


def split(x):
    high = x.astype(BF16)
    return high, (x - high.astype(F32)).astype(BF16)


def dot(a, b):
    return jnp.dot(a, b, preferred_element_type=F32)


def dot_nt(a, b):
    return lax.dot_general(a, b, (((1,), (1,)), ((), ())), preferred_element_type=F32)


def dot_parts(a, b, dot=dot):
    return dot(a[0], b[0]) + (dot(a[0], b[1]) + dot(a[1], b[0]))


def place_operator(weight, i, k, value):
    phases = value.shape[0]
    for n, part in enumerate(split(value.T)):
        weight[i, (2 * k + n) * phases : (2 * k + n + 1) * phases] = part


def operator(weight, i, k):
    phases = weight.shape[2]
    at = 2 * k * phases
    return weight[i, at : at + phases], weight[i, at + phases : at + 2 * phases]


def response(first, last, x_high, x_low, weight, base, kept):
    _, columns, phases = base.shape
    rows = phases + columns

    def store(i, new):
        top = new[0:phases]
        end = new[phases:rows] + base[i]
        x_high[i, 0:phases], x_low[i, 0:phases] = split(top)
        x_high[i, phases:rows], x_low[i, phases:rows] = split(end)
        return top, end

    def from_below(i):
        return dot_parts((x_high[i - 1], x_low[i - 1]), operator(weight, i, 0))

    def from_above(i):
        return dot_parts((x_high[i + 1], x_low[i + 1]), operator(weight, i, 1))

    for d in range(first, last):
        if d == 0:
            high, low = weight[0, 0:phases], weight[0, phases : 2 * phases]
            x_high[0, 0:phases], x_low[0, 0:phases] = high, low
            x_high[0, phases:rows], x_low[0, phases:rows] = split(base[0])
            kept[0, 0:phases] = high.astype(F32) + low.astype(F32)
            kept[0, phases:rows] = base[0]
            continue
        store(d, from_below(d))

        def level(k, _, d=d):
            i = d - k
            store(i, from_below(i) + from_above(i))
            return 0

        lax.fori_loop(1, d, level, 0)
        kept[d - first, 0:phases], kept[d - first, phases:rows] = store(0, from_above(0))


def products(wanted, here_from, weight, base, inv, down, up, pay):
    for i in wanted:
        here_from(i)
        here = split(inv[i])
        for k, block in ((0, down), (1, up)):
            if k in wanted[i]:
                place_operator(weight, i, k, dot_parts(here, split(block[i])))
        if 2 in wanted[i]:
            base[i] = dot_parts(split(pay[i]), here, dot_nt)


def prepare_kernel(inv_far, down_far, up_far, pay_far, weight, base, x_high, x_low, kept, inv, down, up, pay, sems):
    levels = pay.shape[0]

    def copies(i):
        pairs = ((inv_far, inv), (down_far, down), (pay_far, pay), (up_far, up))
        return [pltpu.make_async_copy(far.at[i], near.at[i], sems.at[n, i]) for n, (far, near) in enumerate(pairs)]

    def wait(i):
        for copy in copies(i):
            copy.wait()

    for i in range(levels):
        for copy in copies(i):
            copy.start()
    wanted = {i: (0, 1, 2) if i < SOON - 1 else (0, 2) for i in range(SOON)}
    products(wanted, wait, weight, base, inv, down, up, pay)
    response(0, SOON, x_high, x_low, weight, base, kept)
    for i in range(SOON, levels):
        wait(i)


def prepare_rest_kernel(weight_soon, base_soon, inv, down, up, pay, weight, base):
    levels, _, phases = pay.shape
    for i in range(SOON):
        rows = (4 if i < SOON - 1 else 2) * phases
        weight[i, 0:rows] = weight_soon[i, 0:rows]
    base[0:SOON] = base_soon[...]
    wanted = {i: (0, 1, 2) if i >= SOON else (1,) for i in range(SOON - 1, levels)}
    products(wanted, lambda i: None, weight, base, inv, down, up, pay)


def respond_kernel(places, weight, base, x_high_soon, x_low_soon, kept, x_high, x_low):
    @pl.when(among(places))
    def _():
        x_high[0:SOON] = x_high_soon[...]
        x_low[0:SOON] = x_low_soon[...]
        response(SOON, AHEAD, x_high, x_low, weight, base, kept)


VMEM = pl.BlockSpec(memory_space=pltpu.VMEM)
HBM = pl.BlockSpec(memory_space=pltpu.HBM)


def operators(levels, columns, phases):
    return [resident((levels, 4 * phases, phases), BF16), resident((levels, columns, phases), F32)]


def prepare(inverse_diag, down_block, up_block, reward):
    levels, columns, phases = reward.shape
    rows = phases + columns
    matrix = resident((levels, phases, phases), F32)
    *soon, x_high, x_low, kept_soon, inv, down, up, pay = pl.pallas_call(
        prepare_kernel,
        out_shape=operators(SOON, columns, phases)
        + [resident((SOON, rows, phases), BF16)] * 2
        + [resident((SOON, rows, phases), F32)]
        + [matrix] * 3
        + [resident((levels, columns, phases), F32)],
        in_specs=[HBM] * 4,
        out_specs=[VMEM] * 9,
        scratch_shapes=[pltpu.SemaphoreType.DMA((4, levels))],
        compiler_params=pltpu.CompilerParams(vmem_limit_bytes=16 * 2**20),
        name="prepare",
    )(*[pin(x, pltpu.HBM) for x in (inverse_diag, down_block, up_block, reward)])
    weights = pl.pallas_call(
        prepare_rest_kernel,
        out_shape=operators(levels, columns, phases),
        in_specs=[VMEM] * 6,
        out_specs=[VMEM] * 2,
        compiler_params=pltpu.CompilerParams(vmem_limit_bytes=16 * 2**20),
        name="prepare_rest",
    )(*[pin(x) for x in (*soon, inv, down, up, pay)])
    return weights, (x_high, x_low), kept_soon


def respond(places, weights, started):
    _, rows, phases = started[0].shape
    return pl.pallas_call(
        functools.partial(respond_kernel, tuple(places)),
        out_shape=resident((AHEAD - SOON, rows, phases), F32),
        in_specs=[VMEM] * 4,
        out_specs=VMEM,
        scratch_shapes=[pltpu.VMEM((AHEAD, rows, phases), BF16)] * 2,
        compiler_params=pltpu.CompilerParams(vmem_limit_bytes=16 * 2**20),
        name="respond",
    )(*[pin(x) for x in (*weights, *started)])


def stack(x):
    high = x.astype(BF16).astype(F32)
    return jnp.concatenate([high, x - high], axis=0).astype(BF16)


def fold(total):
    half = total.shape[0] // 2
    return total[:half] + total[half:]


def apply(terms):
    values = jnp.concatenate([x for x, _ in terms for _ in range(2)], axis=1)
    return fold(dot(values, jnp.concatenate([operator for _, operator in terms], axis=0)))


def apply_each(values, operator, columns):
    phases = operator.shape[1]
    values = jnp.concatenate(values, axis=0) if len(values) > 1 else values[0]
    total = dot(values, operator[0:phases]) + dot(values, operator[phases:])
    return [fold(total[at : at + 2 * columns]) for at in range(0, total.shape[0], 2 * columns)]


def whole(operator):
    return jnp.concatenate(split(operator), axis=0)


def kept_at(soon, late, j):
    return soon[j] if j < SOON else late[j - SOON]


def carried(soon, late, past, first, last):
    phases = soon.shape[2]
    above = {n: kept_at(soon, late, n - 1)[phases:] for n in range(max(first, 1), last + 1)}
    columns = soon.shape[1] - phases
    for j in range(last) if past else ():
        pairs = [(n, n - j) for n in above if n - j in past]
        if pairs:
            terms = [past[m] for _, m in pairs]
            for (n, _), term in zip(pairs, apply_each(terms, whole(kept_at(soon, late, j)[0:phases]), columns)):
                above[n] += term
    return above


def wave(first, weight, base, now, above, feedback, due, emit):
    levels, _, phases = base.shape
    for turn in range(levels + 2 * (CHUNK - 1)):
        for k in range(CHUNK):
            i = turn - 2 * k
            if not (0 <= i < levels and due(i, k)):
                continue
            n = first + 1 + k
            terms = []
            if (i - 1, n) in now:
                terms.append((now[i - 1, n], weight[i, 0 : 2 * phases]))
            if n > 1:
                over = stack(above[n - 1]) if i == levels - 1 else now[i + 1, n - 1]
                terms.append((over, weight[i, 2 * phases : 4 * phases]))
            value = base[i] + apply(terms) if terms else base[i]
            now[i, n] = stack(value)
            emit(i, k, value)
            if i == levels - 1:
                for later in range(n, first + CHUNK):
                    above[later] += apply([(now[i, n], feedback[later - n])])


def edge_level(levels, k):
    return levels - 2 - k


def chunk_kernel(chunk, places, part, names, *refs):
    given = dict(zip(names, refs))
    new_state, leaving = refs[len(names) :]
    weight, base = given["weight"], given["base"]
    levels, columns, phases = base.shape
    first = chunk * CHUNK

    @pl.when(jnp.logical_not(among(places)))
    def _():
        for name, target in (("state", new_state), ("leaving", leaving)):
            target[...] = given[name][...] if name in given else jnp.zeros_like(target)

    @pl.when(among(places))
    def _():
        zero = jnp.zeros((columns, phases), F32)
        above, feedback = {first + k: zero for k in range(CHUNK)}, []
        if part != "early":
            soon = given["soon"]
            feedback = [whole(soon[j, 0:phases]) for j in range(SOON)]
            if not first:
                above = carried(soon, None, {}, first, first + CHUNK - 1)
            elif "late" in given:
                past = {n + 1: stack(given["earlier"][n]) for n in range(first)}
                above = carried(soon, given["late"], past, first, first + CHUNK - 1)
            elif "returned" in given:
                above = {first + k: given["returned"][k] for k in range(CHUNK)}

        now = {}
        if part == "late":
            for k in range(CHUNK):
                now[edge_level(levels, k), first + 1 + k] = stack(given["edge"][k])
            new_state[...] = given["state"][...]
        elif first:
            for i in range(levels):
                now[i, first] = stack(given["state"][i])
        if part != "late" and "entering" in given:
            for k in range(CHUNK):
                now[-1, first + 1 + k] = stack(given["entering"][k])

        def due(i, k):
            return part == "all" or (i <= edge_level(levels, k)) == (part == "early")

        def emit(i, k, value):
            if k == CHUNK - 1:
                new_state[i] = value
            if i == (edge_level(levels, k) if part == "early" else levels - 1):
                leaving[k] = value

        wave(first, weight, base, now, above, feedback, due, emit)


def run_chunk(chunk, places, given, part="all"):
    given = {name: x for name, x in given.items() if x is not None}
    levels, columns, phases = given["base"].shape
    return pl.pallas_call(
        functools.partial(chunk_kernel, chunk, tuple(places), part, tuple(given)),
        out_shape=[resident((levels, columns, phases), F32), resident((CHUNK, columns, phases), F32)],
        in_specs=[VMEM] * len(given),
        out_specs=[VMEM] * 2,
        compiler_params=pltpu.CompilerParams(vmem_limit_bytes=16 * 2**20),
        name="chunk",
    )(*[pin(x) for x in given.values()])


def among(places):
    return functools.reduce(jnp.logical_or, [lax.axis_index("lvl") == place for place in places])


def is_open(levels, a, i):
    return i + a < levels


def slot_of(levels, a, i):
    if not is_open(levels, a, i):
        return sum(range(1, a)) + i - (levels - a)
    return sum(levels - n if n < CHUNK else AHEAD - n for n in range(a)) + i


def get_answer(ways, levels, a, i, rows=slice(None)):
    high, low = ways[0:2] if is_open(levels, a, i) else ways[2:4]
    at = slot_of(levels, a, i)
    return high[at, rows], low[at, rows]


def spread_open_kernel(places, weight, base, high, low, kept):
    levels, columns, phases = base.shape
    rows = phases + columns

    def step(at, i, terms, keep=None):
        new = sum(dot_parts((high[x], low[x]), operator(weight, i, k)) for x, k in terms)
        unit, run = new[0:phases], new[phases:rows] + base[i]
        high[at, 0:phases], low[at, 0:phases] = split(unit)
        high[at, phases:rows], low[at, phases:rows] = split(run)
        if keep is not None:
            kept[keep, 0:phases], kept[keep, phases:rows] = unit, run

    @pl.when(among(places))
    def _():
        high[0, 0:phases], low[0, 0:phases] = operator(weight, 0, 0)
        high[0, phases:rows], low[0, phases:rows] = split(base[0])

        def up(i, _):
            step(i, i, [(i - 1, 0)])
            return 0

        lax.fori_loop(1, levels, up, 0)
        for a in range(1, AHEAD):
            first, old = slot_of(levels, a, 0), slot_of(levels, a - 1, 0)
            step(first, 0, [(old + 1, 1)], a - SOON if a >= SOON else None)

            def both(i, _, first=first, old=old):
                step(first + i, i, [(first + i - 1, 0), (old + i + 1, 1)])
                return 0

            lax.fori_loop(1, levels - a if a < CHUNK else AHEAD - a, both, 0)


def spread_close_kernel(
    places, weight, base, soon, open_high, open_low, before, high, low, state, leaving, feed_high, feed_low
):
    levels, columns, phases = base.shape
    rows = phases + columns
    top = levels - 1
    ways = (open_high, open_low, high, low)

    @pl.when(jnp.logical_not(among(places)))
    def _():
        state[...] = before[...]

    @pl.when(among(places))
    def _():
        for j in range(CHUNK - 1):
            feed_high[j], feed_low[j] = split(soon[j, 0:phases])
        for a in range(1, CHUNK):
            for i in range(levels - a, levels):
                new = dot_parts(get_answer(ways, levels, a, i - 1), operator(weight, i, 0))
                if i < top:
                    over = get_answer(ways, levels, a - 1, i + 1)
                else:
                    back = sum(
                        dot_parts(get_answer(ways, levels, a - 1 - j, top), (feed_high[j], feed_low[j])) for j in range(a)
                    )
                    end = back[phases:rows] + soon[a - 1, phases:rows]
                    over = split(jnp.concatenate([back[0:phases], end], axis=0))
                new += dot_parts(over, operator(weight, i, 1))
                at = slot_of(levels, a, i)
                high[at, 0:phases], low[at, 0:phases] = split(new[0:phases])
                high[at, phases:rows], low[at, phases:rows] = split(new[phases:rows] + base[i])

        def run(a, i):
            return sum(part.astype(F32) for part in get_answer(ways, levels, a, i, slice(phases, rows)))

        for i in range(levels):
            state[i] = run(CHUNK - 1, i)
        for a in range(CHUNK):
            leaving[a] = run(a, top)


def spread_open(places, weight, base):
    levels, columns, phases = base.shape
    assert levels > AHEAD and levels >= 2 * CHUNK - 1
    rows = phases + columns
    slots = slot_of(levels, AHEAD, 0)
    *ways, kept = pl.pallas_call(
        functools.partial(spread_open_kernel, tuple(places)),
        out_shape=[resident((slots, rows, phases), BF16)] * 2 + [resident((AHEAD - SOON, rows, phases), F32)],
        in_specs=[VMEM] * 2,
        out_specs=[VMEM] * 3,
        compiler_params=pltpu.CompilerParams(vmem_limit_bytes=16 * 2**20),
        name="spread_open",
    )(*[pin(x) for x in (weight, base)])
    return ways, kept


def spread_close(places, weight, base, soon, ways, state):
    levels, columns, phases = base.shape
    rows = phases + columns
    *more, state, leaving = pl.pallas_call(
        functools.partial(spread_close_kernel, tuple(places)),
        out_shape=[resident((sum(range(CHUNK)), rows, phases), BF16)] * 2
        + [resident((levels, columns, phases), F32), resident((CHUNK, columns, phases), F32)],
        in_specs=[VMEM] * 6,
        out_specs=[VMEM] * 4,
        scratch_shapes=[pltpu.VMEM((CHUNK - 1, phases, phases), BF16)] * 2,
        compiler_params=pltpu.CompilerParams(vmem_limit_bytes=16 * 2**20),
        name="spread_close",
    )(*[pin(x) for x in (weight, base, soon, *ways, state)])
    return [*ways, *more], state, leaving


def finish_leaving_kernel(place, *refs, levels):
    *ways, entering, leaving, before, new = refs
    columns, phases = entering.shape[1:]

    @pl.when(lax.axis_index("lvl") != place)
    def _():
        new[...] = before[...]

    @pl.when(lax.axis_index("lvl") == place)
    def _():
        values = [stack(entering[k]) for k in range(CHUNK)]
        total = [leaving[k] for k in range(CHUNK)]
        for a in range(CHUNK):
            pair = jnp.concatenate(get_answer(ways, levels, a, levels - 1, slice(0, phases)), axis=0)
            for k, term in enumerate(apply_each(values[: CHUNK - a], pair, columns)):
                total[a + k] += term
        for k in range(CHUNK):
            new[k] = total[k]


def finish_leaving(place, ways, entering, leaving, before, levels):
    return pl.pallas_call(
        functools.partial(finish_leaving_kernel, place, levels=levels),
        out_shape=resident(leaving.shape, F32),
        in_specs=[VMEM] * 7,
        out_specs=VMEM,
        compiler_params=pltpu.CompilerParams(vmem_limit_bytes=8 * 2**20),
        name="finish_leaving",
    )(*[pin(x) for x in (*ways, entering, leaving, before)])


def finish_state_kernel(place, *refs):
    *ways, entering, state, new = refs
    levels, _, phases = state.shape

    @pl.when(lax.axis_index("lvl") != place)
    def _():
        new[...] = state[...]

    @pl.when(lax.axis_index("lvl") == place)
    def _():
        values = [stack(entering[CHUNK - 1 - a]) for a in range(CHUNK)]
        for i in range(levels):
            terms = []
            for a in range(CHUNK):
                pair = jnp.concatenate(get_answer(ways, levels, a, i, slice(0, phases)), axis=0)
                terms.append((values[a], pair))
            new[i] = state[i] + apply(terms)


def finish_state(place, ways, entering, state, last):
    return pl.pallas_call(
        functools.partial(finish_state_kernel, place),
        out_shape=(jax.ShapeDtypeStruct if last else resident)(state.shape, F32),
        in_specs=[VMEM] * 6,
        out_specs=VMEM,
        compiler_params=pltpu.CompilerParams(vmem_limit_bytes=8 * 2**20),
        name="finish_state",
    )(*[pin(x) for x in (*ways, entering, state)])


def answer_kernel(step, soon, late, entering, returned):
    @pl.when(lax.axis_index("lvl") == step)
    def _():
        past = {n + 1: stack(entering[n]) for n in range(CHUNK)}
        above = carried(soon, late, past, CHUNK, 2 * CHUNK - 1)
        for k in range(CHUNK):
            returned[k] = above[CHUNK + k]


def answer(step, soon, late, entering):
    return pl.pallas_call(
        functools.partial(answer_kernel, step),
        out_shape=resident(entering.shape, F32),
        in_specs=[VMEM] * 3,
        out_specs=VMEM,
        compiler_params=pltpu.CompilerParams(vmem_limit_bytes=8 * 2**20),
        name="answer",
    )(*[pin(x) for x in (soon, late, entering)])


def local(inverse_diag, down_block, up_block, reward):
    given = reward.shape[1]
    columns = -(-given // 16) * 16
    if columns != given:
        reward = jnp.pad(reward, ((0, 0), (0, columns - given), (0, 0)))
    count = lax.axis_size("lvl")
    assert CHUNKS == 2 and count > 1
    top = count - 1
    ready = [d for d in range(1, count) if d % 2 == 0 or d == top]
    odd = [d for d in range(1, top, 2)]
    weights, begun, soon_here = prepare(inverse_diag, down_block, up_block, reward)
    weight, base = weights
    late_odd = respond(odd, weights, begun) if odd else None
    ways, late_here = spread_open(ready, weight, base)
    soon_odd = lax.ppermute(soon_here, "lvl", [(d + 1, d) for d in range(1, top, 2)])
    soon = lax.ppermute(soon_here, "lvl", [(d + 1, d) for d in range(0, top, 2)])
    late = lax.ppermute(late_odd, "lvl", [(d, d - 1) for d in odd]) if odd else None
    soon, late_here, late_odd = lax.optimization_barrier((soon, late_here, late_odd))
    late_top = None
    own = {"weight": weight, "base": base, "soon": soon}
    state = leaving = entering = parted = None
    for step in range(count + 1):
        place = step - 1
        earlier = leaving
        returned = edge = None
        if step % 2 == 0 and 0 < step < count:
            returned = lax.ppermute(answer(step, soon_here, late_here, entering), "lvl", [(step, place)])
            given_early = {"weight": weight, "base": base, "entering": entering, "state": state}
            state, edge = run_chunk(1, [place], given_early, "early")
        if place in ready and place < top:
            leaving = finish_leaving(place, ways, entering, parted, leaving, base.shape[0])
        if step in ready:
            if step < top:
                leaving = finish_leaving(step, ways, entering, parted_first, leaving, base.shape[0])
        elif step < count:
            state, leaving = run_chunk(
                0, [step], {**own, "soon": soon_odd if step % 2 else soon, "entering": entering, "state": state, "leaving": leaving}
            )
        if step == 1:
            top_sent, leaving = lax.optimization_barrier((late_here, leaving))
            late_top = lax.ppermute(top_sent, "lvl", [(top, top - 1)]) if top % 2 else None
            first_late = late if odd else late_top
            given_first = {**own, "late": first_late, "earlier": earlier, "state": state, "leaving": leaving}
            state, leaving = run_chunk(1, [0], given_first)
        if returned is not None:
            given_rest = {**own, "soon": soon_odd, "returned": returned, "edge": edge, "state": state, "leaving": leaving}
            state, leaving = run_chunk(1, [place], given_rest, "late")
        came = entering
        if step < count:
            pairs = [(d, d + 1) for d in (place, step) if 0 <= d < top]
            entering = lax.ppermute(leaving, "lvl", pairs) if pairs else None
        if step == 1:
            ways_then, leaving = lax.optimization_barrier((ways, leaving))
            ways, state, parted_first = spread_close(ready, weight, base, soon, ways_then, state)
            if entering is not None:
                entering, state = lax.optimization_barrier((entering, state))
        if place in ready:
            state = finish_state(place, ways, came, state, step == count)
        if step in ready:
            state = finish_state(step, ways, came, state, False)
            extra = {} if step == top else {"late": late_top if step == top - 1 else late, "earlier": leaving}
            state, parted = run_chunk(1, [step], {**own, **extra, "state": state})
    return state[:, :given] if columns != given else state


def solution(mesh):
    placed = (
        P(("grp", "lvl"), None, None),
        P(("grp", "lvl"), None, None),
        P(("grp", "lvl"), None, None),
        P(("grp", "lvl"), "col", None),
    )
    return jax.shard_map(
        local, mesh=mesh, in_specs=placed, out_specs=P(("grp", "lvl"), "col", None), check_vma=False
    )
```

```python
import functools

import jax
import jax.numpy as jnp
from jax import lax
from jax.experimental import pallas as pl
from jax.experimental.pallas import tpu as pltpu
from jax.sharding import PartitionSpec as P

SWEEPS = 8
CHUNK = 4
CHUNKS = SWEEPS // CHUNK
AHEAD = SWEEPS - 1
SOON = CHUNK - 1
F32 = jnp.float32
BF16 = jnp.bfloat16


def resident(shape, dtype):
    return pltpu.VMEM(shape, dtype)


def pin(x, memory=pltpu.VMEM):
    return pltpu.with_memory_space_constraint(x, memory)


def split(x):
    high = x.astype(BF16)
    return high, (x - high.astype(F32)).astype(BF16)


def dot(a, b):
    return jnp.dot(a, b, preferred_element_type=F32)


def dot_nt(a, b):
    return lax.dot_general(a, b, (((1,), (1,)), ((), ())), preferred_element_type=F32)


def dot_parts(a, b, dot=dot):
    return dot(a[0], b[0]) + (dot(a[0], b[1]) + dot(a[1], b[0]))


def place_operator(weight, i, k, value):
    phases = value.shape[0]
    for n, part in enumerate(split(value.T)):
        weight[i, (2 * k + n) * phases : (2 * k + n + 1) * phases] = part


def operator(weight, i, k):
    phases = weight.shape[2]
    at = 2 * k * phases
    return weight[i, at : at + phases], weight[i, at + phases : at + 2 * phases]


def response(first, last, x_high, x_low, weight, base, kept):
    _, columns, phases = base.shape
    rows = phases + columns

    def store(i, new):
        top = new[0:phases]
        end = new[phases:rows] + base[i]
        x_high[i, 0:phases], x_low[i, 0:phases] = split(top)
        x_high[i, phases:rows], x_low[i, phases:rows] = split(end)
        return top, end

    def from_below(i):
        return dot_parts((x_high[i - 1], x_low[i - 1]), operator(weight, i, 0))

    def from_above(i):
        return dot_parts((x_high[i + 1], x_low[i + 1]), operator(weight, i, 1))

    for d in range(first, last):
        if d == 0:
            high, low = weight[0, 0:phases], weight[0, phases : 2 * phases]
            x_high[0, 0:phases], x_low[0, 0:phases] = high, low
            x_high[0, phases:rows], x_low[0, phases:rows] = split(base[0])
            kept[0, 0:phases] = high.astype(F32) + low.astype(F32)
            kept[0, phases:rows] = base[0]
            continue
        store(d, from_below(d))

        def level(k, _, d=d):
            i = d - k
            store(i, from_below(i) + from_above(i))
            return 0

        lax.fori_loop(1, d, level, 0)
        kept[d - first, 0:phases], kept[d - first, phases:rows] = store(0, from_above(0))


def products(wanted, here_from, weight, base, inv, down, up, pay):
    for i in wanted:
        here_from(i)
        here = split(inv[i])
        for k, block in ((0, down), (1, up)):
            if k in wanted[i]:
                place_operator(weight, i, k, dot_parts(here, split(block[i])))
        if 2 in wanted[i]:
            base[i] = dot_parts(split(pay[i]), here, dot_nt)


def prepare_kernel(inv_far, down_far, up_far, pay_far, weight, base, x_high, x_low, kept, inv, down, up, pay, sems):
    levels = pay.shape[0]
    cuts = ((0, 1), (1, SOON), (SOON, levels))

    def copies(part):
        at, end = cuts[part]
        pairs = [(inv_far, inv), (down_far, down), (up_far, up)]
        found = [
            pltpu.make_async_copy(far.at[at:end], near.at[at:end], sems.at[n, part])
            for n, (far, near) in enumerate(pairs)
        ]
        return found + ([pltpu.make_async_copy(pay_far, pay, sems.at[3, 0])] if part == 0 else [])

    def wait(i):
        for part, (at, _) in enumerate(cuts):
            if i == at:
                for copy in copies(part):
                    copy.wait()

    for part in range(len(cuts)):
        for copy in copies(part):
            copy.start()
    wanted = {i: (0, 1, 2) if i < SOON - 1 else (0, 2) for i in range(SOON)}
    products(wanted, wait, weight, base, inv, down, up, pay)
    response(0, SOON, x_high, x_low, weight, base, kept)
    wait(SOON)


def prepare_rest_kernel(weight_soon, base_soon, inv, down, up, pay, weight, base):
    levels, _, phases = pay.shape
    for i in range(SOON):
        rows = (4 if i < SOON - 1 else 2) * phases
        weight[i, 0:rows] = weight_soon[i, 0:rows]
    base[0:SOON] = base_soon[...]
    wanted = {i: (0, 1, 2) if i >= SOON else (1,) for i in range(SOON - 1, levels)}
    products(wanted, lambda i: None, weight, base, inv, down, up, pay)


def respond_kernel(places, weight, base, x_high_soon, x_low_soon, kept, x_high, x_low):
    @pl.when(among(places))
    def _():
        x_high[0:SOON] = x_high_soon[...]
        x_low[0:SOON] = x_low_soon[...]
        response(SOON, AHEAD, x_high, x_low, weight, base, kept)


VMEM = pl.BlockSpec(memory_space=pltpu.VMEM)
HBM = pl.BlockSpec(memory_space=pltpu.HBM)


def operators(levels, columns, phases):
    return [resident((levels, 4 * phases, phases), BF16), resident((levels, columns, phases), F32)]


def prepare(inverse_diag, down_block, up_block, reward):
    levels, columns, phases = reward.shape
    rows = phases + columns
    matrix = resident((levels, phases, phases), F32)
    *soon, x_high, x_low, kept_soon, inv, down, up, pay = pl.pallas_call(
        prepare_kernel,
        out_shape=operators(SOON, columns, phases)
        + [resident((SOON, rows, phases), BF16)] * 2
        + [resident((SOON, rows, phases), F32)]
        + [matrix] * 3
        + [resident((levels, columns, phases), F32)],
        in_specs=[HBM] * 4,
        out_specs=[VMEM] * 9,
        scratch_shapes=[pltpu.SemaphoreType.DMA((4, 3))],
        compiler_params=pltpu.CompilerParams(vmem_limit_bytes=16 * 2**20),
        name="prepare",
    )(*[pin(x, pltpu.HBM) for x in (inverse_diag, down_block, up_block, reward)])
    weights = pl.pallas_call(
        prepare_rest_kernel,
        out_shape=operators(levels, columns, phases),
        in_specs=[VMEM] * 6,
        out_specs=[VMEM] * 2,
        compiler_params=pltpu.CompilerParams(vmem_limit_bytes=16 * 2**20),
        name="prepare_rest",
    )(*[pin(x) for x in (*soon, inv, down, up, pay)])
    return weights, (x_high, x_low), kept_soon


def respond(places, weights, started):
    _, rows, phases = started[0].shape
    return pl.pallas_call(
        functools.partial(respond_kernel, tuple(places)),
        out_shape=resident((AHEAD - SOON, rows, phases), F32),
        in_specs=[VMEM] * 4,
        out_specs=VMEM,
        scratch_shapes=[pltpu.VMEM((AHEAD, rows, phases), BF16)] * 2,
        compiler_params=pltpu.CompilerParams(vmem_limit_bytes=16 * 2**20),
        name="respond",
    )(*[pin(x) for x in (*weights, *started)])


def stack(x):
    high = x.astype(BF16).astype(F32)
    return jnp.concatenate([high, x - high], axis=0).astype(BF16)


def fold(total):
    half = total.shape[0] // 2
    return total[:half] + total[half:]


def apply(terms):
    values = jnp.concatenate([x for x, _ in terms for _ in range(2)], axis=1)
    return fold(dot(values, jnp.concatenate([operator for _, operator in terms], axis=0)))


def apply_each(values, operator, columns):
    phases = operator.shape[1]
    values = jnp.concatenate(values, axis=0) if len(values) > 1 else values[0]
    total = dot(values, operator[0:phases]) + dot(values, operator[phases:])
    return [fold(total[at : at + 2 * columns]) for at in range(0, total.shape[0], 2 * columns)]


def whole(operator):
    return jnp.concatenate(split(operator), axis=0)


def kept_at(soon, late, j):
    return soon[j] if j < SOON else late[j - SOON]


def carried(soon, late, past, first, last):
    phases = soon.shape[2]
    above = {n: kept_at(soon, late, n - 1)[phases:] for n in range(max(first, 1), last + 1)}
    columns = soon.shape[1] - phases
    for j in range(last) if past else ():
        pairs = [(n, n - j) for n in above if n - j in past]
        if pairs:
            terms = [past[m] for _, m in pairs]
            for (n, _), term in zip(pairs, apply_each(terms, whole(kept_at(soon, late, j)[0:phases]), columns)):
                above[n] += term
    return above


def wave(first, weight, base, now, above, feedback, due, emit):
    levels, _, phases = base.shape
    for turn in range(levels + 2 * (CHUNK - 1)):
        for k in range(CHUNK):
            i = turn - 2 * k
            if not (0 <= i < levels and due(i, k)):
                continue
            n = first + 1 + k
            terms = []
            if (i - 1, n) in now:
                terms.append((now[i - 1, n], weight[i, 0 : 2 * phases]))
            if n > 1:
                over = stack(above[n - 1]) if i == levels - 1 else now[i + 1, n - 1]
                terms.append((over, weight[i, 2 * phases : 4 * phases]))
            value = base[i] + apply(terms) if terms else base[i]
            now[i, n] = stack(value)
            emit(i, k, value)
            if i == levels - 1:
                for later in range(n, first + CHUNK):
                    above[later] += apply([(now[i, n], feedback[later - n])])


def edge_level(levels, k):
    return levels - 2 - k


def chunk_kernel(chunk, places, part, names, *refs):
    given = dict(zip(names, refs))
    new_state, leaving = refs[len(names) :]
    weight, base = given["weight"], given["base"]
    levels, columns, phases = base.shape
    first = chunk * CHUNK

    @pl.when(jnp.logical_not(among(places)))
    def _():
        for name, target in (("state", new_state), ("leaving", leaving)):
            target[...] = given[name][...] if name in given else jnp.zeros_like(target)

    @pl.when(among(places))
    def _():
        zero = jnp.zeros((columns, phases), F32)
        above, feedback = {first + k: zero for k in range(CHUNK)}, []
        if part != "early":
            soon = given["soon"]
            feedback = [whole(soon[j, 0:phases]) for j in range(SOON)]
            if not first:
                above = carried(soon, None, {}, first, first + CHUNK - 1)
            elif "late" in given:
                past = {n + 1: stack(given["earlier"][n]) for n in range(first)}
                above = carried(soon, given["late"], past, first, first + CHUNK - 1)
            elif "returned" in given:
                above = {first + k: given["returned"][k] for k in range(CHUNK)}

        now = {}
        if part == "late":
            for k in range(CHUNK):
                now[edge_level(levels, k), first + 1 + k] = stack(given["edge"][k])
            new_state[...] = given["state"][...]
        elif first:
            for i in range(levels):
                now[i, first] = stack(given["state"][i])
        if part != "late" and "entering" in given:
            for k in range(CHUNK):
                now[-1, first + 1 + k] = stack(given["entering"][k])

        def due(i, k):
            return part == "all" or (i <= edge_level(levels, k)) == (part == "early")

        def emit(i, k, value):
            if k == CHUNK - 1:
                new_state[i] = value
            if i == (edge_level(levels, k) if part == "early" else levels - 1):
                leaving[k] = value

        wave(first, weight, base, now, above, feedback, due, emit)


def run_chunk(chunk, places, given, part="all"):
    given = {name: x for name, x in given.items() if x is not None}
    levels, columns, phases = given["base"].shape
    return pl.pallas_call(
        functools.partial(chunk_kernel, chunk, tuple(places), part, tuple(given)),
        out_shape=[resident((levels, columns, phases), F32), resident((CHUNK, columns, phases), F32)],
        in_specs=[VMEM] * len(given),
        out_specs=[VMEM] * 2,
        compiler_params=pltpu.CompilerParams(vmem_limit_bytes=16 * 2**20),
        name="chunk",
    )(*[pin(x) for x in given.values()])


def among(places):
    return functools.reduce(jnp.logical_or, [lax.axis_index("lvl") == place for place in places])


def is_open(levels, a, i):
    return i + a < levels


def slot_of(levels, a, i):
    if not is_open(levels, a, i):
        return sum(range(1, a)) + i - (levels - a)
    return sum(levels - n if n < CHUNK else AHEAD - n for n in range(a)) + i


def get_answer(ways, levels, a, i, rows=slice(None)):
    high, low = ways[0:2] if is_open(levels, a, i) else ways[2:4]
    at = slot_of(levels, a, i)
    return high[at, rows], low[at, rows]


def spread_open_kernel(places, weight, base, high, low, kept):
    levels, columns, phases = base.shape
    rows = phases + columns

    def step(at, i, terms, keep=None):
        new = sum(dot_parts((high[x], low[x]), operator(weight, i, k)) for x, k in terms)
        unit, run = new[0:phases], new[phases:rows] + base[i]
        high[at, 0:phases], low[at, 0:phases] = split(unit)
        high[at, phases:rows], low[at, phases:rows] = split(run)
        if keep is not None:
            kept[keep, 0:phases], kept[keep, phases:rows] = unit, run

    @pl.when(among(places))
    def _():
        high[0, 0:phases], low[0, 0:phases] = operator(weight, 0, 0)
        high[0, phases:rows], low[0, phases:rows] = split(base[0])

        def up(i, _):
            step(i, i, [(i - 1, 0)])
            return 0

        lax.fori_loop(1, levels, up, 0)
        for a in range(1, AHEAD):
            first, old = slot_of(levels, a, 0), slot_of(levels, a - 1, 0)
            step(first, 0, [(old + 1, 1)], a - SOON if a >= SOON else None)

            def both(i, _, first=first, old=old):
                step(first + i, i, [(first + i - 1, 0), (old + i + 1, 1)])
                return 0

            lax.fori_loop(1, levels - a if a < CHUNK else AHEAD - a, both, 0)


def spread_close_kernel(
    places, weight, base, soon, open_high, open_low, before, high, low, state, leaving, feed_high, feed_low
):
    levels, columns, phases = base.shape
    rows = phases + columns
    top = levels - 1
    ways = (open_high, open_low, high, low)

    @pl.when(jnp.logical_not(among(places)))
    def _():
        state[...] = before[...]

    @pl.when(among(places))
    def _():
        for j in range(CHUNK - 1):
            feed_high[j], feed_low[j] = split(soon[j, 0:phases])
        for a in range(1, CHUNK):
            for i in range(levels - a, levels):
                new = dot_parts(get_answer(ways, levels, a, i - 1), operator(weight, i, 0))
                if i < top:
                    over = get_answer(ways, levels, a - 1, i + 1)
                else:
                    back = sum(
                        dot_parts(get_answer(ways, levels, a - 1 - j, top), (feed_high[j], feed_low[j])) for j in range(a)
                    )
                    end = back[phases:rows] + soon[a - 1, phases:rows]
                    over = split(jnp.concatenate([back[0:phases], end], axis=0))
                new += dot_parts(over, operator(weight, i, 1))
                at = slot_of(levels, a, i)
                high[at, 0:phases], low[at, 0:phases] = split(new[0:phases])
                high[at, phases:rows], low[at, phases:rows] = split(new[phases:rows] + base[i])

        def run(a, i):
            return sum(part.astype(F32) for part in get_answer(ways, levels, a, i, slice(phases, rows)))

        for i in range(levels):
            state[i] = run(CHUNK - 1, i)
        for a in range(CHUNK):
            leaving[a] = run(a, top)


def spread_open(places, weight, base):
    levels, columns, phases = base.shape
    assert levels > AHEAD and levels >= 2 * CHUNK - 1
    rows = phases + columns
    slots = slot_of(levels, AHEAD, 0)
    *ways, kept = pl.pallas_call(
        functools.partial(spread_open_kernel, tuple(places)),
        out_shape=[resident((slots, rows, phases), BF16)] * 2 + [resident((AHEAD - SOON, rows, phases), F32)],
        in_specs=[VMEM] * 2,
        out_specs=[VMEM] * 3,
        compiler_params=pltpu.CompilerParams(vmem_limit_bytes=16 * 2**20),
        name="spread_open",
    )(*[pin(x) for x in (weight, base)])
    return ways, kept


def spread_close(places, weight, base, soon, ways, state):
    levels, columns, phases = base.shape
    rows = phases + columns
    *more, state, leaving = pl.pallas_call(
        functools.partial(spread_close_kernel, tuple(places)),
        out_shape=[resident((sum(range(CHUNK)), rows, phases), BF16)] * 2
        + [resident((levels, columns, phases), F32), resident((CHUNK, columns, phases), F32)],
        in_specs=[VMEM] * 6,
        out_specs=[VMEM] * 4,
        scratch_shapes=[pltpu.VMEM((CHUNK - 1, phases, phases), BF16)] * 2,
        compiler_params=pltpu.CompilerParams(vmem_limit_bytes=16 * 2**20),
        name="spread_close",
    )(*[pin(x) for x in (weight, base, soon, *ways, state)])
    return [*ways, *more], state, leaving


def finish_leaving_kernel(place, *refs, levels):
    *ways, entering, leaving, before, new = refs
    columns, phases = entering.shape[1:]

    @pl.when(lax.axis_index("lvl") != place)
    def _():
        new[...] = before[...]

    @pl.when(lax.axis_index("lvl") == place)
    def _():
        values = [stack(entering[k]) for k in range(CHUNK)]
        total = [leaving[k] for k in range(CHUNK)]
        for a in range(CHUNK):
            pair = jnp.concatenate(get_answer(ways, levels, a, levels - 1, slice(0, phases)), axis=0)
            for k, term in enumerate(apply_each(values[: CHUNK - a], pair, columns)):
                total[a + k] += term
        for k in range(CHUNK):
            new[k] = total[k]


def finish_leaving(place, ways, entering, leaving, before, levels):
    return pl.pallas_call(
        functools.partial(finish_leaving_kernel, place, levels=levels),
        out_shape=resident(leaving.shape, F32),
        in_specs=[VMEM] * 7,
        out_specs=VMEM,
        compiler_params=pltpu.CompilerParams(vmem_limit_bytes=8 * 2**20),
        name="finish_leaving",
    )(*[pin(x) for x in (*ways, entering, leaving, before)])


def finish_state_kernel(place, *refs):
    *ways, entering, state, new = refs
    levels, _, phases = state.shape

    @pl.when(lax.axis_index("lvl") != place)
    def _():
        new[...] = state[...]

    @pl.when(lax.axis_index("lvl") == place)
    def _():
        values = [stack(entering[CHUNK - 1 - a]) for a in range(CHUNK)]
        for i in range(levels):
            terms = []
            for a in range(CHUNK):
                pair = jnp.concatenate(get_answer(ways, levels, a, i, slice(0, phases)), axis=0)
                terms.append((values[a], pair))
            new[i] = state[i] + apply(terms)


def finish_state(place, ways, entering, state, last):
    return pl.pallas_call(
        functools.partial(finish_state_kernel, place),
        out_shape=(jax.ShapeDtypeStruct if last else resident)(state.shape, F32),
        in_specs=[VMEM] * 6,
        out_specs=VMEM,
        compiler_params=pltpu.CompilerParams(vmem_limit_bytes=8 * 2**20),
        name="finish_state",
    )(*[pin(x) for x in (*ways, entering, state)])


def answer_kernel(step, soon, late, entering, returned):
    @pl.when(lax.axis_index("lvl") == step)
    def _():
        past = {n + 1: stack(entering[n]) for n in range(CHUNK)}
        above = carried(soon, late, past, CHUNK, 2 * CHUNK - 1)
        for k in range(CHUNK):
            returned[k] = above[CHUNK + k]


def answer(step, soon, late, entering):
    return pl.pallas_call(
        functools.partial(answer_kernel, step),
        out_shape=resident(entering.shape, F32),
        in_specs=[VMEM] * 3,
        out_specs=VMEM,
        compiler_params=pltpu.CompilerParams(vmem_limit_bytes=8 * 2**20),
        name="answer",
    )(*[pin(x) for x in (soon, late, entering)])


def local(inverse_diag, down_block, up_block, reward):
    given = reward.shape[1]
    columns = -(-given // 16) * 16
    if columns != given:
        reward = jnp.pad(reward, ((0, 0), (0, columns - given), (0, 0)))
    count = lax.axis_size("lvl")
    assert CHUNKS == 2 and count > 1
    top = count - 1
    ready = [d for d in range(1, count) if d % 2 == 0 or d == top]
    odd = [d for d in range(1, top, 2)]
    weights, begun, soon_here = prepare(inverse_diag, down_block, up_block, reward)
    weight, base = weights
    late_odd = respond(odd, weights, begun) if odd else None
    ways, late_here = spread_open(ready, weight, base)
    soon_odd = lax.ppermute(soon_here, "lvl", [(d + 1, d) for d in range(1, top, 2)])
    soon = lax.ppermute(soon_here, "lvl", [(d + 1, d) for d in range(0, top, 2)])
    late = lax.ppermute(late_odd, "lvl", [(d, d - 1) for d in odd]) if odd else None
    soon, late_here, late_odd = lax.optimization_barrier((soon, late_here, late_odd))
    late_top = None
    own = {"weight": weight, "base": base, "soon": soon}
    state = leaving = entering = parted = None
    for step in range(count + 1):
        place = step - 1
        earlier = leaving
        returned = edge = None
        if step % 2 == 0 and 0 < step < count:
            returned = lax.ppermute(answer(step, soon_here, late_here, entering), "lvl", [(step, place)])
            given_early = {"weight": weight, "base": base, "entering": entering, "state": state}
            state, edge = run_chunk(1, [place], given_early, "early")
        if place in ready and place < top:
            leaving = finish_leaving(place, ways, entering, parted, leaving, base.shape[0])
        if step in ready:
            if step < top:
                leaving = finish_leaving(step, ways, entering, parted_first, leaving, base.shape[0])
        elif step < count:
            state, leaving = run_chunk(
                0, [step], {**own, "soon": soon_odd if step % 2 else soon, "entering": entering, "state": state, "leaving": leaving}
            )
        if step == 1:
            top_sent, leaving = lax.optimization_barrier((late_here, leaving))
            late_top = lax.ppermute(top_sent, "lvl", [(top, top - 1)]) if top % 2 else None
            first_late = late if odd else late_top
            given_first = {**own, "late": first_late, "earlier": earlier, "state": state, "leaving": leaving}
            state, leaving = run_chunk(1, [0], given_first)
        if returned is not None:
            given_rest = {**own, "soon": soon_odd, "returned": returned, "edge": edge, "state": state, "leaving": leaving}
            state, leaving = run_chunk(1, [place], given_rest, "late")
        came = entering
        if step < count:
            pairs = [(d, d + 1) for d in (place, step) if 0 <= d < top]
            entering = lax.ppermute(leaving, "lvl", pairs) if pairs else None
        if step == 1:
            ways_then, leaving = lax.optimization_barrier((ways, leaving))
            ways, state, parted_first = spread_close(ready, weight, base, soon, ways_then, state)
            if entering is not None:
                entering, state = lax.optimization_barrier((entering, state))
        if place in ready:
            state = finish_state(place, ways, came, state, step == count)
        if step in ready:
            state = finish_state(step, ways, came, state, False)
            extra = {} if step == top else {"late": late_top if step == top - 1 else late, "earlier": leaving}
            state, parted = run_chunk(1, [step], {**own, **extra, "state": state})
    return state[:, :given] if columns != given else state


def solution(mesh):
    placed = (
        P(("grp", "lvl"), None, None),
        P(("grp", "lvl"), None, None),
        P(("grp", "lvl"), None, None),
        P(("grp", "lvl"), "col", None),
    )
    return jax.shard_map(
        local, mesh=mesh, in_specs=placed, out_specs=P(("grp", "lvl"), "col", None), check_vma=False
    )
```

```python
import functools

import jax
import jax.numpy as jnp
from jax import lax
from jax.experimental import pallas as pl
from jax.experimental.pallas import tpu as pltpu
from jax.sharding import PartitionSpec as P

SWEEPS = 8
CHUNK = 4
CHUNKS = SWEEPS // CHUNK
AHEAD = SWEEPS - 1
SOON = CHUNK - 1
F32 = jnp.float32
BF16 = jnp.bfloat16


def resident(shape, dtype):
    return pltpu.VMEM(shape, dtype)


def pin(x, memory=pltpu.VMEM):
    return pltpu.with_memory_space_constraint(x, memory)


def split(x):
    high = x.astype(BF16)
    return high, (x - high.astype(F32)).astype(BF16)


def dot(a, b):
    return jnp.dot(a, b, preferred_element_type=F32)


def dot_nt(a, b):
    return lax.dot_general(a, b, (((1,), (1,)), ((), ())), preferred_element_type=F32)


def dot_parts(a, b, dot=dot):
    return dot(a[0], b[0]) + (dot(a[0], b[1]) + dot(a[1], b[0]))


def place_operator(weight, i, k, value):
    phases = value.shape[0]
    for n, part in enumerate(split(value.T)):
        weight[i, (2 * k + n) * phases : (2 * k + n + 1) * phases] = part


def operator(weight, i, k):
    phases = weight.shape[2]
    at = 2 * k * phases
    return weight[i, at : at + phases], weight[i, at + phases : at + 2 * phases]


def response(first, last, x_high, x_low, weight, base, kept):
    _, columns, phases = base.shape
    rows = phases + columns

    def store(i, new):
        top = new[0:phases]
        end = new[phases:rows] + base[i]
        x_high[i, 0:phases], x_low[i, 0:phases] = split(top)
        x_high[i, phases:rows], x_low[i, phases:rows] = split(end)
        return top, end

    def from_below(i):
        return dot_parts((x_high[i - 1], x_low[i - 1]), operator(weight, i, 0))

    def from_above(i):
        return dot_parts((x_high[i + 1], x_low[i + 1]), operator(weight, i, 1))

    for d in range(first, last):
        if d == 0:
            high, low = weight[0, 0:phases], weight[0, phases : 2 * phases]
            x_high[0, 0:phases], x_low[0, 0:phases] = high, low
            x_high[0, phases:rows], x_low[0, phases:rows] = split(base[0])
            kept[0, 0:phases] = high.astype(F32) + low.astype(F32)
            kept[0, phases:rows] = base[0]
            continue
        store(d, from_below(d))

        def level(k, _, d=d):
            i = d - k
            store(i, from_below(i) + from_above(i))
            return 0

        lax.fori_loop(1, d, level, 0)
        kept[d - first, 0:phases], kept[d - first, phases:rows] = store(0, from_above(0))


def products(wanted, here_from, weight, base, inv, down, up, pay):
    for i in wanted:
        here_from(i)
        here = split(inv[i])
        for k, block in ((0, down), (1, up)):
            if k in wanted[i]:
                place_operator(weight, i, k, dot_parts(here, split(block[i])))
        if 2 in wanted[i]:
            base[i] = dot_parts(split(pay[i]), here, dot_nt)


def prepare_kernel(inv_far, down_far, up_far, pay_far, weight, base, x_high, x_low, kept, inv, down, up, pay, sems):
    levels = pay.shape[0]
    cuts = ((0, 1), (1, SOON), (SOON, levels))

    def copies(part):
        at, end = cuts[part]
        pairs = [(inv_far, inv), (down_far, down), (up_far, up)]
        found = [
            pltpu.make_async_copy(far.at[at:end], near.at[at:end], sems.at[n, part])
            for n, (far, near) in enumerate(pairs)
        ]
        return found + ([pltpu.make_async_copy(pay_far, pay, sems.at[3, 0])] if part == 0 else [])

    def wait(i):
        for part, (at, _) in enumerate(cuts):
            if i == at:
                for copy in copies(part):
                    copy.wait()

    for part in range(len(cuts)):
        for copy in copies(part):
            copy.start()
    wanted = {i: (0, 1, 2) if i < SOON - 1 else (0, 2) for i in range(SOON)}
    products(wanted, wait, weight, base, inv, down, up, pay)
    response(0, SOON, x_high, x_low, weight, base, kept)
    wait(SOON)


def prepare_rest_kernel(weight_soon, base_soon, inv, down, up, pay, weight, base):
    levels, _, phases = pay.shape
    for i in range(SOON):
        rows = (4 if i < SOON - 1 else 2) * phases
        weight[i, 0:rows] = weight_soon[i, 0:rows]
    base[0:SOON] = base_soon[...]
    wanted = {i: (0, 1, 2) if i >= SOON else (1,) for i in range(SOON - 1, levels)}
    products(wanted, lambda i: None, weight, base, inv, down, up, pay)


def respond_kernel(places, weight, base, x_high_soon, x_low_soon, kept, x_high, x_low):
    @pl.when(among(places))
    def _():
        x_high[0:SOON] = x_high_soon[...]
        x_low[0:SOON] = x_low_soon[...]
        response(SOON, AHEAD, x_high, x_low, weight, base, kept)


VMEM = pl.BlockSpec(memory_space=pltpu.VMEM)
HBM = pl.BlockSpec(memory_space=pltpu.HBM)


def operators(levels, columns, phases):
    return [resident((levels, 4 * phases, phases), BF16), resident((levels, columns, phases), F32)]


def prepare(inverse_diag, down_block, up_block, reward):
    levels, columns, phases = reward.shape
    rows = phases + columns
    matrix = resident((levels, phases, phases), F32)
    *soon, x_high, x_low, kept_soon, inv, down, up, pay = pl.pallas_call(
        prepare_kernel,
        out_shape=operators(SOON, columns, phases)
        + [resident((SOON, rows, phases), BF16)] * 2
        + [resident((SOON, rows, phases), F32)]
        + [matrix] * 3
        + [resident((levels, columns, phases), F32)],
        in_specs=[HBM] * 4,
        out_specs=[VMEM] * 9,
        scratch_shapes=[pltpu.SemaphoreType.DMA((4, 3))],
        compiler_params=pltpu.CompilerParams(vmem_limit_bytes=16 * 2**20),
        name="prepare",
    )(*[pin(x, pltpu.HBM) for x in (inverse_diag, down_block, up_block, reward)])
    weights = pl.pallas_call(
        prepare_rest_kernel,
        out_shape=operators(levels, columns, phases),
        in_specs=[VMEM] * 6,
        out_specs=[VMEM] * 2,
        compiler_params=pltpu.CompilerParams(vmem_limit_bytes=16 * 2**20),
        name="prepare_rest",
    )(*[pin(x) for x in (*soon, inv, down, up, pay)])
    return weights, (x_high, x_low), kept_soon


def respond(places, weights, started):
    _, rows, phases = started[0].shape
    return pl.pallas_call(
        functools.partial(respond_kernel, tuple(places)),
        out_shape=resident((AHEAD - SOON, rows, phases), F32),
        in_specs=[VMEM] * 4,
        out_specs=VMEM,
        scratch_shapes=[pltpu.VMEM((AHEAD, rows, phases), BF16)] * 2,
        compiler_params=pltpu.CompilerParams(vmem_limit_bytes=16 * 2**20),
        name="respond",
    )(*[pin(x) for x in (*weights, *started)])


def stack(x):
    high = x.astype(BF16).astype(F32)
    return jnp.concatenate([high, x - high], axis=0).astype(BF16)


def fold(total):
    half = total.shape[0] // 2
    return total[:half] + total[half:]


def apply(terms):
    values = jnp.concatenate([x for x, _ in terms for _ in range(2)], axis=1)
    return fold(dot(values, jnp.concatenate([operator for _, operator in terms], axis=0)))


def apply_each(values, operator, columns):
    phases = operator.shape[1]
    values = jnp.concatenate(values, axis=0) if len(values) > 1 else values[0]
    total = dot(values, operator[0:phases]) + dot(values, operator[phases:])
    return [fold(total[at : at + 2 * columns]) for at in range(0, total.shape[0], 2 * columns)]


def whole(operator):
    return jnp.concatenate(split(operator), axis=0)


def kept_at(soon, late, j):
    return soon[j] if j < SOON else late[j - SOON]


def carry_terms(soon, late, past, first, last):
    phases = soon.shape[2]
    columns = soon.shape[1] - phases
    above = {n: kept_at(soon, late, n - 1)[phases:] for n in range(max(first, 1), last + 1)}

    def add(j):
        pairs = [(n, n - j) for n in above if n - j in past]
        held = whole(kept_at(soon, late, j)[0:phases])
        for (n, _), term in zip(pairs, apply_each([past[m] for _, m in pairs], held, columns)):
            above[n] += term
        return held

    return above, [functools.partial(add, j) for j in range(last)]


def carried(soon, late, past, first, last):
    above, calls = carry_terms(soon, late, past, first, last)
    for call in calls:
        call()
    return above


def wave(first, weight, base, now, above, feedback, due, emit, chores):
    levels, _, phases = base.shape
    for turn in range(levels + 2 * (CHUNK - 1)):
        for k in range(CHUNK):
            i = turn - 2 * k
            if not (0 <= i < levels and due(i, k)):
                continue
            n = first + 1 + k
            terms = []
            if (i - 1, n) in now:
                terms.append((now[i - 1, n], weight[i, 0 : 2 * phases]))
            if n > 1:
                over = stack(above[n - 1]) if i == levels - 1 else now[i + 1, n - 1]
                terms.append((over, weight[i, 2 * phases : 4 * phases]))
            value = base[i] + apply(terms) if terms else base[i]
            now[i, n] = stack(value)
            emit(i, k, value)
            if i == levels - 1:
                for later in range(n, first + CHUNK):
                    above[later] += apply([(now[i, n], feedback[later - n])])
        if chores and levels - 2 - turn < len(chores):
            chores.pop(0)()


def edge_level(levels, k):
    return levels - 2 - k


def chunk_kernel(chunk, places, part, names, *refs):
    given = dict(zip(names, refs))
    new_state, leaving = refs[len(names) :]
    weight, base = given["weight"], given["base"]
    levels, columns, phases = base.shape
    first = chunk * CHUNK

    @pl.when(jnp.logical_not(among(places)))
    def _():
        for name, target in (("state", new_state), ("leaving", leaving)):
            target[...] = given[name][...] if name in given else jnp.zeros_like(target)

    @pl.when(among(places))
    def _():
        zero = jnp.zeros((columns, phases), F32)
        above, feedback, chores = {first + k: zero for k in range(CHUNK)}, {}, []
        if part != "early":
            soon = given["soon"]

            def hold(j, call):
                feedback[j] = call()

            if first and "late" in given:
                past = {n + 1: stack(given["earlier"][n]) for n in range(first)}
                above, calls = carry_terms(soon, given["late"], past, first, first + CHUNK - 1)
            else:
                if not first:
                    above, _ = carry_terms(soon, None, {}, first, first + CHUNK - 1)
                elif "returned" in given:
                    above = {first + k: given["returned"][k] for k in range(CHUNK)}
                calls = [lambda j=j: whole(soon[j, 0:phases]) for j in range(SOON)]
            chores = [functools.partial(hold, j, call) for j, call in enumerate(calls)]
            while part == "late" and chores:
                chores.pop(0)()

        now = {}
        if part == "late":
            for k in range(CHUNK):
                now[edge_level(levels, k), first + 1 + k] = stack(given["edge"][k])
            new_state[...] = given["state"][...]
        elif first:
            for i in range(levels):
                now[i, first] = stack(given["state"][i])
        if part != "late" and "entering" in given:
            for k in range(CHUNK):
                now[-1, first + 1 + k] = stack(given["entering"][k])

        def due(i, k):
            return part == "all" or (i <= edge_level(levels, k)) == (part == "early")

        def emit(i, k, value):
            if k == CHUNK - 1:
                new_state[i] = value
            if i == (edge_level(levels, k) if part == "early" else levels - 1):
                leaving[k] = value

        wave(first, weight, base, now, above, feedback, due, emit, chores)


def run_chunk(chunk, places, given, part="all"):
    given = {name: x for name, x in given.items() if x is not None}
    levels, columns, phases = given["base"].shape
    return pl.pallas_call(
        functools.partial(chunk_kernel, chunk, tuple(places), part, tuple(given)),
        out_shape=[resident((levels, columns, phases), F32), resident((CHUNK, columns, phases), F32)],
        in_specs=[VMEM] * len(given),
        out_specs=[VMEM] * 2,
        compiler_params=pltpu.CompilerParams(vmem_limit_bytes=16 * 2**20),
        name="chunk",
    )(*[pin(x) for x in given.values()])


def among(places):
    return functools.reduce(jnp.logical_or, [lax.axis_index("lvl") == place for place in places])


def is_open(levels, a, i):
    return i + a < levels


def slot_of(levels, a, i):
    if not is_open(levels, a, i):
        return sum(range(1, a)) + i - (levels - a)
    return sum(levels - n if n < CHUNK else AHEAD - n for n in range(a)) + i


def get_answer(ways, levels, a, i, rows=slice(None)):
    high, low = ways[0:2] if is_open(levels, a, i) else ways[2:4]
    at = slot_of(levels, a, i)
    return high[at, rows], low[at, rows]


def spread_open_kernel(places, weight, base, high, low, kept):
    levels, columns, phases = base.shape
    rows = phases + columns

    def step(at, i, terms, keep=None):
        new = sum(dot_parts((high[x], low[x]), operator(weight, i, k)) for x, k in terms)
        unit, run = new[0:phases], new[phases:rows] + base[i]
        high[at, 0:phases], low[at, 0:phases] = split(unit)
        high[at, phases:rows], low[at, phases:rows] = split(run)
        if keep is not None:
            kept[keep, 0:phases], kept[keep, phases:rows] = unit, run

    @pl.when(among(places))
    def _():
        high[0, 0:phases], low[0, 0:phases] = operator(weight, 0, 0)
        high[0, phases:rows], low[0, phases:rows] = split(base[0])

        def up(i, _):
            step(i, i, [(i - 1, 0)])
            return 0

        lax.fori_loop(1, levels, up, 0)
        for a in range(1, AHEAD):
            first, old = slot_of(levels, a, 0), slot_of(levels, a - 1, 0)
            step(first, 0, [(old + 1, 1)], a - SOON if a >= SOON else None)

            def both(i, _, first=first, old=old):
                step(first + i, i, [(first + i - 1, 0), (old + i + 1, 1)])
                return 0

            lax.fori_loop(1, levels - a if a < CHUNK else AHEAD - a, both, 0)


def spread_close_kernel(
    places, weight, base, soon, open_high, open_low, before, high, low, state, leaving, feed_high, feed_low
):
    levels, columns, phases = base.shape
    rows = phases + columns
    top = levels - 1
    ways = (open_high, open_low, high, low)

    @pl.when(jnp.logical_not(among(places)))
    def _():
        state[...] = before[...]

    @pl.when(among(places))
    def _():
        for j in range(CHUNK - 1):
            feed_high[j], feed_low[j] = split(soon[j, 0:phases])
        for a in range(1, CHUNK):
            for i in range(levels - a, levels):
                new = dot_parts(get_answer(ways, levels, a, i - 1), operator(weight, i, 0))
                if i < top:
                    over = get_answer(ways, levels, a - 1, i + 1)
                else:
                    back = sum(
                        dot_parts(get_answer(ways, levels, a - 1 - j, top), (feed_high[j], feed_low[j])) for j in range(a)
                    )
                    end = back[phases:rows] + soon[a - 1, phases:rows]
                    over = split(jnp.concatenate([back[0:phases], end], axis=0))
                new += dot_parts(over, operator(weight, i, 1))
                at = slot_of(levels, a, i)
                high[at, 0:phases], low[at, 0:phases] = split(new[0:phases])
                high[at, phases:rows], low[at, phases:rows] = split(new[phases:rows] + base[i])

        def run(a, i):
            return sum(part.astype(F32) for part in get_answer(ways, levels, a, i, slice(phases, rows)))

        for i in range(levels):
            state[i] = run(CHUNK - 1, i)
        for a in range(CHUNK):
            leaving[a] = run(a, top)


def spread_open(places, weight, base):
    levels, columns, phases = base.shape
    assert levels > AHEAD and levels >= 2 * CHUNK - 1
    rows = phases + columns
    slots = slot_of(levels, AHEAD, 0)
    *ways, kept = pl.pallas_call(
        functools.partial(spread_open_kernel, tuple(places)),
        out_shape=[resident((slots, rows, phases), BF16)] * 2 + [resident((AHEAD - SOON, rows, phases), F32)],
        in_specs=[VMEM] * 2,
        out_specs=[VMEM] * 3,
        compiler_params=pltpu.CompilerParams(vmem_limit_bytes=16 * 2**20),
        name="spread_open",
    )(*[pin(x) for x in (weight, base)])
    return ways, kept


def spread_close(places, weight, base, soon, ways, state):
    levels, columns, phases = base.shape
    rows = phases + columns
    *more, state, leaving = pl.pallas_call(
        functools.partial(spread_close_kernel, tuple(places)),
        out_shape=[resident((sum(range(CHUNK)), rows, phases), BF16)] * 2
        + [resident((levels, columns, phases), F32), resident((CHUNK, columns, phases), F32)],
        in_specs=[VMEM] * 6,
        out_specs=[VMEM] * 4,
        scratch_shapes=[pltpu.VMEM((CHUNK - 1, phases, phases), BF16)] * 2,
        compiler_params=pltpu.CompilerParams(vmem_limit_bytes=16 * 2**20),
        name="spread_close",
    )(*[pin(x) for x in (weight, base, soon, *ways, state)])
    return [*ways, *more], state, leaving


def finish_leaving_kernel(place, *refs, levels):
    *ways, entering, leaving, before, new = refs
    columns, phases = entering.shape[1:]

    @pl.when(lax.axis_index("lvl") != place)
    def _():
        new[...] = before[...]

    @pl.when(lax.axis_index("lvl") == place)
    def _():
        values = [stack(entering[k]) for k in range(CHUNK)]
        total = [leaving[k] for k in range(CHUNK)]
        for a in range(CHUNK):
            pair = jnp.concatenate(get_answer(ways, levels, a, levels - 1, slice(0, phases)), axis=0)
            for k, term in enumerate(apply_each(values[: CHUNK - a], pair, columns)):
                total[a + k] += term
        for k in range(CHUNK):
            new[k] = total[k]


def finish_leaving(place, ways, entering, leaving, before, levels):
    return pl.pallas_call(
        functools.partial(finish_leaving_kernel, place, levels=levels),
        out_shape=resident(leaving.shape, F32),
        in_specs=[VMEM] * 7,
        out_specs=VMEM,
        compiler_params=pltpu.CompilerParams(vmem_limit_bytes=8 * 2**20),
        name="finish_leaving",
    )(*[pin(x) for x in (*ways, entering, leaving, before)])


def finish_state_kernel(place, *refs):
    *ways, entering, state, new = refs
    levels, _, phases = state.shape

    @pl.when(lax.axis_index("lvl") != place)
    def _():
        new[...] = state[...]

    @pl.when(lax.axis_index("lvl") == place)
    def _():
        values = [stack(entering[CHUNK - 1 - a]) for a in range(CHUNK)]
        for i in range(levels):
            terms = []
            for a in range(CHUNK):
                pair = jnp.concatenate(get_answer(ways, levels, a, i, slice(0, phases)), axis=0)
                terms.append((values[a], pair))
            new[i] = state[i] + apply(terms)


def finish_state(place, ways, entering, state, last):
    return pl.pallas_call(
        functools.partial(finish_state_kernel, place),
        out_shape=(jax.ShapeDtypeStruct if last else resident)(state.shape, F32),
        in_specs=[VMEM] * 6,
        out_specs=VMEM,
        compiler_params=pltpu.CompilerParams(vmem_limit_bytes=8 * 2**20),
        name="finish_state",
    )(*[pin(x) for x in (*ways, entering, state)])


def answer_kernel(step, soon, late, entering, returned):
    @pl.when(lax.axis_index("lvl") == step)
    def _():
        past = {n + 1: stack(entering[n]) for n in range(CHUNK)}
        above = carried(soon, late, past, CHUNK, 2 * CHUNK - 1)
        for k in range(CHUNK):
            returned[k] = above[CHUNK + k]


def answer(step, soon, late, entering):
    return pl.pallas_call(
        functools.partial(answer_kernel, step),
        out_shape=resident(entering.shape, F32),
        in_specs=[VMEM] * 3,
        out_specs=VMEM,
        compiler_params=pltpu.CompilerParams(vmem_limit_bytes=8 * 2**20),
        name="answer",
    )(*[pin(x) for x in (soon, late, entering)])


def local(inverse_diag, down_block, up_block, reward):
    given = reward.shape[1]
    columns = -(-given // 16) * 16
    if columns != given:
        reward = jnp.pad(reward, ((0, 0), (0, columns - given), (0, 0)))
    count = lax.axis_size("lvl")
    assert CHUNKS == 2 and count > 1
    top = count - 1
    ready = [d for d in range(1, count) if d % 2 == 0 or d == top]
    odd = [d for d in range(1, top, 2)]
    weights, begun, soon_here = prepare(inverse_diag, down_block, up_block, reward)
    weight, base = weights
    late_odd = respond(odd, weights, begun) if odd else None
    ways, late_here = spread_open(ready, weight, base)
    soon_odd = lax.ppermute(soon_here, "lvl", [(d + 1, d) for d in range(1, top, 2)])
    soon = lax.ppermute(soon_here, "lvl", [(d + 1, d) for d in range(0, top, 2)])
    late = lax.ppermute(late_odd, "lvl", [(d, d - 1) for d in odd]) if odd else None
    soon, late_here, late_odd = lax.optimization_barrier((soon, late_here, late_odd))
    late_top = None
    own = {"weight": weight, "base": base, "soon": soon}
    state = leaving = entering = parted = None
    for step in range(count + 1):
        place = step - 1
        earlier = leaving
        returned = edge = None
        if step % 2 == 0 and 0 < step < count:
            returned = lax.ppermute(answer(step, soon_here, late_here, entering), "lvl", [(step, place)])
            given_early = {"weight": weight, "base": base, "entering": entering, "state": state}
            state, edge = run_chunk(1, [place], given_early, "early")
        if place in ready and place < top:
            leaving = finish_leaving(place, ways, entering, parted, leaving, base.shape[0])
        if step in ready:
            if step < top:
                leaving = finish_leaving(step, ways, entering, parted_first, leaving, base.shape[0])
        elif step < count:
            state, leaving = run_chunk(
                0, [step], {**own, "soon": soon_odd if step % 2 else soon, "entering": entering, "state": state, "leaving": leaving}
            )
        if step == 1:
            top_sent, leaving = lax.optimization_barrier((late_here, leaving))
            late_top = lax.ppermute(top_sent, "lvl", [(top, top - 1)]) if top % 2 else None
            first_late = late if odd else late_top
            given_first = {**own, "late": first_late, "earlier": earlier, "state": state, "leaving": leaving}
            state, leaving = run_chunk(1, [0], given_first)
        if step in ready and step > 1:
            state = finish_state(step, ways, entering, state, False)
        if returned is not None:
            given_rest = {**own, "soon": soon_odd, "returned": returned, "edge": edge, "state": state, "leaving": leaving}
            state, leaving = run_chunk(1, [place], given_rest, "late")
        came = entering
        if step < count:
            pairs = [(d, d + 1) for d in (place, step) if 0 <= d < top]
            entering = lax.ppermute(leaving, "lvl", pairs) if pairs else None
        if step == 1:
            ways_then, leaving = lax.optimization_barrier((ways, leaving))
            ways, state, parted_first = spread_close(ready, weight, base, soon, ways_then, state)
            if entering is not None:
                entering, state = lax.optimization_barrier((entering, state))
        if place in ready:
            state = finish_state(place, ways, came, state, step == count)
        if step in ready:
            if step == 1:
                state = finish_state(step, ways, came, state, False)
            extra = {} if step == top else {"late": late_top if step == top - 1 else late, "earlier": leaving}
            state, parted = run_chunk(1, [step], {**own, **extra, "state": state})
    return state[:, :given] if columns != given else state


def solution(mesh):
    placed = (
        P(("grp", "lvl"), None, None),
        P(("grp", "lvl"), None, None),
        P(("grp", "lvl"), None, None),
        P(("grp", "lvl"), "col", None),
    )
    return jax.shard_map(
        local, mesh=mesh, in_specs=placed, out_specs=P(("grp", "lvl"), "col", None), check_vma=False
    )
```

```python
import functools

import jax
import jax.numpy as jnp
from jax import lax
from jax.experimental import pallas as pl
from jax.experimental.pallas import tpu as pltpu
from jax.sharding import PartitionSpec as P

SWEEPS = 8
CHUNK = 4
CHUNKS = SWEEPS // CHUNK
AHEAD = SWEEPS - 1
SOON = CHUNK - 1
F32 = jnp.float32
BF16 = jnp.bfloat16


def resident(shape, dtype):
    return pltpu.VMEM(shape, dtype)


def pin(x, memory=pltpu.VMEM):
    return pltpu.with_memory_space_constraint(x, memory)


def split(x):
    high = x.astype(BF16)
    return high, (x - high.astype(F32)).astype(BF16)


def dot(a, b):
    return jnp.dot(a, b, preferred_element_type=F32)


def dot_nt(a, b):
    return lax.dot_general(a, b, (((1,), (1,)), ((), ())), preferred_element_type=F32)


def dot_parts(a, b, dot=dot):
    return dot(a[0], b[0]) + (dot(a[0], b[1]) + dot(a[1], b[0]))


def place_operator(weight, i, k, value):
    phases = value.shape[0]
    for n, part in enumerate(split(value.T)):
        weight[i, (2 * k + n) * phases : (2 * k + n + 1) * phases] = part


def operator(weight, i, k):
    phases = weight.shape[2]
    at = 2 * k * phases
    return weight[i, at : at + phases], weight[i, at + phases : at + 2 * phases]


def response(first, last, x_high, x_low, weight, base, kept):
    _, columns, phases = base.shape
    rows = phases + columns

    def store(i, new):
        top = new[0:phases]
        end = new[phases:rows] + base[i]
        x_high[i, 0:phases], x_low[i, 0:phases] = split(top)
        x_high[i, phases:rows], x_low[i, phases:rows] = split(end)
        return top, end

    def from_below(i):
        return dot_parts((x_high[i - 1], x_low[i - 1]), operator(weight, i, 0))

    def from_above(i):
        return dot_parts((x_high[i + 1], x_low[i + 1]), operator(weight, i, 1))

    for d in range(first, last):
        if d == 0:
            high, low = weight[0, 0:phases], weight[0, phases : 2 * phases]
            x_high[0, 0:phases], x_low[0, 0:phases] = high, low
            x_high[0, phases:rows], x_low[0, phases:rows] = split(base[0])
            kept[0, 0:phases] = high.astype(F32) + low.astype(F32)
            kept[0, phases:rows] = base[0]
            continue
        store(d, from_below(d))

        for i in range(d - 1, 0, -1):
            store(i, from_below(i) + from_above(i))
        kept[d - first, 0:phases], kept[d - first, phases:rows] = store(0, from_above(0))


def products(wanted, here_from, weight, base, inv, down, up, pay):
    for i in wanted:
        here_from(i)
        here = split(inv[i])
        for k, block in ((0, down), (1, up)):
            if k in wanted[i]:
                place_operator(weight, i, k, dot_parts(here, split(block[i])))
        if 2 in wanted[i]:
            base[i] = dot_parts(split(pay[i]), here, dot_nt)


def prepare_kernel(inv_far, down_far, up_far, pay_far, weight, base, x_high, x_low, kept, inv, down, up, pay, sems):
    levels = pay.shape[0]
    cuts = ((0, 1), (1, SOON), (SOON, levels))

    def copies(part):
        at, end = cuts[part]
        pairs = [(inv_far, inv), (down_far, down), (up_far, up)]
        found = [
            pltpu.make_async_copy(far.at[at:end], near.at[at:end], sems.at[n, part])
            for n, (far, near) in enumerate(pairs)
        ]
        return found + ([pltpu.make_async_copy(pay_far, pay, sems.at[3, 0])] if part == 0 else [])

    def wait(i):
        for part, (at, _) in enumerate(cuts):
            if i == at:
                for copy in copies(part):
                    copy.wait()

    for part in range(len(cuts)):
        for copy in copies(part):
            copy.start()
    wanted = {i: (0, 1, 2) if i < SOON - 1 else (0, 2) for i in range(SOON)}
    products(wanted, wait, weight, base, inv, down, up, pay)
    response(0, SOON, x_high, x_low, weight, base, kept)
    wait(SOON)


def prepare_rest_kernel(weight_soon, base_soon, inv, down, up, pay, weight, base):
    levels, _, phases = pay.shape
    for i in range(SOON):
        rows = (4 if i < SOON - 1 else 2) * phases
        weight[i, 0:rows] = weight_soon[i, 0:rows]
    base[0:SOON] = base_soon[...]
    wanted = {i: (0, 1, 2) if i >= SOON else (1,) for i in range(SOON - 1, levels)}
    products(wanted, lambda i: None, weight, base, inv, down, up, pay)


def respond_kernel(places, weight, base, x_high_soon, x_low_soon, kept, x_high, x_low):
    @pl.when(among(places))
    def _():
        x_high[0:SOON] = x_high_soon[...]
        x_low[0:SOON] = x_low_soon[...]
        response(SOON, AHEAD, x_high, x_low, weight, base, kept)


VMEM = pl.BlockSpec(memory_space=pltpu.VMEM)
HBM = pl.BlockSpec(memory_space=pltpu.HBM)


def operators(levels, columns, phases):
    return [resident((levels, 4 * phases, phases), BF16), resident((levels, columns, phases), F32)]


def prepare(inverse_diag, down_block, up_block, reward):
    levels, columns, phases = reward.shape
    rows = phases + columns
    matrix = resident((levels, phases, phases), F32)
    *soon, x_high, x_low, kept_soon, inv, down, up, pay = pl.pallas_call(
        prepare_kernel,
        out_shape=operators(SOON, columns, phases)
        + [resident((SOON, rows, phases), BF16)] * 2
        + [resident((SOON, rows, phases), F32)]
        + [matrix] * 3
        + [resident((levels, columns, phases), F32)],
        in_specs=[HBM] * 4,
        out_specs=[VMEM] * 9,
        scratch_shapes=[pltpu.SemaphoreType.DMA((4, 3))],
        compiler_params=pltpu.CompilerParams(vmem_limit_bytes=16 * 2**20),
        name="prepare",
    )(*[pin(x, pltpu.HBM) for x in (inverse_diag, down_block, up_block, reward)])
    weights = pl.pallas_call(
        prepare_rest_kernel,
        out_shape=operators(levels, columns, phases),
        in_specs=[VMEM] * 6,
        out_specs=[VMEM] * 2,
        compiler_params=pltpu.CompilerParams(vmem_limit_bytes=16 * 2**20),
        name="prepare_rest",
    )(*[pin(x) for x in (*soon, inv, down, up, pay)])
    return weights, (x_high, x_low), kept_soon


def respond(places, weights, started):
    _, rows, phases = started[0].shape
    return pl.pallas_call(
        functools.partial(respond_kernel, tuple(places)),
        out_shape=resident((AHEAD - SOON, rows, phases), F32),
        in_specs=[VMEM] * 4,
        out_specs=VMEM,
        scratch_shapes=[pltpu.VMEM((AHEAD, rows, phases), BF16)] * 2,
        compiler_params=pltpu.CompilerParams(vmem_limit_bytes=16 * 2**20),
        name="respond",
    )(*[pin(x) for x in (*weights, *started)])


def stack(x):
    high = x.astype(BF16).astype(F32)
    return jnp.concatenate([high, x - high], axis=0).astype(BF16)


def fold(total):
    half = total.shape[0] // 2
    return total[:half] + total[half:]


def apply(terms):
    values = jnp.concatenate([x for x, _ in terms for _ in range(2)], axis=1)
    return fold(dot(values, jnp.concatenate([operator for _, operator in terms], axis=0)))


def apply_each(values, operator, columns):
    phases = operator.shape[1]
    values = jnp.concatenate(values, axis=0) if len(values) > 1 else values[0]
    total = dot(values, operator[0:phases]) + dot(values, operator[phases:])
    return [fold(total[at : at + 2 * columns]) for at in range(0, total.shape[0], 2 * columns)]


def whole(operator):
    return jnp.concatenate(split(operator), axis=0)


def kept_at(soon, late, j):
    return soon[j] if j < SOON else late[j - SOON]


def carry_terms(soon, late, past, first, last):
    phases = soon.shape[2]
    columns = soon.shape[1] - phases
    above = {n: kept_at(soon, late, n - 1)[phases:] for n in range(max(first, 1), last + 1)}

    def add(j):
        pairs = [(n, n - j) for n in above if n - j in past]
        held = whole(kept_at(soon, late, j)[0:phases])
        for (n, _), term in zip(pairs, apply_each([past[m] for _, m in pairs], held, columns)):
            above[n] += term
        return held

    return above, [functools.partial(add, j) for j in range(last)]


def carried(soon, late, past, first, last):
    above, calls = carry_terms(soon, late, past, first, last)
    for call in calls:
        call()
    return above


def wave(first, weight, base, now, above, feedback, due, emit, chores):
    levels, _, phases = base.shape
    for turn in range(levels + 2 * (CHUNK - 1)):
        for k in range(CHUNK):
            i = turn - 2 * k
            if not (0 <= i < levels and due(i, k)):
                continue
            n = first + 1 + k
            terms = []
            if (i - 1, n) in now:
                terms.append((now[i - 1, n], weight[i, 0 : 2 * phases]))
            if n > 1 and not (i == levels - 1 and above is None):
                over = stack(above[n - 1]) if i == levels - 1 else now[i + 1, n - 1]
                terms.append((over, weight[i, 2 * phases : 4 * phases]))
            value = base[i] + apply(terms) if terms else base[i]
            now[i, n] = stack(value)
            emit(i, k, value)
            if i == levels - 1 and above is not None:
                for later in range(n, first + CHUNK):
                    above[later] += apply([(now[i, n], feedback[later - n])])
        if chores and levels - 2 - turn < len(chores):
            chores.pop(0)()


def edge_level(levels, k):
    return levels - 2 - k


def chunk_kernel(chunk, places, part, names, *refs):
    given = dict(zip(names, refs))
    new_state, *leaving = refs[len(names) :]
    leaving = leaving[0] if leaving else None
    weight, base = given["weight"], given["base"]
    levels, columns, phases = base.shape
    first = chunk * CHUNK

    @pl.when(jnp.logical_not(among(places)))
    def _():
        for name, target in (("state", new_state), ("leaving", leaving)):
            if target is not None:
                target[...] = given[name][...] if name in given else jnp.zeros_like(target)

    @pl.when(among(places))
    def _():
        zero = jnp.zeros((columns, phases), F32)
        above, feedback, chores = {first + k: zero for k in range(CHUNK)}, {}, []
        if "soon" not in given and part != "early":
            above = None
        elif part != "early":
            soon = given["soon"]

            def hold(j, call):
                feedback[j] = call()

            if first and "late" in given:
                past = {n + 1: stack(given["earlier"][n]) for n in range(first)}
                above, calls = carry_terms(soon, given["late"], past, first, first + CHUNK - 1)
            else:
                if not first:
                    above, _ = carry_terms(soon, None, {}, first, first + CHUNK - 1)
                elif "returned" in given:
                    above = {first + k: given["returned"][k] for k in range(CHUNK)}
                calls = [lambda j=j: whole(soon[j, 0:phases]) for j in range(SOON)]
            chores = [functools.partial(hold, j, call) for j, call in enumerate(calls)]
            while part == "late" and chores:
                chores.pop(0)()

        now = {}
        if part == "late":
            for k in range(CHUNK):
                now[edge_level(levels, k), first + 1 + k] = stack(given["edge"][k])
            new_state[...] = given["state"][...]
        elif first:
            for i in range(levels):
                now[i, first] = stack(given["state"][i])
        if part != "late" and "entering" in given:
            for k in range(CHUNK):
                now[-1, first + 1 + k] = stack(given["entering"][k])

        def due(i, k):
            return part == "all" or (i <= edge_level(levels, k)) == (part == "early")

        def emit(i, k, value):
            if k == CHUNK - 1:
                new_state[i] = value
            if leaving is not None and i == (edge_level(levels, k) if part == "early" else levels - 1):
                leaving[k] = value

        wave(first, weight, base, now, above, feedback, due, emit, chores)


def run_chunk(chunk, places, given, part="all", sends=True):
    given = {name: x for name, x in given.items() if x is not None}
    levels, columns, phases = given["base"].shape
    return pl.pallas_call(
        functools.partial(chunk_kernel, chunk, tuple(places), part, tuple(given)),
        out_shape=[resident((levels, columns, phases), F32)] + [resident((CHUNK, columns, phases), F32)] * sends,
        in_specs=[VMEM] * len(given),
        out_specs=[VMEM] * (1 + sends),
        compiler_params=pltpu.CompilerParams(vmem_limit_bytes=16 * 2**20),
        name="chunk",
    )(*[pin(x) for x in given.values()])


def among(places):
    return functools.reduce(jnp.logical_or, [lax.axis_index("lvl") == place for place in places])


def is_open(levels, a, i):
    return i + a < levels


def slot_of(levels, a, i):
    if not is_open(levels, a, i):
        return sum(range(1, a)) + i - (levels - a)
    return sum(levels - n if n < CHUNK else AHEAD - n for n in range(a)) + i


def get_answer(ways, levels, a, i, rows=slice(None)):
    high, low = ways[0:2] if is_open(levels, a, i) else ways[2:4]
    at = slot_of(levels, a, i)
    return high[at, rows], low[at, rows]


def spread_open_kernel(places, weight, base, high, low, kept):
    levels, columns, phases = base.shape
    rows = phases + columns

    def step(at, i, terms, keep=None):
        new = sum(dot_parts((high[x], low[x]), operator(weight, i, k)) for x, k in terms)
        unit, run = new[0:phases], new[phases:rows] + base[i]
        high[at, 0:phases], low[at, 0:phases] = split(unit)
        high[at, phases:rows], low[at, phases:rows] = split(run)
        if keep is not None:
            kept[keep, 0:phases], kept[keep, phases:rows] = unit, run

    @pl.when(among(places))
    def _():
        high[0, 0:phases], low[0, 0:phases] = operator(weight, 0, 0)
        high[0, phases:rows], low[0, phases:rows] = split(base[0])

        for i in range(1, levels):
            step(i, i, [(i - 1, 0)])
        for a in range(1, AHEAD):
            first, old = slot_of(levels, a, 0), slot_of(levels, a - 1, 0)
            step(first, 0, [(old + 1, 1)], a - SOON if a >= SOON else None)

            for i in range(1, levels - a if a < CHUNK else AHEAD - a):
                step(first + i, i, [(first + i - 1, 0), (old + i + 1, 1)])


def spread_close_kernel(
    places, weight, base, soon, open_high, open_low, before, high, low, state, leaving, feed_high, feed_low
):
    levels, columns, phases = base.shape
    rows = phases + columns
    top = levels - 1
    ways = (open_high, open_low, high, low)

    @pl.when(jnp.logical_not(among(places)))
    def _():
        state[...] = before[...]

    @pl.when(among(places))
    def _():
        for j in range(CHUNK - 1):
            feed_high[j], feed_low[j] = split(soon[j, 0:phases])
        for a in range(1, CHUNK):
            for i in range(levels - a, levels):
                new = dot_parts(get_answer(ways, levels, a, i - 1), operator(weight, i, 0))
                if i < top:
                    over = get_answer(ways, levels, a - 1, i + 1)
                else:
                    back = sum(
                        dot_parts(get_answer(ways, levels, a - 1 - j, top), (feed_high[j], feed_low[j])) for j in range(a)
                    )
                    end = back[phases:rows] + soon[a - 1, phases:rows]
                    over = split(jnp.concatenate([back[0:phases], end], axis=0))
                new += dot_parts(over, operator(weight, i, 1))
                at = slot_of(levels, a, i)
                high[at, 0:phases], low[at, 0:phases] = split(new[0:phases])
                high[at, phases:rows], low[at, phases:rows] = split(new[phases:rows] + base[i])

        def run(a, i):
            return sum(part.astype(F32) for part in get_answer(ways, levels, a, i, slice(phases, rows)))

        for i in range(levels):
            state[i] = run(CHUNK - 1, i)
        for a in range(CHUNK):
            leaving[a] = run(a, top)


def spread_open(places, weight, base):
    levels, columns, phases = base.shape
    assert levels > AHEAD and levels >= 2 * CHUNK - 1
    rows = phases + columns
    slots = slot_of(levels, AHEAD, 0)
    *ways, kept = pl.pallas_call(
        functools.partial(spread_open_kernel, tuple(places)),
        out_shape=[resident((slots, rows, phases), BF16)] * 2 + [resident((AHEAD - SOON, rows, phases), F32)],
        in_specs=[VMEM] * 2,
        out_specs=[VMEM] * 3,
        compiler_params=pltpu.CompilerParams(vmem_limit_bytes=16 * 2**20),
        name="spread_open",
    )(*[pin(x) for x in (weight, base)])
    return ways, kept


def spread_close(places, weight, base, soon, ways, state):
    levels, columns, phases = base.shape
    rows = phases + columns
    *more, state, leaving = pl.pallas_call(
        functools.partial(spread_close_kernel, tuple(places)),
        out_shape=[resident((sum(range(CHUNK)), rows, phases), BF16)] * 2
        + [resident((levels, columns, phases), F32), resident((CHUNK, columns, phases), F32)],
        in_specs=[VMEM] * 6,
        out_specs=[VMEM] * 4,
        scratch_shapes=[pltpu.VMEM((CHUNK - 1, phases, phases), BF16)] * 2,
        compiler_params=pltpu.CompilerParams(vmem_limit_bytes=16 * 2**20),
        name="spread_close",
    )(*[pin(x) for x in (weight, base, soon, *ways, state)])
    return [*ways, *more], state, leaving


def finish_leaving_kernel(place, *refs, levels):
    *ways, entering, leaving, before, new = refs
    columns, phases = entering.shape[1:]

    @pl.when(lax.axis_index("lvl") != place)
    def _():
        new[...] = before[...]

    @pl.when(lax.axis_index("lvl") == place)
    def _():
        values = [stack(entering[k]) for k in range(CHUNK)]
        total = [leaving[k] for k in range(CHUNK)]
        for a in range(CHUNK):
            pair = jnp.concatenate(get_answer(ways, levels, a, levels - 1, slice(0, phases)), axis=0)
            for k, term in enumerate(apply_each(values[: CHUNK - a], pair, columns)):
                total[a + k] += term
        for k in range(CHUNK):
            new[k] = total[k]


def finish_leaving(place, ways, entering, leaving, before, levels):
    return pl.pallas_call(
        functools.partial(finish_leaving_kernel, place, levels=levels),
        out_shape=resident(leaving.shape, F32),
        in_specs=[VMEM] * 7,
        out_specs=VMEM,
        compiler_params=pltpu.CompilerParams(vmem_limit_bytes=8 * 2**20),
        name="finish_leaving",
    )(*[pin(x) for x in (*ways, entering, leaving, before)])


def finish_state_kernel(place, *refs):
    *ways, entering, state, new = refs
    levels, _, phases = state.shape

    @pl.when(lax.axis_index("lvl") != place)
    def _():
        new[...] = state[...]

    @pl.when(lax.axis_index("lvl") == place)
    def _():
        values = [stack(entering[CHUNK - 1 - a]) for a in range(CHUNK)]
        for i in range(levels):
            terms = []
            for a in range(CHUNK):
                pair = jnp.concatenate(get_answer(ways, levels, a, i, slice(0, phases)), axis=0)
                terms.append((values[a], pair))
            new[i] = state[i] + apply(terms)


def finish_state(place, ways, entering, state, last):
    return pl.pallas_call(
        functools.partial(finish_state_kernel, place),
        out_shape=(jax.ShapeDtypeStruct if last else resident)(state.shape, F32),
        in_specs=[VMEM] * 6,
        out_specs=VMEM,
        compiler_params=pltpu.CompilerParams(vmem_limit_bytes=8 * 2**20),
        name="finish_state",
    )(*[pin(x) for x in (*ways, entering, state)])


def answer_kernel(step, soon, late, entering, returned):
    @pl.when(lax.axis_index("lvl") == step)
    def _():
        past = {n + 1: stack(entering[n]) for n in range(CHUNK)}
        above = carried(soon, late, past, CHUNK, 2 * CHUNK - 1)
        for k in range(CHUNK):
            returned[k] = above[CHUNK + k]


def answer(step, soon, late, entering):
    return pl.pallas_call(
        functools.partial(answer_kernel, step),
        out_shape=resident(entering.shape, F32),
        in_specs=[VMEM] * 3,
        out_specs=VMEM,
        compiler_params=pltpu.CompilerParams(vmem_limit_bytes=8 * 2**20),
        name="answer",
    )(*[pin(x) for x in (soon, late, entering)])


def local(inverse_diag, down_block, up_block, reward):
    given = reward.shape[1]
    columns = -(-given // 16) * 16
    if columns != given:
        reward = jnp.pad(reward, ((0, 0), (0, columns - given), (0, 0)))
    count = lax.axis_size("lvl")
    assert CHUNKS == 2 and count > 1
    top = count - 1
    ready = [d for d in range(1, count) if d % 2 == 0 or d == top]
    odd = [d for d in range(1, top, 2)]
    weights, begun, soon_here = prepare(inverse_diag, down_block, up_block, reward)
    weight, base = weights
    late_odd = respond(odd, weights, begun) if odd else None
    ways, late_here = spread_open(ready, weight, base)
    soon_odd = lax.ppermute(soon_here, "lvl", [(d + 1, d) for d in range(1, top, 2)])
    soon = lax.ppermute(soon_here, "lvl", [(d + 1, d) for d in range(0, top, 2)])
    late = lax.ppermute(late_odd, "lvl", [(d, d - 1) for d in odd]) if odd else None
    soon, late_here, late_odd = lax.optimization_barrier((soon, late_here, late_odd))
    late_top = None
    own = {"weight": weight, "base": base, "soon": soon}
    state = leaving = entering = parted = None
    for step in range(count + 1):
        place = step - 1
        earlier = leaving
        returned = edge = None
        if step % 2 == 0 and 0 < step < count:
            returned = lax.ppermute(answer(step, soon_here, late_here, entering), "lvl", [(step, place)])
            given_early = {"weight": weight, "base": base, "entering": entering, "state": state}
            state, edge = run_chunk(1, [place], given_early, "early")
        if place in ready and place < top:
            leaving = finish_leaving(place, ways, entering, parted, leaving, base.shape[0])
        if step in ready:
            if step < top:
                leaving = finish_leaving(step, ways, entering, parted_first, leaving, base.shape[0])
        elif step < count:
            state, leaving = run_chunk(
                0, [step], {**own, "soon": soon_odd if step % 2 else soon, "entering": entering, "state": state, "leaving": leaving}
            )
        if step == 1:
            top_sent, leaving = lax.optimization_barrier((late_here, leaving))
            late_top = lax.ppermute(top_sent, "lvl", [(top, top - 1)]) if top % 2 else None
            first_late = late if odd else late_top
            given_first = {**own, "late": first_late, "earlier": earlier, "state": state, "leaving": leaving}
            state, leaving = run_chunk(1, [0], given_first)
        if step in ready and step > 1:
            state = finish_state(step, ways, entering, state, False)
        if returned is not None:
            given_rest = {**own, "soon": soon_odd, "returned": returned, "edge": edge, "state": state, "leaving": leaving}
            state, leaving = run_chunk(1, [place], given_rest, "late")
        came = entering
        if step < count:
            pairs = [(d, d + 1) for d in (place, step) if 0 <= d < top]
            entering = lax.ppermute(leaving, "lvl", pairs) if pairs else None
        if step == 1:
            ways_then, leaving = lax.optimization_barrier((ways, leaving))
            ways, state, parted_first = spread_close(ready, weight, base, soon, ways_then, state)
            if entering is not None:
                entering, state = lax.optimization_barrier((entering, state))
        if place in ready:
            state = finish_state(place, ways, came, state, step == count)
        if step in ready:
            if step == 1:
                state = finish_state(step, ways, came, state, False)
            if step == top:
                (state,) = run_chunk(1, [step], {"weight": weight, "base": base, "state": state}, sends=False)
            else:
                extra = {"late": late_top if step == top - 1 else late, "earlier": leaving}
                state, parted = run_chunk(1, [step], {**own, **extra, "state": state})
    return state[:, :given] if columns != given else state


def solution(mesh):
    placed = (
        P(("grp", "lvl"), None, None),
        P(("grp", "lvl"), None, None),
        P(("grp", "lvl"), None, None),
        P(("grp", "lvl"), "col", None),
    )
    return jax.shard_map(
        local, mesh=mesh, in_specs=placed, out_specs=P(("grp", "lvl"), "col", None), check_vma=False
    )
```

```python
import functools

import jax
import jax.numpy as jnp
from jax import lax
from jax.experimental import pallas as pl
from jax.experimental.pallas import tpu as pltpu
from jax.sharding import PartitionSpec as P

SWEEPS = 8
CHUNK = 4
CHUNKS = SWEEPS // CHUNK
AHEAD = SWEEPS - 1
SOON = CHUNK - 1
F32 = jnp.float32
BF16 = jnp.bfloat16


def resident(shape, dtype):
    return pltpu.VMEM(shape, dtype)


def pin(x, memory=pltpu.VMEM):
    return pltpu.with_memory_space_constraint(x, memory)


def split(x):
    high = x.astype(BF16)
    return high, (x - high.astype(F32)).astype(BF16)


def dot(a, b):
    return jnp.dot(a, b, preferred_element_type=F32)


def dot_nt(a, b):
    return lax.dot_general(a, b, (((1,), (1,)), ((), ())), preferred_element_type=F32)


def dot_parts(a, b, dot=dot):
    return dot(a[0], b[0]) + (dot(a[0], b[1]) + dot(a[1], b[0]))


def place_operator(weight, i, k, value):
    phases = value.shape[0]
    for n, part in enumerate(split(value.T)):
        weight[i, (2 * k + n) * phases : (2 * k + n + 1) * phases] = part


def operator(weight, i, k):
    phases = weight.shape[2]
    at = 2 * k * phases
    return weight[i, at : at + phases], weight[i, at + phases : at + 2 * phases]


def response(first, last, x_high, x_low, weight, base, kept):
    _, columns, phases = base.shape
    rows = phases + columns

    def store(i, new):
        top = new[0:phases]
        end = new[phases:rows] + base[i]
        x_high[i, 0:phases], x_low[i, 0:phases] = split(top)
        x_high[i, phases:rows], x_low[i, phases:rows] = split(end)
        return top, end

    def from_below(i):
        return dot_parts((x_high[i - 1], x_low[i - 1]), operator(weight, i, 0))

    def from_above(i):
        return dot_parts((x_high[i + 1], x_low[i + 1]), operator(weight, i, 1))

    if first == 0:
        high, low = operator(weight, 0, 0)
        x_high[0, 0:phases], x_low[0, 0:phases] = high, low
        x_high[0, phases:rows], x_low[0, phases:rows] = split(base[0])
        kept[0, 0:phases] = high.astype(F32) + low.astype(F32)
        kept[0, phases:rows] = base[0]
    units = [(a, d - a) for d in range(max(first, 1), last) for a in range(d + 1)]
    for a, i in sorted(units, key=lambda unit: (unit[1] + 2 * unit[0], unit)):
        if a == 0:
            store(i, from_below(i))
        elif i > 0:
            store(i, from_below(i) + from_above(i))
        else:
            kept[a - first, 0:phases], kept[a - first, phases:rows] = store(0, from_above(0))


def products(wanted, here_from, weight, base, inv, down, up, pay):
    for i in wanted:
        here_from(i)
        here = split(inv[i])
        for k, block in ((0, down), (1, up)):
            if k in wanted[i]:
                place_operator(weight, i, k, dot_parts(here, split(block[i])))
        if 2 in wanted[i]:
            base[i] = dot_parts(split(pay[i]), here, dot_nt)


def prepare_kernel(inv_far, down_far, up_far, pay_far, weight, base, x_high, x_low, kept, inv, down, up, pay, sems):
    levels = pay.shape[0]
    cuts = ((0, 1), (1, SOON), (SOON, levels))

    def copies(part):
        at, end = cuts[part]
        pairs = [(inv_far, inv), (down_far, down), (up_far, up)]
        found = [
            pltpu.make_async_copy(far.at[at:end], near.at[at:end], sems.at[n, part])
            for n, (far, near) in enumerate(pairs)
        ]
        return found + ([pltpu.make_async_copy(pay_far, pay, sems.at[3, 0])] if part == 0 else [])

    def wait(i):
        for part, (at, _) in enumerate(cuts):
            if i == at:
                for copy in copies(part):
                    copy.wait()

    for part in range(len(cuts)):
        for copy in copies(part):
            copy.start()
    wanted = {i: (0, 1, 2) if i < SOON - 1 else (0, 2) for i in range(SOON)}
    products(wanted, wait, weight, base, inv, down, up, pay)
    response(0, SOON, x_high, x_low, weight, base, kept)
    wait(SOON)


def prepare_rest_kernel(weight_soon, base_soon, inv, down, up, pay, weight, base):
    levels, _, phases = pay.shape
    for i in range(SOON):
        rows = (4 if i < SOON - 1 else 2) * phases
        weight[i, 0:rows] = weight_soon[i, 0:rows]
    base[0:SOON] = base_soon[...]
    wanted = {i: (0, 1, 2) if i >= SOON else (1,) for i in range(SOON - 1, levels)}
    products(wanted, lambda i: None, weight, base, inv, down, up, pay)


def respond_kernel(places, weight, base, x_high_soon, x_low_soon, kept, x_high, x_low):
    @pl.when(among(places))
    def _():
        x_high[0:SOON] = x_high_soon[...]
        x_low[0:SOON] = x_low_soon[...]
        response(SOON, AHEAD, x_high, x_low, weight, base, kept)


VMEM = pl.BlockSpec(memory_space=pltpu.VMEM)
HBM = pl.BlockSpec(memory_space=pltpu.HBM)


def operators(levels, columns, phases):
    return [resident((levels, 4 * phases, phases), BF16), resident((levels, columns, phases), F32)]


def prepare(inverse_diag, down_block, up_block, reward):
    levels, columns, phases = reward.shape
    rows = phases + columns
    matrix = resident((levels, phases, phases), F32)
    *soon, x_high, x_low, kept_soon, inv, down, up, pay = pl.pallas_call(
        prepare_kernel,
        out_shape=operators(SOON, columns, phases)
        + [resident((SOON, rows, phases), BF16)] * 2
        + [resident((SOON, rows, phases), F32)]
        + [matrix] * 3
        + [resident((levels, columns, phases), F32)],
        in_specs=[HBM] * 4,
        out_specs=[VMEM] * 9,
        scratch_shapes=[pltpu.SemaphoreType.DMA((4, 3))],
        compiler_params=pltpu.CompilerParams(vmem_limit_bytes=16 * 2**20),
        name="prepare",
    )(*[pin(x, pltpu.HBM) for x in (inverse_diag, down_block, up_block, reward)])
    weights = pl.pallas_call(
        prepare_rest_kernel,
        out_shape=operators(levels, columns, phases),
        in_specs=[VMEM] * 6,
        out_specs=[VMEM] * 2,
        compiler_params=pltpu.CompilerParams(vmem_limit_bytes=16 * 2**20),
        name="prepare_rest",
    )(*[pin(x) for x in (*soon, inv, down, up, pay)])
    return weights, (x_high, x_low), kept_soon


def respond(places, weights, started):
    _, rows, phases = started[0].shape
    return pl.pallas_call(
        functools.partial(respond_kernel, tuple(places)),
        out_shape=resident((AHEAD - SOON, rows, phases), F32),
        in_specs=[VMEM] * 4,
        out_specs=VMEM,
        scratch_shapes=[pltpu.VMEM((AHEAD, rows, phases), BF16)] * 2,
        compiler_params=pltpu.CompilerParams(vmem_limit_bytes=16 * 2**20),
        name="respond",
    )(*[pin(x) for x in (*weights, *started)])


def stack(x):
    high = x.astype(BF16).astype(F32)
    return jnp.concatenate([high, x - high], axis=0).astype(BF16)


def fold(total):
    half = total.shape[0] // 2
    return total[:half] + total[half:]


def apply(terms):
    values = jnp.concatenate([x for x, _ in terms for _ in range(2)], axis=1)
    return fold(dot(values, jnp.concatenate([operator for _, operator in terms], axis=0)))


def apply_each(values, operator, columns):
    phases = operator.shape[1]
    values = jnp.concatenate(values, axis=0) if len(values) > 1 else values[0]
    total = dot(values, operator[0:phases]) + dot(values, operator[phases:])
    return [fold(total[at : at + 2 * columns]) for at in range(0, total.shape[0], 2 * columns)]


def whole(operator):
    return jnp.concatenate(split(operator), axis=0)


def kept_at(soon, late, j):
    return soon[j] if j < SOON else late[j - SOON]


def carry_terms(soon, late, past, first, last):
    phases = soon.shape[2]
    columns = soon.shape[1] - phases
    above = {n: kept_at(soon, late, n - 1)[phases:] for n in range(max(first, 1), last + 1)}

    def add(j):
        pairs = [(n, n - j) for n in above if n - j in past]
        held = whole(kept_at(soon, late, j)[0:phases])
        for (n, _), term in zip(pairs, apply_each([past[m] for _, m in pairs], held, columns)):
            above[n] += term
        return held

    return above, [functools.partial(add, j) for j in range(last)]


def carried(soon, late, past, first, last):
    above, calls = carry_terms(soon, late, past, first, last)
    for call in calls:
        call()
    return above


def wave(first, weight, base, now, above, feedback, due, emit, chores):
    levels, _, phases = base.shape
    for turn in range(levels + 2 * (CHUNK - 1)):
        for k in range(CHUNK):
            i = turn - 2 * k
            if not (0 <= i < levels and due(i, k)):
                continue
            n = first + 1 + k
            terms = []
            if (i - 1, n) in now:
                terms.append((now[i - 1, n], weight[i, 0 : 2 * phases]))
            if n > 1 and not (i == levels - 1 and above is None):
                over = stack(above[n - 1]) if i == levels - 1 else now[i + 1, n - 1]
                terms.append((over, weight[i, 2 * phases : 4 * phases]))
            value = base[i] + apply(terms) if terms else base[i]
            now[i, n] = stack(value)
            emit(i, k, value)
            if i == levels - 1 and above is not None:
                for later in range(n, first + CHUNK):
                    above[later] += apply([(now[i, n], feedback[later - n])])
        if chores and levels - 2 - turn < len(chores):
            chores.pop(0)()


def edge_level(levels, k):
    return levels - 2 - k


def chunk_kernel(chunk, places, part, names, *refs):
    given = dict(zip(names, refs))
    new_state, *leaving = refs[len(names) :]
    leaving = leaving[0] if leaving else None
    weight, base = given["weight"], given["base"]
    levels, columns, phases = base.shape
    first = chunk * CHUNK

    @pl.when(jnp.logical_not(among(places)))
    def _():
        for name, target in (("state", new_state), ("leaving", leaving)):
            if target is not None:
                target[...] = given[name][...] if name in given else jnp.zeros_like(target)

    @pl.when(among(places))
    def _():
        zero = jnp.zeros((columns, phases), F32)
        above, feedback, chores = {first + k: zero for k in range(CHUNK)}, {}, []
        if "soon" not in given and part != "early":
            above = None
        elif part != "early":
            soon = given["soon"]

            def hold(j, call):
                feedback[j] = call()

            if first and "late" in given:
                past = {n + 1: stack(given["earlier"][n]) for n in range(first)}
                above, calls = carry_terms(soon, given["late"], past, first, first + CHUNK - 1)
            else:
                if not first:
                    above, _ = carry_terms(soon, None, {}, first, first + CHUNK - 1)
                elif "returned" in given:
                    above = {first + k: given["returned"][k] for k in range(CHUNK)}
                calls = [lambda j=j: whole(soon[j, 0:phases]) for j in range(SOON)]
            chores = [functools.partial(hold, j, call) for j, call in enumerate(calls)]
            while part == "late" and chores:
                chores.pop(0)()

        now = {}
        if part == "late":
            for k in range(CHUNK):
                now[edge_level(levels, k), first + 1 + k] = stack(given["edge"][k])
            new_state[...] = given["state"][...]
        elif first:
            for i in range(levels):
                now[i, first] = stack(given["state"][i])
        if part != "late" and "entering" in given:
            for k in range(CHUNK):
                now[-1, first + 1 + k] = stack(given["entering"][k])

        def due(i, k):
            return part == "all" or (i <= edge_level(levels, k)) == (part == "early")

        def emit(i, k, value):
            if k == CHUNK - 1:
                new_state[i] = value
            if leaving is not None and i == (edge_level(levels, k) if part == "early" else levels - 1):
                leaving[k] = value

        wave(first, weight, base, now, above, feedback, due, emit, chores)


def run_chunk(chunk, places, given, part="all", sends=True):
    given = {name: x for name, x in given.items() if x is not None}
    levels, columns, phases = given["base"].shape
    return pl.pallas_call(
        functools.partial(chunk_kernel, chunk, tuple(places), part, tuple(given)),
        out_shape=[resident((levels, columns, phases), F32)] + [resident((CHUNK, columns, phases), F32)] * sends,
        in_specs=[VMEM] * len(given),
        out_specs=[VMEM] * (1 + sends),
        compiler_params=pltpu.CompilerParams(vmem_limit_bytes=16 * 2**20),
        name="chunk",
    )(*[pin(x) for x in given.values()])


def among(places):
    return functools.reduce(jnp.logical_or, [lax.axis_index("lvl") == place for place in places])


def is_open(levels, a, i):
    return i + a < levels


def slot_of(levels, a, i):
    if not is_open(levels, a, i):
        return sum(range(1, a)) + i - (levels - a)
    return sum(levels - n if n < CHUNK else AHEAD - n for n in range(a)) + i


def get_answer(ways, levels, a, i, rows=slice(None)):
    high, low = ways[0:2] if is_open(levels, a, i) else ways[2:4]
    at = slot_of(levels, a, i)
    return high[at, rows], low[at, rows]


def spread_open_kernel(places, weight, base, high, low, kept):
    levels, columns, phases = base.shape
    rows = phases + columns

    def step(at, i, terms, keep=None):
        new = sum(dot_parts((high[x], low[x]), operator(weight, i, k)) for x, k in terms)
        unit, run = new[0:phases], new[phases:rows] + base[i]
        high[at, 0:phases], low[at, 0:phases] = split(unit)
        high[at, phases:rows], low[at, phases:rows] = split(run)
        if keep is not None:
            kept[keep, 0:phases], kept[keep, phases:rows] = unit, run

    @pl.when(among(places))
    def _():
        high[0, 0:phases], low[0, 0:phases] = operator(weight, 0, 0)
        high[0, phases:rows], low[0, phases:rows] = split(base[0])

        units = [(a, i) for a in range(AHEAD) for i in range(levels - a if a < CHUNK else AHEAD - a) if a + i]
        for a, i in sorted(units, key=lambda unit: (unit[1] + 2 * unit[0], unit)):
            terms = []
            if i > 0:
                terms.append((slot_of(levels, a, i - 1), 0))
            if a > 0:
                terms.append((slot_of(levels, a - 1, i + 1), 1))
            step(slot_of(levels, a, i), i, terms, a - SOON if i == 0 and a >= SOON else None)


def spread_close_kernel(
    places, weight, base, soon, open_high, open_low, before, high, low, state, leaving, feed_high, feed_low
):
    levels, columns, phases = base.shape
    rows = phases + columns
    top = levels - 1
    ways = (open_high, open_low, high, low)

    @pl.when(jnp.logical_not(among(places)))
    def _():
        state[...] = before[...]

    @pl.when(among(places))
    def _():
        for j in range(CHUNK - 1):
            feed_high[j], feed_low[j] = split(soon[j, 0:phases])
        units = [(a, i) for a in range(1, CHUNK) for i in range(levels - a, levels)]
        for a, i in sorted(units, key=lambda unit: (unit[1] + 2 * unit[0], unit[1])):
            new = dot_parts(get_answer(ways, levels, a, i - 1), operator(weight, i, 0))
            if i < top:
                over = get_answer(ways, levels, a - 1, i + 1)
            else:
                back = sum(
                    dot_parts(get_answer(ways, levels, a - 1 - j, top), (feed_high[j], feed_low[j])) for j in range(a)
                )
                end = back[phases:rows] + soon[a - 1, phases:rows]
                over = split(jnp.concatenate([back[0:phases], end], axis=0))
            new += dot_parts(over, operator(weight, i, 1))
            at = slot_of(levels, a, i)
            high[at, 0:phases], low[at, 0:phases] = split(new[0:phases])
            high[at, phases:rows], low[at, phases:rows] = split(new[phases:rows] + base[i])

        def run(a, i):
            return sum(part.astype(F32) for part in get_answer(ways, levels, a, i, slice(phases, rows)))

        for i in range(levels):
            state[i] = run(CHUNK - 1, i)
        for a in range(CHUNK):
            leaving[a] = run(a, top)


def spread_open(places, weight, base):
    levels, columns, phases = base.shape
    assert levels > AHEAD and levels >= 2 * CHUNK - 1
    rows = phases + columns
    slots = slot_of(levels, AHEAD, 0)
    *ways, kept = pl.pallas_call(
        functools.partial(spread_open_kernel, tuple(places)),
        out_shape=[resident((slots, rows, phases), BF16)] * 2 + [resident((AHEAD - SOON, rows, phases), F32)],
        in_specs=[VMEM] * 2,
        out_specs=[VMEM] * 3,
        compiler_params=pltpu.CompilerParams(vmem_limit_bytes=16 * 2**20),
        name="spread_open",
    )(*[pin(x) for x in (weight, base)])
    return ways, kept


def spread_close(places, weight, base, soon, ways, state):
    levels, columns, phases = base.shape
    rows = phases + columns
    *more, state, leaving = pl.pallas_call(
        functools.partial(spread_close_kernel, tuple(places)),
        out_shape=[resident((sum(range(CHUNK)), rows, phases), BF16)] * 2
        + [resident((levels, columns, phases), F32), resident((CHUNK, columns, phases), F32)],
        in_specs=[VMEM] * 6,
        out_specs=[VMEM] * 4,
        scratch_shapes=[pltpu.VMEM((CHUNK - 1, phases, phases), BF16)] * 2,
        compiler_params=pltpu.CompilerParams(vmem_limit_bytes=16 * 2**20),
        name="spread_close",
    )(*[pin(x) for x in (weight, base, soon, *ways, state)])
    return [*ways, *more], state, leaving


def finish_leaving_kernel(place, *refs, levels):
    *ways, entering, leaving, before, new = refs
    columns, phases = entering.shape[1:]

    @pl.when(lax.axis_index("lvl") != place)
    def _():
        new[...] = before[...]

    @pl.when(lax.axis_index("lvl") == place)
    def _():
        values = [stack(entering[k]) for k in range(CHUNK)]
        total = [leaving[k] for k in range(CHUNK)]
        for a in range(CHUNK):
            pair = jnp.concatenate(get_answer(ways, levels, a, levels - 1, slice(0, phases)), axis=0)
            for k, term in enumerate(apply_each(values[: CHUNK - a], pair, columns)):
                total[a + k] += term
        for k in range(CHUNK):
            new[k] = total[k]


def finish_leaving(place, ways, entering, leaving, before, levels):
    return pl.pallas_call(
        functools.partial(finish_leaving_kernel, place, levels=levels),
        out_shape=resident(leaving.shape, F32),
        in_specs=[VMEM] * 7,
        out_specs=VMEM,
        compiler_params=pltpu.CompilerParams(vmem_limit_bytes=8 * 2**20),
        name="finish_leaving",
    )(*[pin(x) for x in (*ways, entering, leaving, before)])


def finish_state_kernel(place, *refs):
    *ways, entering, state, new = refs
    levels, _, phases = state.shape

    @pl.when(lax.axis_index("lvl") != place)
    def _():
        new[...] = state[...]

    @pl.when(lax.axis_index("lvl") == place)
    def _():
        values = [stack(entering[CHUNK - 1 - a]) for a in range(CHUNK)]
        for i in range(levels):
            terms = []
            for a in range(CHUNK):
                pair = jnp.concatenate(get_answer(ways, levels, a, i, slice(0, phases)), axis=0)
                terms.append((values[a], pair))
            new[i] = state[i] + apply(terms)


def finish_state(place, ways, entering, state, last):
    return pl.pallas_call(
        functools.partial(finish_state_kernel, place),
        out_shape=(jax.ShapeDtypeStruct if last else resident)(state.shape, F32),
        in_specs=[VMEM] * 6,
        out_specs=VMEM,
        compiler_params=pltpu.CompilerParams(vmem_limit_bytes=8 * 2**20),
        name="finish_state",
    )(*[pin(x) for x in (*ways, entering, state)])


def answer_kernel(step, soon, late, entering, returned):
    @pl.when(lax.axis_index("lvl") == step)
    def _():
        past = {n + 1: stack(entering[n]) for n in range(CHUNK)}
        above = carried(soon, late, past, CHUNK, 2 * CHUNK - 1)
        for k in range(CHUNK):
            returned[k] = above[CHUNK + k]


def answer(step, soon, late, entering):
    return pl.pallas_call(
        functools.partial(answer_kernel, step),
        out_shape=resident(entering.shape, F32),
        in_specs=[VMEM] * 3,
        out_specs=VMEM,
        compiler_params=pltpu.CompilerParams(vmem_limit_bytes=8 * 2**20),
        name="answer",
    )(*[pin(x) for x in (soon, late, entering)])


def local(inverse_diag, down_block, up_block, reward):
    given = reward.shape[1]
    columns = -(-given // 16) * 16
    if columns != given:
        reward = jnp.pad(reward, ((0, 0), (0, columns - given), (0, 0)))
    count = lax.axis_size("lvl")
    assert CHUNKS == 2 and count > 1
    top = count - 1
    ready = [d for d in range(1, count) if d % 2 == 0 or d == top]
    odd = [d for d in range(1, top, 2)]
    weights, begun, soon_here = prepare(inverse_diag, down_block, up_block, reward)
    weight, base = weights
    late_odd = respond(odd, weights, begun) if odd else None
    ways, late_here = spread_open(ready, weight, base)
    soon_odd = lax.ppermute(soon_here, "lvl", [(d + 1, d) for d in range(1, top, 2)])
    soon = lax.ppermute(soon_here, "lvl", [(d + 1, d) for d in range(0, top, 2)])
    late = lax.ppermute(late_odd, "lvl", [(d, d - 1) for d in odd]) if odd else None
    soon, late_here, late_odd = lax.optimization_barrier((soon, late_here, late_odd))
    late_top = None
    own = {"weight": weight, "base": base, "soon": soon}
    state = leaving = entering = parted = None
    for step in range(count + 1):
        place = step - 1
        earlier = leaving
        returned = edge = None
        if step % 2 == 0 and 0 < step < count:
            returned = lax.ppermute(answer(step, soon_here, late_here, entering), "lvl", [(step, place)])
            given_early = {"weight": weight, "base": base, "entering": entering, "state": state}
            state, edge = run_chunk(1, [place], given_early, "early")
        if place in ready and place < top:
            leaving = finish_leaving(place, ways, entering, parted, leaving, base.shape[0])
        if step in ready:
            if step < top:
                leaving = finish_leaving(step, ways, entering, parted_first, leaving, base.shape[0])
        elif step < count:
            state, leaving = run_chunk(
                0, [step], {**own, "soon": soon_odd if step % 2 else soon, "entering": entering, "state": state, "leaving": leaving}
            )
        if step == 1:
            top_sent, leaving = lax.optimization_barrier((late_here, leaving))
            late_top = lax.ppermute(top_sent, "lvl", [(top, top - 1)]) if top % 2 else None
            first_late = late if odd else late_top
            given_first = {**own, "late": first_late, "earlier": earlier, "state": state, "leaving": leaving}
            state, leaving = run_chunk(1, [0], given_first)
        if step in ready and step > 1:
            state = finish_state(step, ways, entering, state, False)
        if returned is not None:
            given_rest = {**own, "soon": soon_odd, "returned": returned, "edge": edge, "state": state, "leaving": leaving}
            state, leaving = run_chunk(1, [place], given_rest, "late")
        came = entering
        if step < count:
            pairs = [(d, d + 1) for d in (place, step) if 0 <= d < top]
            entering = lax.ppermute(leaving, "lvl", pairs) if pairs else None
        if step == 1:
            ways_then, leaving = lax.optimization_barrier((ways, leaving))
            ways, state, parted_first = spread_close(ready, weight, base, soon, ways_then, state)
            if entering is not None:
                entering, state = lax.optimization_barrier((entering, state))
        if place in ready:
            state = finish_state(place, ways, came, state, step == count)
        if step in ready:
            if step == 1:
                state = finish_state(step, ways, came, state, False)
            if step == top:
                (state,) = run_chunk(1, [step], {"weight": weight, "base": base, "state": state}, sends=False)
            else:
                extra = {"late": late_top if step == top - 1 else late, "earlier": leaving}
                state, parted = run_chunk(1, [step], {**own, **extra, "state": state})
    return state[:, :given] if columns != given else state


def solution(mesh):
    placed = (
        P(("grp", "lvl"), None, None),
        P(("grp", "lvl"), None, None),
        P(("grp", "lvl"), None, None),
        P(("grp", "lvl"), "col", None),
    )
    return jax.shard_map(
        local, mesh=mesh, in_specs=placed, out_specs=P(("grp", "lvl"), "col", None), check_vma=False
    )
```

```python
import functools

import jax
import jax.numpy as jnp
from jax import lax
from jax.experimental import pallas as pl
from jax.experimental.pallas import tpu as pltpu
from jax.sharding import PartitionSpec as P

SWEEPS = 8
CHUNK = 4
CHUNKS = SWEEPS // CHUNK
AHEAD = SWEEPS - 1
SOON = CHUNK - 1
F32 = jnp.float32
BF16 = jnp.bfloat16


def resident(shape, dtype):
    return pltpu.VMEM(shape, dtype)


def pin(x, memory=pltpu.VMEM):
    return pltpu.with_memory_space_constraint(x, memory)


def split(x):
    high = x.astype(BF16)
    return high, (x - high.astype(F32)).astype(BF16)


def dot(a, b):
    return jnp.dot(a, b, preferred_element_type=F32)


def dot_nt(a, b):
    return lax.dot_general(a, b, (((1,), (1,)), ((), ())), preferred_element_type=F32)


def dot_parts(a, b, dot=dot):
    return dot(a[0], b[0]) + (dot(a[0], b[1]) + dot(a[1], b[0]))


def place_operator(weight, i, k, value):
    phases = value.shape[0]
    for n, part in enumerate(split(value.T)):
        weight[i, (2 * k + n) * phases : (2 * k + n + 1) * phases] = part


def operator(weight, i, k):
    phases = weight.shape[2]
    at = 2 * k * phases
    return weight[i, at : at + phases], weight[i, at + phases : at + 2 * phases]


def response(first, last, x_high, x_low, weight, base, kept, before=None):
    _, columns, phases = base.shape
    rows = phases + columns

    def store(i, new):
        top = new[0:phases]
        end = new[phases:rows] + base[i]
        x_high[i, 0:phases], x_low[i, 0:phases] = split(top)
        x_high[i, phases:rows], x_low[i, phases:rows] = split(end)
        return top, end

    def from_below(i):
        return dot_parts((x_high[i - 1], x_low[i - 1]), operator(weight, i, 0))

    def from_above(i):
        return dot_parts((x_high[i + 1], x_low[i + 1]), operator(weight, i, 1))

    if first == 0:
        high, low = operator(weight, 0, 0)
        x_high[0, 0:phases], x_low[0, 0:phases] = high, low
        x_high[0, phases:rows], x_low[0, phases:rows] = split(base[0])
        kept[0, 0:phases] = high.astype(F32) + low.astype(F32)
        kept[0, phases:rows] = base[0]
    units = [(a, d - a) for d in range(max(first, 1), last) for a in range(d + 1)]
    for a, i in sorted(units, key=lambda unit: (unit[1] + 2 * unit[0], unit)):
        if before is not None:
            before(a, i)
        if a == 0:
            store(i, from_below(i))
        elif i > 0:
            store(i, from_below(i) + from_above(i))
        else:
            kept[a - first, 0:phases], kept[a - first, phases:rows] = store(0, from_above(0))


def products(wanted, weight, base, inv, down, up, pay):
    for i in wanted:
        here = split(inv[i])
        for k, block in ((0, down), (1, up)):
            if k in wanted[i]:
                place_operator(weight, i, k, dot_parts(here, split(block[i])))
        if 2 in wanted[i]:
            base[i] = dot_parts(split(pay[i]), here, dot_nt)


def prepare_kernel(inv_far, down_far, up_far, pay_far, weight, base, x_high, x_low, kept, inv, down, up, pay, sems):
    levels = pay.shape[0]
    cuts = ((0, 1), (1, SOON), (SOON, levels))

    def copies(part):
        at, end = cuts[part]
        pairs = [(inv_far, inv), (down_far, down), (up_far, up)]
        found = [
            pltpu.make_async_copy(far.at[at:end], near.at[at:end], sems.at[n, part])
            for n, (far, near) in enumerate(pairs)
        ]
        return found + ([pltpu.make_async_copy(pay_far, pay, sems.at[3, 0])] if part == 0 else [])

    def wait(i):
        for part, (at, _) in enumerate(cuts):
            if i == at:
                for copy in copies(part):
                    copy.wait()

    for part in range(len(cuts)):
        for copy in copies(part):
            copy.start()
    need = functools.partial(products, weight=weight, base=base, inv=inv, down=down, up=up, pay=pay)
    wait(0)
    need({0: (0, 1, 2)})
    ahead = {(0, 1): {1: (0, 2)}, (0, 2): {2: (0, 2)}, (1, 0): {1: (1,)}}
    assert SOON == 3

    def before(a, i):
        if (a, i) == (0, 1):
            wait(1)
        need(ahead.get((a, i), {}))

    response(0, SOON, x_high, x_low, weight, base, kept, before)
    wait(SOON)


def prepare_rest_kernel(weight_soon, base_soon, inv, down, up, pay, weight, base):
    levels, _, phases = pay.shape
    for i in range(SOON):
        rows = (4 if i < SOON - 1 else 2) * phases
        weight[i, 0:rows] = weight_soon[i, 0:rows]
    base[0:SOON] = base_soon[...]
    wanted = {i: (0, 1, 2) if i >= SOON else (1,) for i in range(SOON - 1, levels)}
    products(wanted, weight, base, inv, down, up, pay)


def respond_kernel(places, weight, base, x_high_soon, x_low_soon, kept, x_high, x_low):
    @pl.when(among(places))
    def _():
        x_high[0:SOON] = x_high_soon[...]
        x_low[0:SOON] = x_low_soon[...]
        response(SOON, AHEAD, x_high, x_low, weight, base, kept)


VMEM = pl.BlockSpec(memory_space=pltpu.VMEM)
HBM = pl.BlockSpec(memory_space=pltpu.HBM)


def operators(levels, columns, phases):
    return [resident((levels, 4 * phases, phases), BF16), resident((levels, columns, phases), F32)]


def prepare(inverse_diag, down_block, up_block, reward):
    levels, columns, phases = reward.shape
    rows = phases + columns
    matrix = resident((levels, phases, phases), F32)
    *soon, x_high, x_low, kept_soon, inv, down, up, pay = pl.pallas_call(
        prepare_kernel,
        out_shape=operators(SOON, columns, phases)
        + [resident((SOON, rows, phases), BF16)] * 2
        + [resident((SOON, rows, phases), F32)]
        + [matrix] * 3
        + [resident((levels, columns, phases), F32)],
        in_specs=[HBM] * 4,
        out_specs=[VMEM] * 9,
        scratch_shapes=[pltpu.SemaphoreType.DMA((4, 3))],
        compiler_params=pltpu.CompilerParams(vmem_limit_bytes=16 * 2**20),
        name="prepare",
    )(*[pin(x, pltpu.HBM) for x in (inverse_diag, down_block, up_block, reward)])
    weights = pl.pallas_call(
        prepare_rest_kernel,
        out_shape=operators(levels, columns, phases),
        in_specs=[VMEM] * 6,
        out_specs=[VMEM] * 2,
        compiler_params=pltpu.CompilerParams(vmem_limit_bytes=16 * 2**20),
        name="prepare_rest",
    )(*[pin(x) for x in (*soon, inv, down, up, pay)])
    return weights, (x_high, x_low), kept_soon


def respond(places, weights, started):
    _, rows, phases = started[0].shape
    return pl.pallas_call(
        functools.partial(respond_kernel, tuple(places)),
        out_shape=resident((AHEAD - SOON, rows, phases), F32),
        in_specs=[VMEM] * 4,
        out_specs=VMEM,
        scratch_shapes=[pltpu.VMEM((AHEAD, rows, phases), BF16)] * 2,
        compiler_params=pltpu.CompilerParams(vmem_limit_bytes=16 * 2**20),
        name="respond",
    )(*[pin(x) for x in (*weights, *started)])


def stack(x):
    high = x.astype(BF16).astype(F32)
    return jnp.concatenate([high, x - high], axis=0).astype(BF16)


def fold(total):
    half = total.shape[0] // 2
    return total[:half] + total[half:]


def apply(terms):
    values = jnp.concatenate([x for x, _ in terms for _ in range(2)], axis=1)
    return fold(dot(values, jnp.concatenate([operator for _, operator in terms], axis=0)))


def apply_each(values, operator, columns):
    phases = operator.shape[1]
    values = jnp.concatenate(values, axis=0) if len(values) > 1 else values[0]
    total = dot(values, operator[0:phases]) + dot(values, operator[phases:])
    return [fold(total[at : at + 2 * columns]) for at in range(0, total.shape[0], 2 * columns)]


def whole(operator):
    return jnp.concatenate(split(operator), axis=0)


def kept_at(soon, late, j):
    return soon[j] if j < SOON else late[j - SOON]


def carry_terms(soon, late, past, first, last):
    phases = soon.shape[2]
    columns = soon.shape[1] - phases
    above = {n: kept_at(soon, late, n - 1)[phases:] for n in range(max(first, 1), last + 1)}

    def add(j):
        pairs = [(n, n - j) for n in above if n - j in past]
        held = whole(kept_at(soon, late, j)[0:phases])
        for (n, _), term in zip(pairs, apply_each([past[m] for _, m in pairs], held, columns)):
            above[n] += term
        return held

    return above, [functools.partial(add, j) for j in range(last)]


def carried(soon, late, past, first, last):
    above, calls = carry_terms(soon, late, past, first, last)
    for call in calls:
        call()
    return above


def wave(first, weight, base, now, above, feedback, due, emit, chores):
    levels, _, phases = base.shape
    for turn in range(levels + 2 * (CHUNK - 1)):
        for k in range(CHUNK):
            i = turn - 2 * k
            if not (0 <= i < levels and due(i, k)):
                continue
            n = first + 1 + k
            terms = []
            if (i - 1, n) in now:
                terms.append((now[i - 1, n], weight[i, 0 : 2 * phases]))
            if n > 1 and not (i == levels - 1 and above is None):
                over = stack(above[n - 1]) if i == levels - 1 else now[i + 1, n - 1]
                terms.append((over, weight[i, 2 * phases : 4 * phases]))
            value = base[i] + apply(terms) if terms else base[i]
            now[i, n] = stack(value)
            emit(i, k, value)
            if i == levels - 1 and above is not None:
                for later in range(n, first + CHUNK):
                    above[later] += apply([(now[i, n], feedback[later - n])])
        if chores and levels - 2 - turn < len(chores):
            chores.pop(0)()


def edge_level(levels, k):
    return levels - 2 - k


def chunk_kernel(chunk, places, part, names, *refs):
    given = dict(zip(names, refs))
    new_state, *leaving = refs[len(names) :]
    leaving = leaving[0] if leaving else None
    weight, base = given["weight"], given["base"]
    levels, columns, phases = base.shape
    first = chunk * CHUNK

    @pl.when(jnp.logical_not(among(places)))
    def _():
        for name, target in (("state", new_state), ("leaving", leaving)):
            if target is not None:
                target[...] = given[name][...] if name in given else jnp.zeros_like(target)

    @pl.when(among(places))
    def _():
        zero = jnp.zeros((columns, phases), F32)
        above, feedback, chores = {first + k: zero for k in range(CHUNK)}, {}, []
        if "soon" not in given and part != "early":
            above = None
        elif part != "early":
            soon = given["soon"]

            def hold(j, call):
                feedback[j] = call()

            if first and "late" in given:
                past = {n + 1: stack(given["earlier"][n]) for n in range(first)}
                above, calls = carry_terms(soon, given["late"], past, first, first + CHUNK - 1)
            else:
                if not first:
                    above, _ = carry_terms(soon, None, {}, first, first + CHUNK - 1)
                elif "returned" in given:
                    above = {first + k: given["returned"][k] for k in range(CHUNK)}
                calls = [lambda j=j: whole(soon[j, 0:phases]) for j in range(SOON)]
            chores = [functools.partial(hold, j, call) for j, call in enumerate(calls)]
            while part == "late" and chores:
                chores.pop(0)()

        now = {}
        if part == "late":
            for k in range(CHUNK):
                now[edge_level(levels, k), first + 1 + k] = stack(given["edge"][k])
            new_state[...] = given["state"][...]
        elif first:
            for i in range(levels):
                now[i, first] = stack(given["state"][i])
        if part != "late" and "entering" in given:
            for k in range(CHUNK):
                now[-1, first + 1 + k] = stack(given["entering"][k])

        def due(i, k):
            return part == "all" or (i <= edge_level(levels, k)) == (part == "early")

        def emit(i, k, value):
            if k == CHUNK - 1:
                new_state[i] = value
            if leaving is not None and i == (edge_level(levels, k) if part == "early" else levels - 1):
                leaving[k] = value

        wave(first, weight, base, now, above, feedback, due, emit, chores)


def run_chunk(chunk, places, given, part="all", sends=True):
    given = {name: x for name, x in given.items() if x is not None}
    levels, columns, phases = given["base"].shape
    return pl.pallas_call(
        functools.partial(chunk_kernel, chunk, tuple(places), part, tuple(given)),
        out_shape=[resident((levels, columns, phases), F32)] + [resident((CHUNK, columns, phases), F32)] * sends,
        in_specs=[VMEM] * len(given),
        out_specs=[VMEM] * (1 + sends),
        compiler_params=pltpu.CompilerParams(vmem_limit_bytes=16 * 2**20),
        name="chunk",
    )(*[pin(x) for x in given.values()])


def among(places):
    return functools.reduce(jnp.logical_or, [lax.axis_index("lvl") == place for place in places])


def is_open(levels, a, i):
    return i + a < levels


def slot_of(levels, a, i):
    if not is_open(levels, a, i):
        return sum(range(1, a)) + i - (levels - a)
    return sum(levels - n if n < CHUNK else AHEAD - n for n in range(a)) + i


def get_answer(ways, levels, a, i, rows=slice(None)):
    high, low = ways[0:2] if is_open(levels, a, i) else ways[2:4]
    at = slot_of(levels, a, i)
    return high[at, rows], low[at, rows]


def spread_open_kernel(places, weight, base, high, low, kept):
    levels, columns, phases = base.shape
    rows = phases + columns

    def step(at, i, terms, keep=None):
        new = sum(dot_parts((high[x], low[x]), operator(weight, i, k)) for x, k in terms)
        unit, run = new[0:phases], new[phases:rows] + base[i]
        high[at, 0:phases], low[at, 0:phases] = split(unit)
        high[at, phases:rows], low[at, phases:rows] = split(run)
        if keep is not None:
            kept[keep, 0:phases], kept[keep, phases:rows] = unit, run

    @pl.when(among(places))
    def _():
        high[0, 0:phases], low[0, 0:phases] = operator(weight, 0, 0)
        high[0, phases:rows], low[0, phases:rows] = split(base[0])

        units = [(a, i) for a in range(AHEAD) for i in range(levels - a if a < CHUNK else AHEAD - a) if a + i]
        for a, i in sorted(units, key=lambda unit: (unit[1] + 2 * unit[0], unit)):
            terms = []
            if i > 0:
                terms.append((slot_of(levels, a, i - 1), 0))
            if a > 0:
                terms.append((slot_of(levels, a - 1, i + 1), 1))
            step(slot_of(levels, a, i), i, terms, a - SOON if i == 0 and a >= SOON else None)


def spread_close_kernel(
    places, weight, base, soon, open_high, open_low, before, high, low, state, leaving, feed_high, feed_low
):
    levels, columns, phases = base.shape
    rows = phases + columns
    top = levels - 1
    ways = (open_high, open_low, high, low)

    @pl.when(jnp.logical_not(among(places)))
    def _():
        state[...] = before[...]

    @pl.when(among(places))
    def _():
        for j in range(CHUNK - 1):
            feed_high[j], feed_low[j] = split(soon[j, 0:phases])
        units = [(a, i) for a in range(1, CHUNK) for i in range(levels - a, levels)]
        for a, i in sorted(units, key=lambda unit: (unit[1] + 2 * unit[0], unit[1])):
            new = dot_parts(get_answer(ways, levels, a, i - 1), operator(weight, i, 0))
            if i < top:
                over = get_answer(ways, levels, a - 1, i + 1)
            else:
                back = sum(
                    dot_parts(get_answer(ways, levels, a - 1 - j, top), (feed_high[j], feed_low[j])) for j in range(a)
                )
                end = back[phases:rows] + soon[a - 1, phases:rows]
                over = split(jnp.concatenate([back[0:phases], end], axis=0))
            new += dot_parts(over, operator(weight, i, 1))
            at = slot_of(levels, a, i)
            high[at, 0:phases], low[at, 0:phases] = split(new[0:phases])
            high[at, phases:rows], low[at, phases:rows] = split(new[phases:rows] + base[i])

        def run(a, i):
            return sum(part.astype(F32) for part in get_answer(ways, levels, a, i, slice(phases, rows)))

        for i in range(levels):
            state[i] = run(CHUNK - 1, i)
        for a in range(CHUNK):
            leaving[a] = run(a, top)


def spread_open(places, weight, base):
    levels, columns, phases = base.shape
    assert levels > AHEAD and levels >= 2 * CHUNK - 1
    rows = phases + columns
    slots = slot_of(levels, AHEAD, 0)
    *ways, kept = pl.pallas_call(
        functools.partial(spread_open_kernel, tuple(places)),
        out_shape=[resident((slots, rows, phases), BF16)] * 2 + [resident((AHEAD - SOON, rows, phases), F32)],
        in_specs=[VMEM] * 2,
        out_specs=[VMEM] * 3,
        compiler_params=pltpu.CompilerParams(vmem_limit_bytes=16 * 2**20),
        name="spread_open",
    )(*[pin(x) for x in (weight, base)])
    return ways, kept


def spread_close(places, weight, base, soon, ways, state):
    levels, columns, phases = base.shape
    rows = phases + columns
    *more, state, leaving = pl.pallas_call(
        functools.partial(spread_close_kernel, tuple(places)),
        out_shape=[resident((sum(range(CHUNK)), rows, phases), BF16)] * 2
        + [resident((levels, columns, phases), F32), resident((CHUNK, columns, phases), F32)],
        in_specs=[VMEM] * 6,
        out_specs=[VMEM] * 4,
        scratch_shapes=[pltpu.VMEM((CHUNK - 1, phases, phases), BF16)] * 2,
        compiler_params=pltpu.CompilerParams(vmem_limit_bytes=16 * 2**20),
        name="spread_close",
    )(*[pin(x) for x in (weight, base, soon, *ways, state)])
    return [*ways, *more], state, leaving


def finish_leaving_kernel(place, *refs, levels):
    *ways, entering, leaving, before, new = refs
    columns, phases = entering.shape[1:]

    @pl.when(lax.axis_index("lvl") != place)
    def _():
        new[...] = before[...]

    @pl.when(lax.axis_index("lvl") == place)
    def _():
        values = [stack(entering[k]) for k in range(CHUNK)]
        total = [leaving[k] for k in range(CHUNK)]
        for a in range(CHUNK):
            pair = jnp.concatenate(get_answer(ways, levels, a, levels - 1, slice(0, phases)), axis=0)
            for k, term in enumerate(apply_each(values[: CHUNK - a], pair, columns)):
                total[a + k] += term
        for k in range(CHUNK):
            new[k] = total[k]


def finish_leaving(place, ways, entering, leaving, before, levels):
    return pl.pallas_call(
        functools.partial(finish_leaving_kernel, place, levels=levels),
        out_shape=resident(leaving.shape, F32),
        in_specs=[VMEM] * 7,
        out_specs=VMEM,
        compiler_params=pltpu.CompilerParams(vmem_limit_bytes=8 * 2**20),
        name="finish_leaving",
    )(*[pin(x) for x in (*ways, entering, leaving, before)])


def finish_state_kernel(place, *refs):
    *ways, entering, state, new = refs
    levels, _, phases = state.shape

    @pl.when(lax.axis_index("lvl") != place)
    def _():
        new[...] = state[...]

    @pl.when(lax.axis_index("lvl") == place)
    def _():
        values = [stack(entering[CHUNK - 1 - a]) for a in range(CHUNK)]
        for i in range(levels):
            terms = []
            for a in range(CHUNK):
                pair = jnp.concatenate(get_answer(ways, levels, a, i, slice(0, phases)), axis=0)
                terms.append((values[a], pair))
            new[i] = state[i] + apply(terms)


def finish_state(place, ways, entering, state, last):
    return pl.pallas_call(
        functools.partial(finish_state_kernel, place),
        out_shape=(jax.ShapeDtypeStruct if last else resident)(state.shape, F32),
        in_specs=[VMEM] * 6,
        out_specs=VMEM,
        compiler_params=pltpu.CompilerParams(vmem_limit_bytes=8 * 2**20),
        name="finish_state",
    )(*[pin(x) for x in (*ways, entering, state)])


def answer_kernel(step, soon, late, entering, returned):
    @pl.when(lax.axis_index("lvl") == step)
    def _():
        past = {n + 1: stack(entering[n]) for n in range(CHUNK)}
        above = carried(soon, late, past, CHUNK, 2 * CHUNK - 1)
        for k in range(CHUNK):
            returned[k] = above[CHUNK + k]


def answer(step, soon, late, entering):
    return pl.pallas_call(
        functools.partial(answer_kernel, step),
        out_shape=resident(entering.shape, F32),
        in_specs=[VMEM] * 3,
        out_specs=VMEM,
        compiler_params=pltpu.CompilerParams(vmem_limit_bytes=8 * 2**20),
        name="answer",
    )(*[pin(x) for x in (soon, late, entering)])


def local(inverse_diag, down_block, up_block, reward):
    given = reward.shape[1]
    columns = -(-given // 16) * 16
    if columns != given:
        reward = jnp.pad(reward, ((0, 0), (0, columns - given), (0, 0)))
    count = lax.axis_size("lvl")
    assert CHUNKS == 2 and count > 1
    top = count - 1
    ready = [d for d in range(1, count) if d % 2 == 0 or d == top]
    odd = [d for d in range(1, top, 2)]
    weights, begun, soon_here = prepare(inverse_diag, down_block, up_block, reward)
    weight, base = weights
    late_odd = respond(odd, weights, begun) if odd else None
    ways, late_here = spread_open(ready, weight, base)
    soon_odd = lax.ppermute(soon_here, "lvl", [(d + 1, d) for d in range(1, top, 2)])
    soon = lax.ppermute(soon_here, "lvl", [(d + 1, d) for d in range(0, top, 2)])
    late = lax.ppermute(late_odd, "lvl", [(d, d - 1) for d in odd]) if odd else None
    soon, late_here, late_odd = lax.optimization_barrier((soon, late_here, late_odd))
    late_top = None
    own = {"weight": weight, "base": base, "soon": soon}
    state = leaving = entering = parted = None
    for step in range(count + 1):
        place = step - 1
        earlier = leaving
        returned = edge = None
        if step % 2 == 0 and 0 < step < count:
            returned = lax.ppermute(answer(step, soon_here, late_here, entering), "lvl", [(step, place)])
            given_early = {"weight": weight, "base": base, "entering": entering, "state": state}
            state, edge = run_chunk(1, [place], given_early, "early")
        if place in ready and place < top:
            leaving = finish_leaving(place, ways, entering, parted, leaving, base.shape[0])
        if step in ready:
            if step < top:
                leaving = finish_leaving(step, ways, entering, parted_first, leaving, base.shape[0])
        elif step < count:
            state, leaving = run_chunk(
                0, [step], {**own, "soon": soon_odd if step % 2 else soon, "entering": entering, "state": state, "leaving": leaving}
            )
        if step == 1:
            top_sent, leaving = lax.optimization_barrier((late_here, leaving))
            late_top = lax.ppermute(top_sent, "lvl", [(top, top - 1)]) if top % 2 else None
            first_late = late if odd else late_top
            given_first = {**own, "late": first_late, "earlier": earlier, "state": state, "leaving": leaving}
            state, leaving = run_chunk(1, [0], given_first)
        if step in ready and step > 1:
            state = finish_state(step, ways, entering, state, False)
        if returned is not None:
            given_rest = {**own, "soon": soon_odd, "returned": returned, "edge": edge, "state": state, "leaving": leaving}
            state, leaving = run_chunk(1, [place], given_rest, "late")
        came = entering
        if step < count:
            pairs = [(d, d + 1) for d in (place, step) if 0 <= d < top]
            entering = lax.ppermute(leaving, "lvl", pairs) if pairs else None
        if step == 1:
            ways_then, leaving = lax.optimization_barrier((ways, leaving))
            ways, state, parted_first = spread_close(ready, weight, base, soon, ways_then, state)
            if entering is not None:
                entering, state = lax.optimization_barrier((entering, state))
        if place in ready:
            state = finish_state(place, ways, came, state, step == count)
        if step in ready:
            if step == 1:
                state = finish_state(step, ways, came, state, False)
            if step == top:
                (state,) = run_chunk(1, [step], {"weight": weight, "base": base, "state": state}, sends=False)
            else:
                extra = {"late": late_top if step == top - 1 else late, "earlier": leaving}
                state, parted = run_chunk(1, [step], {**own, **extra, "state": state})
    return state[:, :given] if columns != given else state


def solution(mesh):
    placed = (
        P(("grp", "lvl"), None, None),
        P(("grp", "lvl"), None, None),
        P(("grp", "lvl"), None, None),
        P(("grp", "lvl"), "col", None),
    )
    return jax.shard_map(
        local, mesh=mesh, in_specs=placed, out_specs=P(("grp", "lvl"), "col", None), check_vma=False
    )
```

```python
import functools

import jax
import jax.numpy as jnp
from jax import lax
from jax.experimental import pallas as pl
from jax.experimental.pallas import tpu as pltpu
from jax.sharding import PartitionSpec as P

SWEEPS = 8
CHUNK = 4
CHUNKS = SWEEPS // CHUNK
AHEAD = SWEEPS - 1
SOON = CHUNK - 1
F32 = jnp.float32
BF16 = jnp.bfloat16


def resident(shape, dtype):
    return pltpu.VMEM(shape, dtype)


def pin(x, memory=pltpu.VMEM):
    return pltpu.with_memory_space_constraint(x, memory)


def split(x):
    high = x.astype(BF16)
    return high, (x - high.astype(F32)).astype(BF16)


def dot(a, b):
    return jnp.dot(a, b, preferred_element_type=F32)


def dot_nt(a, b):
    return lax.dot_general(a, b, (((1,), (1,)), ((), ())), preferred_element_type=F32)


def dot_parts(a, b, dot=dot):
    return dot(a[0], b[0]) + (dot(a[0], b[1]) + dot(a[1], b[0]))


def place_operator(weight, i, k, value):
    phases = value.shape[0]
    for n, part in enumerate(split(value.T)):
        weight[i, (2 * k + n) * phases : (2 * k + n + 1) * phases] = part


def operator(weight, i, k):
    phases = weight.shape[2]
    at = 2 * k * phases
    return weight[i, at : at + phases], weight[i, at + phases : at + 2 * phases]


def response(first, last, x_high, x_low, weight, base, kept):
    _, columns, phases = base.shape
    rows = phases + columns

    def store(i, new):
        top = new[0:phases]
        end = new[phases:rows] + base[i]
        x_high[i, 0:phases], x_low[i, 0:phases] = split(top)
        x_high[i, phases:rows], x_low[i, phases:rows] = split(end)
        return top, end

    def from_below(i):
        return dot_parts((x_high[i - 1], x_low[i - 1]), operator(weight, i, 0))

    def from_above(i):
        return dot_parts((x_high[i + 1], x_low[i + 1]), operator(weight, i, 1))

    if first == 0:
        high, low = operator(weight, 0, 0)
        x_high[0, 0:phases], x_low[0, 0:phases] = high, low
        x_high[0, phases:rows], x_low[0, phases:rows] = split(base[0])
        kept[0, 0:phases] = high.astype(F32) + low.astype(F32)
        kept[0, phases:rows] = base[0]
    units = [(a, d - a) for d in range(max(first, 1), last) for a in range(d + 1)]
    for a, i in sorted(units, key=lambda unit: (unit[1] + 2 * unit[0], unit)):
        if a == 0:
            store(i, from_below(i))
        elif i > 0:
            store(i, from_below(i) + from_above(i))
        else:
            kept[a - first, 0:phases], kept[a - first, phases:rows] = store(0, from_above(0))


def products(wanted, here_from, weight, base, inv, down, up, pay):
    for i in wanted:
        here_from(i)
        here = split(inv[i])
        for k, block in ((0, down), (1, up)):
            if k in wanted[i]:
                place_operator(weight, i, k, dot_parts(here, split(block[i])))
        if 2 in wanted[i]:
            base[i] = dot_parts(split(pay[i]), here, dot_nt)


def prepare_kernel(inv_far, down_far, up_far, pay_far, weight, base, x_high, x_low, kept, inv, down, up, pay, sems):
    levels = pay.shape[0]
    cuts = ((0, 1), (1, SOON), (SOON, levels))

    def copies(part):
        at, end = cuts[part]
        pairs = [(inv_far, inv), (down_far, down), (up_far, up)]
        found = [
            pltpu.make_async_copy(far.at[at:end], near.at[at:end], sems.at[n, part])
            for n, (far, near) in enumerate(pairs)
        ]
        return found + ([pltpu.make_async_copy(pay_far, pay, sems.at[3, 0])] if part == 0 else [])

    def wait(i):
        for part, (at, _) in enumerate(cuts):
            if i == at:
                for copy in copies(part):
                    copy.wait()

    for part in range(len(cuts)):
        for copy in copies(part):
            copy.start()
    wanted = {i: (0, 1, 2) if i < SOON - 1 else (0, 2) for i in range(SOON)}
    products(wanted, wait, weight, base, inv, down, up, pay)
    response(0, SOON, x_high, x_low, weight, base, kept)
    wait(SOON)


def prepare_rest_kernel(weight_soon, base_soon, inv, down, up, pay, weight, base):
    levels, _, phases = pay.shape
    for i in range(SOON):
        rows = (4 if i < SOON - 1 else 2) * phases
        weight[i, 0:rows] = weight_soon[i, 0:rows]
    base[0:SOON] = base_soon[...]
    wanted = {i: (0, 1, 2) if i >= SOON else (1,) for i in range(SOON - 1, levels)}
    products(wanted, lambda i: None, weight, base, inv, down, up, pay)


def respond_kernel(places, weight, base, x_high_soon, x_low_soon, kept, x_high, x_low):
    @pl.when(among(places))
    def _():
        x_high[0:SOON] = x_high_soon[...]
        x_low[0:SOON] = x_low_soon[...]
        response(SOON, AHEAD, x_high, x_low, weight, base, kept)


VMEM = pl.BlockSpec(memory_space=pltpu.VMEM)
HBM = pl.BlockSpec(memory_space=pltpu.HBM)


def operators(levels, columns, phases):
    return [resident((levels, 4 * phases, phases), BF16), resident((levels, columns, phases), F32)]


def prepare(inverse_diag, down_block, up_block, reward):
    levels, columns, phases = reward.shape
    rows = phases + columns
    matrix = resident((levels, phases, phases), F32)
    *soon, x_high, x_low, kept_soon, inv, down, up, pay = pl.pallas_call(
        prepare_kernel,
        out_shape=operators(SOON, columns, phases)
        + [resident((SOON, rows, phases), BF16)] * 2
        + [resident((SOON, rows, phases), F32)]
        + [matrix] * 3
        + [resident((levels, columns, phases), F32)],
        in_specs=[HBM] * 4,
        out_specs=[VMEM] * 9,
        scratch_shapes=[pltpu.SemaphoreType.DMA((4, 3))],
        compiler_params=pltpu.CompilerParams(vmem_limit_bytes=16 * 2**20),
        name="prepare",
    )(*[pin(x, pltpu.HBM) for x in (inverse_diag, down_block, up_block, reward)])
    weights = pl.pallas_call(
        prepare_rest_kernel,
        out_shape=operators(levels, columns, phases),
        in_specs=[VMEM] * 6,
        out_specs=[VMEM] * 2,
        compiler_params=pltpu.CompilerParams(vmem_limit_bytes=16 * 2**20),
        name="prepare_rest",
    )(*[pin(x) for x in (*soon, inv, down, up, pay)])
    return weights, (x_high, x_low), kept_soon


def respond(places, weights, started):
    _, rows, phases = started[0].shape
    return pl.pallas_call(
        functools.partial(respond_kernel, tuple(places)),
        out_shape=resident((AHEAD - SOON, rows, phases), F32),
        in_specs=[VMEM] * 4,
        out_specs=VMEM,
        scratch_shapes=[pltpu.VMEM((AHEAD, rows, phases), BF16)] * 2,
        compiler_params=pltpu.CompilerParams(vmem_limit_bytes=16 * 2**20),
        name="respond",
    )(*[pin(x) for x in (*weights, *started)])


def stack(x):
    high = x.astype(BF16).astype(F32)
    return jnp.concatenate([high, x - high], axis=0).astype(BF16)


def fold(total):
    half = total.shape[0] // 2
    return total[:half] + total[half:]


def apply(terms):
    values = jnp.concatenate([x for x, _ in terms for _ in range(2)], axis=1)
    return fold(dot(values, jnp.concatenate([operator for _, operator in terms], axis=0)))


def apply_each(values, operator, columns):
    phases = operator.shape[1]
    values = jnp.concatenate(values, axis=0) if len(values) > 1 else values[0]
    total = dot(values, operator[0:phases]) + dot(values, operator[phases:])
    return [fold(total[at : at + 2 * columns]) for at in range(0, total.shape[0], 2 * columns)]


def whole(operator):
    return jnp.concatenate(split(operator), axis=0)


def kept_at(soon, late, j):
    return soon[j] if j < SOON else late[j - SOON]


def carry_terms(soon, late, past, first, last):
    phases = soon.shape[2]
    columns = soon.shape[1] - phases
    above = {n: kept_at(soon, late, n - 1)[phases:] for n in range(max(first, 1), last + 1)}

    def add(j):
        pairs = [(n, n - j) for n in above if n - j in past]
        held = whole(kept_at(soon, late, j)[0:phases])
        for (n, _), term in zip(pairs, apply_each([past[m] for _, m in pairs], held, columns)):
            above[n] += term
        return held

    return above, [functools.partial(add, j) for j in range(last)]


def carried(soon, late, past, first, last):
    above, calls = carry_terms(soon, late, past, first, last)
    for call in calls:
        call()
    return above


def wave(first, weight, base, now, above, feedback, due, emit, chores):
    levels, _, phases = base.shape
    for turn in range(levels + 2 * (CHUNK - 1)):
        for k in range(CHUNK):
            i = turn - 2 * k
            if not (0 <= i < levels and due(i, k)):
                continue
            n = first + 1 + k
            terms = []
            if (i - 1, n) in now:
                terms.append((now[i - 1, n], weight[i, 0 : 2 * phases]))
            if n > 1 and not (i == levels - 1 and above is None):
                over = stack(above[n - 1]) if i == levels - 1 else now[i + 1, n - 1]
                terms.append((over, weight[i, 2 * phases : 4 * phases]))
            value = base[i] + apply(terms) if terms else base[i]
            now[i, n] = stack(value)
            emit(i, k, value)
            if i == levels - 1 and above is not None:
                for later in range(n, first + CHUNK):
                    above[later] += apply([(now[i, n], feedback[later - n])])
        if chores and levels - 2 - turn < len(chores):
            chores.pop(0)()


def edge_level(levels, k):
    return levels - 2 - k


def chunk_kernel(chunk, places, part, names, *refs):
    given = dict(zip(names, refs))
    new_state, *leaving = refs[len(names) :]
    leaving = leaving[0] if leaving else None
    weight, base = given["weight"], given["base"]
    levels, columns, phases = base.shape
    first = chunk * CHUNK

    @pl.when(jnp.logical_not(among(places)))
    def _():
        for name, target in (("state", new_state), ("leaving", leaving)):
            if target is not None:
                target[...] = given[name][...] if name in given else jnp.zeros_like(target)

    @pl.when(among(places))
    def _():
        zero = jnp.zeros((columns, phases), F32)
        above, feedback, chores = {first + k: zero for k in range(CHUNK)}, {}, []
        if "soon" not in given and part != "early":
            above = None
        elif part != "early":
            soon = given["soon"]

            def hold(j, call):
                feedback[j] = call()

            if first and "late" in given:
                past = {n + 1: stack(given["earlier"][n]) for n in range(first)}
                above, calls = carry_terms(soon, given["late"], past, first, first + CHUNK - 1)
            else:
                if not first:
                    above, _ = carry_terms(soon, None, {}, first, first + CHUNK - 1)
                elif "returned" in given:
                    above = {first + k: given["returned"][k] for k in range(CHUNK)}
                calls = [lambda j=j: whole(soon[j, 0:phases]) for j in range(SOON)]
            chores = [functools.partial(hold, j, call) for j, call in enumerate(calls)]
            while part == "late" and chores:
                chores.pop(0)()

        now = {}
        if part == "late":
            for k in range(CHUNK):
                now[edge_level(levels, k), first + 1 + k] = stack(given["edge"][k])
            new_state[...] = given["state"][...]
        elif first:
            for i in range(levels):
                now[i, first] = stack(given["state"][i])
        if part != "late" and "entering" in given:
            for k in range(CHUNK):
                now[-1, first + 1 + k] = stack(given["entering"][k])

        def due(i, k):
            return part == "all" or (i <= edge_level(levels, k)) == (part == "early")

        def emit(i, k, value):
            if k == CHUNK - 1:
                new_state[i] = value
            if leaving is not None and i == (edge_level(levels, k) if part == "early" else levels - 1):
                leaving[k] = value

        wave(first, weight, base, now, above, feedback, due, emit, chores)


def run_chunk(chunk, places, given, part="all", sends=True):
    given = {name: x for name, x in given.items() if x is not None}
    levels, columns, phases = given["base"].shape
    return pl.pallas_call(
        functools.partial(chunk_kernel, chunk, tuple(places), part, tuple(given)),
        out_shape=[resident((levels, columns, phases), F32)] + [resident((CHUNK, columns, phases), F32)] * sends,
        in_specs=[VMEM] * len(given),
        out_specs=[VMEM] * (1 + sends),
        compiler_params=pltpu.CompilerParams(vmem_limit_bytes=16 * 2**20),
        name="chunk",
    )(*[pin(x) for x in given.values()])


def among(places):
    return functools.reduce(jnp.logical_or, [lax.axis_index("lvl") == place for place in places])


def is_open(levels, a, i):
    return i + a < levels


def slot_of(levels, a, i):
    if not is_open(levels, a, i):
        return sum(range(1, a)) + i - (levels - a)
    return sum(levels - n if n < CHUNK else AHEAD - n for n in range(a)) + i


def get_answer(ways, levels, a, i, rows=slice(None)):
    high, low = ways[0:2] if is_open(levels, a, i) else ways[2:4]
    at = slot_of(levels, a, i)
    return high[at, rows], low[at, rows]


def spread_open_kernel(places, weight, base, high, low, kept):
    levels, columns, phases = base.shape
    rows = phases + columns

    def step(at, i, terms, keep=None):
        new = sum(dot_parts((high[x], low[x]), operator(weight, i, k)) for x, k in terms)
        unit, run = new[0:phases], new[phases:rows] + base[i]
        high[at, 0:phases], low[at, 0:phases] = split(unit)
        high[at, phases:rows], low[at, phases:rows] = split(run)
        if keep is not None:
            kept[keep, 0:phases], kept[keep, phases:rows] = unit, run

    @pl.when(among(places))
    def _():
        high[0, 0:phases], low[0, 0:phases] = operator(weight, 0, 0)
        high[0, phases:rows], low[0, phases:rows] = split(base[0])

        units = [(a, i) for a in range(AHEAD) for i in range(levels - a if a < CHUNK else AHEAD - a) if a + i]
        for a, i in sorted(units, key=lambda unit: (unit[1] + 2 * unit[0], unit)):
            terms = []
            if i > 0:
                terms.append((slot_of(levels, a, i - 1), 0))
            if a > 0:
                terms.append((slot_of(levels, a - 1, i + 1), 1))
            step(slot_of(levels, a, i), i, terms, a - SOON if i == 0 and a >= SOON else None)


def spread_close_kernel(
    places, weight, base, soon, open_high, open_low, before, high, low, state, leaving, feed_high, feed_low
):
    levels, columns, phases = base.shape
    rows = phases + columns
    top = levels - 1
    ways = (open_high, open_low, high, low)

    @pl.when(jnp.logical_not(among(places)))
    def _():
        state[...] = before[...]

    @pl.when(among(places))
    def _():
        for j in range(CHUNK - 1):
            feed_high[j], feed_low[j] = split(soon[j, 0:phases])
        units = [(a, i) for a in range(1, CHUNK) for i in range(levels - a, levels)]
        for a, i in sorted(units, key=lambda unit: (unit[1] + 2 * unit[0], unit[1])):
            new = dot_parts(get_answer(ways, levels, a, i - 1), operator(weight, i, 0))
            if i < top:
                over = get_answer(ways, levels, a - 1, i + 1)
            else:
                back = sum(
                    dot_parts(get_answer(ways, levels, a - 1 - j, top), (feed_high[j], feed_low[j])) for j in range(a)
                )
                end = back[phases:rows] + soon[a - 1, phases:rows]
                over = split(jnp.concatenate([back[0:phases], end], axis=0))
            new += dot_parts(over, operator(weight, i, 1))
            at = slot_of(levels, a, i)
            high[at, 0:phases], low[at, 0:phases] = split(new[0:phases])
            high[at, phases:rows], low[at, phases:rows] = split(new[phases:rows] + base[i])

        def run(a, i):
            return sum(part.astype(F32) for part in get_answer(ways, levels, a, i, slice(phases, rows)))

        for i in range(levels):
            state[i] = run(CHUNK - 1, i)
        for a in range(CHUNK):
            leaving[a] = run(a, top)


def spread_open(places, weight, base):
    levels, columns, phases = base.shape
    assert levels > AHEAD and levels >= 2 * CHUNK - 1
    rows = phases + columns
    slots = slot_of(levels, AHEAD, 0)
    *ways, kept = pl.pallas_call(
        functools.partial(spread_open_kernel, tuple(places)),
        out_shape=[resident((slots, rows, phases), BF16)] * 2 + [resident((AHEAD - SOON, rows, phases), F32)],
        in_specs=[VMEM] * 2,
        out_specs=[VMEM] * 3,
        compiler_params=pltpu.CompilerParams(vmem_limit_bytes=16 * 2**20),
        name="spread_open",
    )(*[pin(x) for x in (weight, base)])
    return ways, kept


def spread_close(places, weight, base, soon, ways, state):
    levels, columns, phases = base.shape
    rows = phases + columns
    *more, state, leaving = pl.pallas_call(
        functools.partial(spread_close_kernel, tuple(places)),
        out_shape=[resident((sum(range(CHUNK)), rows, phases), BF16)] * 2
        + [resident((levels, columns, phases), F32), resident((CHUNK, columns, phases), F32)],
        in_specs=[VMEM] * 6,
        out_specs=[VMEM] * 4,
        scratch_shapes=[pltpu.VMEM((CHUNK - 1, phases, phases), BF16)] * 2,
        compiler_params=pltpu.CompilerParams(vmem_limit_bytes=16 * 2**20),
        name="spread_close",
    )(*[pin(x) for x in (weight, base, soon, *ways, state)])
    return [*ways, *more], state, leaving


def finish_leaving_kernel(place, *refs, levels):
    *ways, entering, leaving, before, new = refs
    columns, phases = entering.shape[1:]

    @pl.when(lax.axis_index("lvl") != place)
    def _():
        new[...] = before[...]

    @pl.when(lax.axis_index("lvl") == place)
    def _():
        values = [stack(entering[k]) for k in range(CHUNK)]
        total = [leaving[k] for k in range(CHUNK)]
        for a in range(CHUNK):
            pair = jnp.concatenate(get_answer(ways, levels, a, levels - 1, slice(0, phases)), axis=0)
            for k, term in enumerate(apply_each(values[: CHUNK - a], pair, columns)):
                total[a + k] += term
        for k in range(CHUNK):
            new[k] = total[k]


def finish_leaving(place, ways, entering, leaving, before, levels):
    return pl.pallas_call(
        functools.partial(finish_leaving_kernel, place, levels=levels),
        out_shape=resident(leaving.shape, F32),
        in_specs=[VMEM] * 7,
        out_specs=VMEM,
        compiler_params=pltpu.CompilerParams(vmem_limit_bytes=8 * 2**20),
        name="finish_leaving",
    )(*[pin(x) for x in (*ways, entering, leaving, before)])


def finish_state_kernel(place, *refs):
    *ways, entering, state, new = refs
    levels, _, phases = state.shape

    @pl.when(lax.axis_index("lvl") != place)
    def _():
        new[...] = state[...]

    @pl.when(lax.axis_index("lvl") == place)
    def _():
        values = [stack(entering[CHUNK - 1 - a]) for a in range(CHUNK)]
        for i in range(levels):
            terms = []
            for a in range(CHUNK):
                pair = jnp.concatenate(get_answer(ways, levels, a, i, slice(0, phases)), axis=0)
                terms.append((values[a], pair))
            new[i] = state[i] + apply(terms)


def finish_state(place, ways, entering, state):
    return pl.pallas_call(
        functools.partial(finish_state_kernel, place),
        out_shape=resident(state.shape, F32),
        in_specs=[VMEM] * 6,
        out_specs=VMEM,
        compiler_params=pltpu.CompilerParams(vmem_limit_bytes=8 * 2**20),
        name="finish_state",
    )(*[pin(x) for x in (*ways, entering, state)])


def finish_last_kernel(place, *refs):
    *ways, entering, state, far, near, sems = refs
    levels, _, phases = state.shape

    @pl.when(lax.axis_index("lvl") != place)
    def _():
        copy = pltpu.make_async_copy(state, far, sems.at[levels])
        copy.start()
        copy.wait()

    @pl.when(lax.axis_index("lvl") == place)
    def _():
        copies = [pltpu.make_async_copy(near.at[i], far.at[i], sems.at[i]) for i in range(levels)]
        values = [stack(entering[CHUNK - 1 - a]) for a in range(CHUNK)]
        for i in range(levels):
            terms = []
            for a in range(CHUNK):
                pair = jnp.concatenate(get_answer(ways, levels, a, i, slice(0, phases)), axis=0)
                terms.append((values[a], pair))
            near[i] = state[i] + apply(terms)
            copies[i].start()
        for copy in copies:
            copy.wait()


def finish_last(place, ways, entering, state):
    return pl.pallas_call(
        functools.partial(finish_last_kernel, place),
        out_shape=jax.ShapeDtypeStruct(state.shape, F32),
        in_specs=[VMEM] * 6,
        out_specs=HBM,
        scratch_shapes=[pltpu.VMEM(state.shape, F32), pltpu.SemaphoreType.DMA((state.shape[0] + 1,))],
        compiler_params=pltpu.CompilerParams(vmem_limit_bytes=8 * 2**20),
        name="finish_last",
    )(*[pin(x) for x in (*ways, entering, state)])


def answer_kernel(step, soon, late, entering, returned):
    @pl.when(lax.axis_index("lvl") == step)
    def _():
        past = {n + 1: stack(entering[n]) for n in range(CHUNK)}
        above = carried(soon, late, past, CHUNK, 2 * CHUNK - 1)
        for k in range(CHUNK):
            returned[k] = above[CHUNK + k]


def answer(step, soon, late, entering):
    return pl.pallas_call(
        functools.partial(answer_kernel, step),
        out_shape=resident(entering.shape, F32),
        in_specs=[VMEM] * 3,
        out_specs=VMEM,
        compiler_params=pltpu.CompilerParams(vmem_limit_bytes=8 * 2**20),
        name="answer",
    )(*[pin(x) for x in (soon, late, entering)])


def local(inverse_diag, down_block, up_block, reward):
    given = reward.shape[1]
    columns = -(-given // 16) * 16
    if columns != given:
        reward = jnp.pad(reward, ((0, 0), (0, columns - given), (0, 0)))
    count = lax.axis_size("lvl")
    assert CHUNKS == 2 and count > 1
    top = count - 1
    ready = [d for d in range(1, count) if d % 2 == 0 or d == top]
    odd = [d for d in range(1, top, 2)]
    weights, begun, soon_here = prepare(inverse_diag, down_block, up_block, reward)
    weight, base = weights
    late_odd = respond(odd, weights, begun) if odd else None
    ways, late_here = spread_open(ready, weight, base)
    soon = lax.ppermute(soon_here, "lvl", [(1, 0)])
    soon_far = lax.ppermute(soon_here, "lvl", [(d + 1, d) for d in range(1, top)]) if top > 1 else soon
    late = lax.ppermute(late_odd, "lvl", [(d, d - 1) for d in odd]) if odd else None
    soon, late_here, late_odd = lax.optimization_barrier((soon, late_here, late_odd))
    late_top = None
    own = {"weight": weight, "base": base, "soon": soon}
    state = leaving = entering = parted = None
    for step in range(count + 1):
        place = step - 1
        earlier = leaving
        returned = edge = None
        if step % 2 == 0 and 0 < step < count:
            returned = lax.ppermute(answer(step, soon_here, late_here, entering), "lvl", [(step, place)])
            given_early = {"weight": weight, "base": base, "entering": entering, "state": state}
            state, edge = run_chunk(1, [place], given_early, "early")
        if place in ready and place < top:
            leaving = finish_leaving(place, ways, entering, parted, leaving, base.shape[0])
        if step in ready:
            if step < top:
                leaving = finish_leaving(step, ways, entering, parted_first, leaving, base.shape[0])
        elif step < count:
            state, leaving = run_chunk(
                0, [step], {**own, "soon": soon_far if step else soon, "entering": entering, "state": state, "leaving": leaving}
            )
        if step == 1:
            top_sent, leaving = lax.optimization_barrier((late_here, leaving))
            late_top = lax.ppermute(top_sent, "lvl", [(top, top - 1)]) if top % 2 else None
            first_late = late if odd else late_top
            given_first = {**own, "late": first_late, "earlier": earlier, "state": state, "leaving": leaving}
            state, leaving = run_chunk(1, [0], given_first)
        if step in ready and step > 1:
            state = finish_state(step, ways, entering, state)
        if returned is not None:
            given_rest = {**own, "soon": soon_far, "returned": returned, "edge": edge, "state": state, "leaving": leaving}
            state, leaving = run_chunk(1, [place], given_rest, "late")
        came = entering
        if step < count:
            pairs = [(d, d + 1) for d in (place, step) if 0 <= d < top]
            entering = lax.ppermute(leaving, "lvl", pairs) if pairs else None
        if step == 1:
            ways_then, leaving = lax.optimization_barrier((ways, leaving))
            ways, state, parted_first = spread_close(ready, weight, base, soon_far, ways_then, state)
            if entering is not None:
                entering, state = lax.optimization_barrier((entering, state))
        if place in ready:
            state = (finish_last if step == count else finish_state)(place, ways, came, state)
        if step in ready:
            if step == 1:
                state = finish_state(step, ways, came, state)
            if step == top:
                (state,) = run_chunk(1, [step], {"weight": weight, "base": base, "state": state}, sends=False)
            else:
                extra = {"late": late_top if step == top - 1 else late, "earlier": leaving}
                state, parted = run_chunk(1, [step], {**own, "soon": soon_far, **extra, "state": state})
    return state[:, :given] if columns != given else state


def solution(mesh):
    placed = (
        P(("grp", "lvl"), None, None),
        P(("grp", "lvl"), None, None),
        P(("grp", "lvl"), None, None),
        P(("grp", "lvl"), "col", None),
    )
    return jax.shard_map(
        local, mesh=mesh, in_specs=placed, out_specs=P(("grp", "lvl"), "col", None), check_vma=False
    )
```

```python
import functools

import jax
import jax.numpy as jnp
from jax import lax
from jax.experimental import pallas as pl
from jax.experimental.pallas import tpu as pltpu
from jax.sharding import PartitionSpec as P

SWEEPS = 8
CHUNK = 4
CHUNKS = SWEEPS // CHUNK
AHEAD = SWEEPS - 1
SOON = CHUNK - 1
F32 = jnp.float32
BF16 = jnp.bfloat16


def resident(shape, dtype):
    return pltpu.VMEM(shape, dtype)


def pin(x, memory=pltpu.VMEM):
    return pltpu.with_memory_space_constraint(x, memory)


def split(x):
    high = x.astype(BF16)
    return high, (x - high.astype(F32)).astype(BF16)


def dot(a, b):
    return jnp.dot(a, b, preferred_element_type=F32)


def dot_nt(a, b):
    return lax.dot_general(a, b, (((1,), (1,)), ((), ())), preferred_element_type=F32)


def dot_parts(a, b, dot=dot):
    return dot(a[0], b[0]) + (dot(a[0], b[1]) + dot(a[1], b[0]))


def place_operator(weight, i, k, value):
    phases = value.shape[0]
    for n, part in enumerate(split(value.T)):
        weight[i, (2 * k + n) * phases : (2 * k + n + 1) * phases] = part


def operator(weight, i, k):
    phases = weight.shape[2]
    at = 2 * k * phases
    return weight[i, at : at + phases], weight[i, at + phases : at + 2 * phases]


def response(first, last, x_high, x_low, weight, base, kept):
    _, columns, phases = base.shape
    rows = phases + columns

    def store(i, new):
        top = new[0:phases]
        end = new[phases:rows] + base[i]
        x_high[i, 0:phases], x_low[i, 0:phases] = split(top)
        x_high[i, phases:rows], x_low[i, phases:rows] = split(end)
        return top, end

    def from_below(i):
        return dot_parts((x_high[i - 1], x_low[i - 1]), operator(weight, i, 0))

    def from_above(i):
        return dot_parts((x_high[i + 1], x_low[i + 1]), operator(weight, i, 1))

    if first == 0:
        high, low = operator(weight, 0, 0)
        x_high[0, 0:phases], x_low[0, 0:phases] = high, low
        x_high[0, phases:rows], x_low[0, phases:rows] = split(base[0])
        kept[0, 0:phases] = high.astype(F32) + low.astype(F32)
        kept[0, phases:rows] = base[0]
    units = [(a, d - a) for d in range(max(first, 1), last) for a in range(d + 1)]
    for a, i in sorted(units, key=lambda unit: (unit[1] + 2 * unit[0], unit)):
        if a == 0:
            store(i, from_below(i))
        elif i > 0:
            store(i, from_below(i) + from_above(i))
        else:
            kept[a - first, 0:phases], kept[a - first, phases:rows] = store(0, from_above(0))


def products(wanted, here_from, weight, base, inv, down, up, pay):
    for i in wanted:
        here_from(i)
        here = split(inv[i])
        for k, block in ((0, down), (1, up)):
            if k in wanted[i]:
                place_operator(weight, i, k, dot_parts(here, split(block[i])))
        if 2 in wanted[i]:
            base[i] = dot_parts(split(pay[i]), here, dot_nt)


def prepare_kernel(inv_far, down_far, up_far, pay_far, weight, base, x_high, x_low, kept, inv, down, up, pay, sems):
    levels = pay.shape[0]
    cuts = ((0, 1), (1, SOON), (SOON, levels))

    def copies(part):
        at, end = cuts[part]
        pairs = [(inv_far, inv), (down_far, down), (up_far, up)]
        found = [
            pltpu.make_async_copy(far.at[at:end], near.at[at:end], sems.at[n, part])
            for n, (far, near) in enumerate(pairs)
        ]
        return found + ([pltpu.make_async_copy(pay_far, pay, sems.at[3, 0])] if part == 0 else [])

    def wait(i):
        for part, (at, _) in enumerate(cuts):
            if i == at:
                for copy in copies(part):
                    copy.wait()

    for part in range(len(cuts)):
        for copy in copies(part):
            copy.start()
    wanted = {i: (0, 1, 2) if i < SOON - 1 else (0, 2) for i in range(SOON)}
    products(wanted, wait, weight, base, inv, down, up, pay)
    response(0, SOON, x_high, x_low, weight, base, kept)
    wait(SOON)


def prepare_rest_kernel(weight_soon, base_soon, inv, down, up, pay, weight, base):
    levels, _, phases = pay.shape
    for i in range(SOON):
        rows = (4 if i < SOON - 1 else 2) * phases
        weight[i, 0:rows] = weight_soon[i, 0:rows]
    base[0:SOON] = base_soon[...]
    wanted = {i: (0, 1, 2) if i >= SOON else (1,) for i in range(SOON - 1, levels)}
    products(wanted, lambda i: None, weight, base, inv, down, up, pay)


def respond_kernel(places, weight, base, x_high_soon, x_low_soon, kept, x_high, x_low):
    @pl.when(among(places))
    def _():
        x_high[0:SOON] = x_high_soon[...]
        x_low[0:SOON] = x_low_soon[...]
        response(SOON, AHEAD, x_high, x_low, weight, base, kept)


VMEM = pl.BlockSpec(memory_space=pltpu.VMEM)
HBM = pl.BlockSpec(memory_space=pltpu.HBM)


def operators(levels, columns, phases):
    return [resident((levels, 4 * phases, phases), BF16), resident((levels, columns, phases), F32)]


def prepare(inverse_diag, down_block, up_block, reward):
    levels, columns, phases = reward.shape
    rows = phases + columns
    matrix = resident((levels, phases, phases), F32)
    *soon, x_high, x_low, kept_soon, inv, down, up, pay = pl.pallas_call(
        prepare_kernel,
        out_shape=operators(SOON, columns, phases)
        + [resident((SOON, rows, phases), BF16)] * 2
        + [resident((SOON, rows, phases), F32)]
        + [matrix] * 3
        + [resident((levels, columns, phases), F32)],
        in_specs=[HBM] * 4,
        out_specs=[VMEM] * 9,
        scratch_shapes=[pltpu.SemaphoreType.DMA((4, 3))],
        compiler_params=pltpu.CompilerParams(vmem_limit_bytes=16 * 2**20),
        name="prepare",
    )(*[pin(x, pltpu.HBM) for x in (inverse_diag, down_block, up_block, reward)])
    weights = pl.pallas_call(
        prepare_rest_kernel,
        out_shape=operators(levels, columns, phases),
        in_specs=[VMEM] * 6,
        out_specs=[VMEM] * 2,
        compiler_params=pltpu.CompilerParams(vmem_limit_bytes=16 * 2**20),
        name="prepare_rest",
    )(*[pin(x) for x in (*soon, inv, down, up, pay)])
    return weights, (x_high, x_low), kept_soon


def respond(places, weights, started):
    _, rows, phases = started[0].shape
    return pl.pallas_call(
        functools.partial(respond_kernel, tuple(places)),
        out_shape=resident((AHEAD - SOON, rows, phases), F32),
        in_specs=[VMEM] * 4,
        out_specs=VMEM,
        scratch_shapes=[pltpu.VMEM((AHEAD, rows, phases), BF16)] * 2,
        compiler_params=pltpu.CompilerParams(vmem_limit_bytes=16 * 2**20),
        name="respond",
    )(*[pin(x) for x in (*weights, *started)])


def stack(x):
    high = x.astype(BF16).astype(F32)
    return jnp.concatenate([high, x - high], axis=0).astype(BF16)


def fold(total):
    half = total.shape[0] // 2
    return total[:half] + total[half:]


def apply(terms):
    values = jnp.concatenate([x for x, _ in terms for _ in range(2)], axis=1)
    return fold(dot(values, jnp.concatenate([operator for _, operator in terms], axis=0)))


def apply_each(values, operator, columns):
    phases = operator.shape[1]
    values = jnp.concatenate(values, axis=0) if len(values) > 1 else values[0]
    total = dot(values, operator[0:phases]) + dot(values, operator[phases:])
    return [fold(total[at : at + 2 * columns]) for at in range(0, total.shape[0], 2 * columns)]


def whole(operator):
    return jnp.concatenate(split(operator), axis=0)


def kept_at(soon, late, j):
    return soon[j] if j < SOON else late[j - SOON]


def carry_terms(soon, late, past, first, last):
    phases = soon.shape[2]
    columns = soon.shape[1] - phases
    above = {n: kept_at(soon, late, n - 1)[phases:] for n in range(max(first, 1), last + 1)}

    def add(j):
        pairs = [(n, n - j) for n in above if n - j in past]
        held = whole(kept_at(soon, late, j)[0:phases])
        for (n, _), term in zip(pairs, apply_each([past[m] for _, m in pairs], held, columns)):
            above[n] += term
        return held

    return above, [functools.partial(add, j) for j in range(last)]


def carried(soon, late, past, first, last):
    above, calls = carry_terms(soon, late, past, first, last)
    for call in calls:
        call()
    return above


def wave(first, weight, base, now, above, feedback, due, emit, chores):
    levels, _, phases = base.shape
    for turn in range(levels + 2 * (CHUNK - 1)):
        for k in range(CHUNK):
            i = turn - 2 * k
            if not (0 <= i < levels and due(i, k)):
                continue
            n = first + 1 + k
            terms = []
            if (i - 1, n) in now:
                terms.append((now[i - 1, n], weight[i, 0 : 2 * phases]))
            if n > 1 and not (i == levels - 1 and above is None):
                over = stack(above[n - 1]) if i == levels - 1 else now[i + 1, n - 1]
                terms.append((over, weight[i, 2 * phases : 4 * phases]))
            value = base[i] + apply(terms) if terms else base[i]
            now[i, n] = stack(value)
            emit(i, k, value)
            if i == levels - 1 and above is not None:
                for later in range(n, first + CHUNK):
                    above[later] += apply([(now[i, n], feedback[later - n])])
        if chores and levels - 2 - turn < len(chores):
            chores.pop(0)()


def edge_level(levels, k):
    return levels - 2 - k


def chunk_kernel(chunk, places, part, names, *refs):
    given = dict(zip(names, refs))
    new_state, *leaving = refs[len(names) :]
    leaving = leaving[0] if leaving else None
    weight, base = given["weight"], given["base"]
    levels, columns, phases = base.shape
    first = chunk * CHUNK

    @pl.when(jnp.logical_not(among(places)))
    def _():
        for name, target in (("state", new_state), ("leaving", leaving)):
            if target is not None:
                target[...] = given[name][...] if name in given else jnp.zeros_like(target)

    @pl.when(among(places))
    def _():
        zero = jnp.zeros((columns, phases), F32)
        above, feedback, chores = {first + k: zero for k in range(CHUNK)}, {}, []
        if "soon" not in given and part != "early":
            above = None
        elif part != "early":
            soon = given["soon"]

            def hold(j, call):
                feedback[j] = call()

            if first and "late" in given:
                past = {n + 1: stack(given["earlier"][n]) for n in range(first)}
                above, calls = carry_terms(soon, given["late"], past, first, first + CHUNK - 1)
            else:
                if not first:
                    above, _ = carry_terms(soon, None, {}, first, first + CHUNK - 1)
                elif "returned" in given:
                    above = {first + k: given["returned"][k] for k in range(CHUNK)}
                calls = [lambda j=j: whole(soon[j, 0:phases]) for j in range(SOON)]
            chores = [functools.partial(hold, j, call) for j, call in enumerate(calls)]
            while part == "late" and chores:
                chores.pop(0)()

        now = {}
        if part == "late":
            for k in range(CHUNK):
                now[edge_level(levels, k), first + 1 + k] = stack(given["edge"][k])
            new_state[...] = given["state"][...]
        elif first:
            for i in range(levels):
                now[i, first] = stack(given["state"][i])
        if part != "late" and "entering" in given:
            for k in range(CHUNK):
                now[-1, first + 1 + k] = stack(given["entering"][k])

        def due(i, k):
            return part == "all" or (i <= edge_level(levels, k)) == (part == "early")

        def emit(i, k, value):
            if k == CHUNK - 1:
                new_state[i] = value
            if leaving is not None and i == (edge_level(levels, k) if part == "early" else levels - 1):
                leaving[k] = value

        wave(first, weight, base, now, above, feedback, due, emit, chores)


def run_chunk(chunk, places, given, part="all", sends=True):
    given = {name: x for name, x in given.items() if x is not None}
    levels, columns, phases = given["base"].shape
    return pl.pallas_call(
        functools.partial(chunk_kernel, chunk, tuple(places), part, tuple(given)),
        out_shape=[resident((levels, columns, phases), F32)] + [resident((CHUNK, columns, phases), F32)] * sends,
        in_specs=[VMEM] * len(given),
        out_specs=[VMEM] * (1 + sends),
        compiler_params=pltpu.CompilerParams(vmem_limit_bytes=16 * 2**20),
        name="chunk",
    )(*[pin(x) for x in given.values()])


def among(places):
    return functools.reduce(jnp.logical_or, [lax.axis_index("lvl") == place for place in places])


def is_open(levels, a, i):
    return i + a < levels


def slot_of(levels, a, i):
    if not is_open(levels, a, i):
        return sum(range(1, a)) + i - (levels - a)
    return sum(levels - n if n < CHUNK else AHEAD - n for n in range(a)) + i


def get_answer(ways, levels, a, i, rows=slice(None)):
    high, low = ways[0:2] if is_open(levels, a, i) else ways[2:4]
    at = slot_of(levels, a, i)
    return high[at, rows], low[at, rows]


def spread_open_kernel(places, weight, base, high, low, kept):
    levels, columns, phases = base.shape
    rows = phases + columns

    def step(at, i, terms, keep=None):
        new = sum(dot_parts((high[x], low[x]), operator(weight, i, k)) for x, k in terms)
        unit, run = new[0:phases], new[phases:rows] + base[i]
        high[at, 0:phases], low[at, 0:phases] = split(unit)
        high[at, phases:rows], low[at, phases:rows] = split(run)
        if keep is not None:
            kept[keep, 0:phases], kept[keep, phases:rows] = unit, run

    @pl.when(among(places))
    def _():
        high[0, 0:phases], low[0, 0:phases] = operator(weight, 0, 0)
        high[0, phases:rows], low[0, phases:rows] = split(base[0])

        units = [(a, i) for a in range(AHEAD) for i in range(levels - a if a < CHUNK else AHEAD - a) if a + i]
        for a, i in sorted(units, key=lambda unit: (unit[1] + 2 * unit[0], unit)):
            terms = []
            if i > 0:
                terms.append((slot_of(levels, a, i - 1), 0))
            if a > 0:
                terms.append((slot_of(levels, a - 1, i + 1), 1))
            step(slot_of(levels, a, i), i, terms, a - SOON if i == 0 and a >= SOON else None)


def spread_close_kernel(
    places, weight, base, soon, open_high, open_low, before, high, low, state, leaving, feed_high, feed_low
):
    levels, columns, phases = base.shape
    rows = phases + columns
    top = levels - 1
    ways = (open_high, open_low, high, low)

    @pl.when(jnp.logical_not(among(places)))
    def _():
        state[...] = before[...]

    @pl.when(among(places))
    def _():
        for j in range(CHUNK - 1):
            feed_high[j], feed_low[j] = split(soon[j, 0:phases])
        units = [(a, i) for a in range(1, CHUNK) for i in range(levels - a, levels)]
        for a, i in sorted(units, key=lambda unit: (unit[1] + 2 * unit[0], unit[1])):
            new = dot_parts(get_answer(ways, levels, a, i - 1), operator(weight, i, 0))
            if i < top:
                over = get_answer(ways, levels, a - 1, i + 1)
            else:
                back = sum(
                    dot_parts(get_answer(ways, levels, a - 1 - j, top), (feed_high[j], feed_low[j])) for j in range(a)
                )
                end = back[phases:rows] + soon[a - 1, phases:rows]
                over = split(jnp.concatenate([back[0:phases], end], axis=0))
            new += dot_parts(over, operator(weight, i, 1))
            at = slot_of(levels, a, i)
            high[at, 0:phases], low[at, 0:phases] = split(new[0:phases])
            high[at, phases:rows], low[at, phases:rows] = split(new[phases:rows] + base[i])

        def run(a, i):
            return sum(part.astype(F32) for part in get_answer(ways, levels, a, i, slice(phases, rows)))

        for i in range(levels):
            state[i] = run(CHUNK - 1, i)
        for a in range(CHUNK):
            leaving[a] = run(a, top)


def spread_open(places, weight, base):
    levels, columns, phases = base.shape
    assert levels > AHEAD and levels >= 2 * CHUNK - 1
    rows = phases + columns
    slots = slot_of(levels, AHEAD, 0)
    *ways, kept = pl.pallas_call(
        functools.partial(spread_open_kernel, tuple(places)),
        out_shape=[resident((slots, rows, phases), BF16)] * 2 + [resident((AHEAD - SOON, rows, phases), F32)],
        in_specs=[VMEM] * 2,
        out_specs=[VMEM] * 3,
        compiler_params=pltpu.CompilerParams(vmem_limit_bytes=16 * 2**20),
        name="spread_open",
    )(*[pin(x) for x in (weight, base)])
    return ways, kept


def spread_close(places, weight, base, soon, ways, state):
    levels, columns, phases = base.shape
    rows = phases + columns
    *more, state, leaving = pl.pallas_call(
        functools.partial(spread_close_kernel, tuple(places)),
        out_shape=[resident((sum(range(CHUNK)), rows, phases), BF16)] * 2
        + [resident((levels, columns, phases), F32), resident((CHUNK, columns, phases), F32)],
        in_specs=[VMEM] * 6,
        out_specs=[VMEM] * 4,
        scratch_shapes=[pltpu.VMEM((CHUNK - 1, phases, phases), BF16)] * 2,
        compiler_params=pltpu.CompilerParams(vmem_limit_bytes=16 * 2**20),
        name="spread_close",
    )(*[pin(x) for x in (weight, base, soon, *ways, state)])
    return [*ways, *more], state, leaving


def finish_leaving_kernel(place, *refs, levels):
    *ways, entering, leaving, before, new = refs
    columns, phases = entering.shape[1:]

    @pl.when(lax.axis_index("lvl") != place)
    def _():
        new[...] = before[...]

    @pl.when(lax.axis_index("lvl") == place)
    def _():
        values = [stack(entering[k]) for k in range(CHUNK)]
        total = [leaving[k] for k in range(CHUNK)]
        for a in range(CHUNK):
            pair = jnp.concatenate(get_answer(ways, levels, a, levels - 1, slice(0, phases)), axis=0)
            for k, term in enumerate(apply_each(values[: CHUNK - a], pair, columns)):
                total[a + k] += term
        for k in range(CHUNK):
            new[k] = total[k]


def finish_leaving(place, ways, entering, leaving, before, levels):
    return pl.pallas_call(
        functools.partial(finish_leaving_kernel, place, levels=levels),
        out_shape=resident(leaving.shape, F32),
        in_specs=[VMEM] * 7,
        out_specs=VMEM,
        compiler_params=pltpu.CompilerParams(vmem_limit_bytes=8 * 2**20),
        name="finish_leaving",
    )(*[pin(x) for x in (*ways, entering, leaving, before)])


def finish_state_kernel(place, *refs):
    *ways, entering, state, new = refs
    levels, _, phases = state.shape

    @pl.when(lax.axis_index("lvl") != place)
    def _():
        new[...] = state[...]

    @pl.when(lax.axis_index("lvl") == place)
    def _():
        values = [stack(entering[CHUNK - 1 - a]) for a in range(CHUNK)]
        for i in range(levels):
            terms = []
            for a in range(CHUNK):
                pair = jnp.concatenate(get_answer(ways, levels, a, i, slice(0, phases)), axis=0)
                terms.append((values[a], pair))
            new[i] = state[i] + apply(terms)


def finish_state(place, ways, entering, state, last):
    return pl.pallas_call(
        functools.partial(finish_state_kernel, place),
        out_shape=(jax.ShapeDtypeStruct if last else resident)(state.shape, F32),
        in_specs=[VMEM] * 6,
        out_specs=VMEM,
        compiler_params=pltpu.CompilerParams(vmem_limit_bytes=8 * 2**20),
        name="finish_state",
    )(*[pin(x) for x in (*ways, entering, state)])


def answer_kernel(step, soon, late, entering, returned):
    @pl.when(lax.axis_index("lvl") == step)
    def _():
        past = {n + 1: stack(entering[n]) for n in range(CHUNK)}
        above = carried(soon, late, past, CHUNK, 2 * CHUNK - 1)
        for k in range(CHUNK):
            returned[k] = above[CHUNK + k]


def answer(step, soon, late, entering):
    return pl.pallas_call(
        functools.partial(answer_kernel, step),
        out_shape=resident(entering.shape, F32),
        in_specs=[VMEM] * 3,
        out_specs=VMEM,
        compiler_params=pltpu.CompilerParams(vmem_limit_bytes=8 * 2**20),
        name="answer",
    )(*[pin(x) for x in (soon, late, entering)])


def local(inverse_diag, down_block, up_block, reward):
    given = reward.shape[1]
    columns = -(-given // 16) * 16
    if columns != given:
        reward = jnp.pad(reward, ((0, 0), (0, columns - given), (0, 0)))
    count = lax.axis_size("lvl")
    assert CHUNKS == 2 and count > 1
    top = count - 1
    ready = [d for d in range(1, count) if d % 2 == 0 or d == top]
    odd = [d for d in range(1, top, 2)]
    weights, begun, soon_here = prepare(inverse_diag, down_block, up_block, reward)
    weight, base = weights
    late_odd = respond(odd, weights, begun) if odd else None
    ways, late_here = spread_open(ready, weight, base)
    soon_odd = lax.ppermute(soon_here, "lvl", [(d + 1, d) for d in range(1, top, 2)])
    soon = lax.ppermute(soon_here, "lvl", [(d + 1, d) for d in range(0, top, 2)])
    late = lax.ppermute(late_odd, "lvl", [(d, d - 1) for d in odd]) if odd else None
    soon, late_here, late_odd = lax.optimization_barrier((soon, late_here, late_odd))
    late_top = None
    own = {"weight": weight, "base": base, "soon": soon}
    state = leaving = entering = parted = None
    for step in range(count + 1):
        place = step - 1
        earlier = leaving
        returned = edge = None
        if step % 2 == 0 and 0 < step < count:
            returned = lax.ppermute(answer(step, soon_here, late_here, entering), "lvl", [(step, place)])
            given_early = {"weight": weight, "base": base, "entering": entering_next, "state": state}
            state, edge = run_chunk(1, [place], given_early, "early")
        if place in ready and place < top:
            leaving = finish_leaving(place, ways, entering, parted, leaving, base.shape[0])
        if step in ready:
            if step < top:
                leaving = finish_leaving(step, ways, entering, parted_first, leaving, base.shape[0])
        elif step < count:
            state, leaving = run_chunk(
                0, [step], {**own, "soon": soon_odd if step % 2 else soon, "entering": entering, "state": state, "leaving": leaving}
            )
        if step == 1 and top > 1:
            sent_first = lax.ppermute(leaving, "lvl", [(1, 2)])
        if step == 1:
            top_sent, leaving = lax.optimization_barrier((late_here, leaving))
            late_top = lax.ppermute(top_sent, "lvl", [(top, top - 1)]) if top % 2 else None
            first_late = late if odd else late_top
            given_first = {**own, "late": first_late, "earlier": earlier, "state": state, "leaving": leaving}
            state, leaving = run_chunk(1, [0], given_first)
        if step in ready and step > 1:
            state = finish_state(step, ways, entering, state, False)
        if returned is not None:
            given_rest = {**own, "soon": soon_odd, "returned": returned, "edge": edge, "state": state, "leaving": leaving}
            state, leaving = run_chunk(1, [place], given_rest, "late")
        came = entering
        if step < count:
            pairs = [(d, d + 1) for d in (place, step) if 0 <= d < top]
            if step == 1 and top > 1:
                entering_next = lax.ppermute(leaving, "lvl", [(0, 1)])
                entering = sent_first
            else:
                entering = entering_next = lax.ppermute(leaving, "lvl", pairs) if pairs else None
        if step == 1:
            ways_then, leaving = lax.optimization_barrier((ways, leaving))
            ways, state, parted_first = spread_close(ready, weight, base, soon, ways_then, state)
            if entering is not None:
                entering, state = lax.optimization_barrier((entering, state))
        if place in ready:
            state = finish_state(place, ways, came, state, step == count)
        if step in ready:
            if step == 1:
                state = finish_state(step, ways, came, state, False)
            if step == top:
                (state,) = run_chunk(1, [step], {"weight": weight, "base": base, "state": state}, sends=False)
            else:
                extra = {"late": late_top if step == top - 1 else late, "earlier": leaving}
                state, parted = run_chunk(1, [step], {**own, **extra, "state": state})
    return state[:, :given] if columns != given else state


def solution(mesh):
    placed = (
        P(("grp", "lvl"), None, None),
        P(("grp", "lvl"), None, None),
        P(("grp", "lvl"), None, None),
        P(("grp", "lvl"), "col", None),
    )
    return jax.shard_map(
        local, mesh=mesh, in_specs=placed, out_specs=P(("grp", "lvl"), "col", None), check_vma=False
    )
```

```python
import functools

import jax
import jax.numpy as jnp
from jax import lax
from jax.experimental import pallas as pl
from jax.experimental.pallas import tpu as pltpu
from jax.sharding import PartitionSpec as P

SWEEPS = 8
CHUNK = 4
CHUNKS = SWEEPS // CHUNK
AHEAD = SWEEPS - 1
SOON = CHUNK - 1
F32 = jnp.float32
BF16 = jnp.bfloat16


def resident(shape, dtype):
    return pltpu.VMEM(shape, dtype)


def pin(x, memory=pltpu.VMEM):
    return pltpu.with_memory_space_constraint(x, memory)


def split(x):
    high = x.astype(BF16)
    return high, (x - high.astype(F32)).astype(BF16)


def dot(a, b):
    return jnp.dot(a, b, preferred_element_type=F32)


def dot_nt(a, b):
    return lax.dot_general(a, b, (((1,), (1,)), ((), ())), preferred_element_type=F32)


def dot_parts(a, b, dot=dot):
    return dot(a[0], b[0]) + (dot(a[0], b[1]) + dot(a[1], b[0]))


def place_operator(weight, i, k, value):
    phases = value.shape[0]
    for n, part in enumerate(split(value.T)):
        weight[i, (2 * k + n) * phases : (2 * k + n + 1) * phases] = part


def operator(weight, i, k):
    phases = weight.shape[2]
    at = 2 * k * phases
    return weight[i, at : at + phases], weight[i, at + phases : at + 2 * phases]


def response(first, last, x_high, x_low, weight, base, kept):
    _, columns, phases = base.shape
    rows = phases + columns

    def store(i, new):
        top = new[0:phases]
        end = new[phases:rows] + base[i]
        x_high[i, 0:phases], x_low[i, 0:phases] = split(top)
        x_high[i, phases:rows], x_low[i, phases:rows] = split(end)
        return top, end

    def from_below(i):
        return dot_parts((x_high[i - 1], x_low[i - 1]), operator(weight, i, 0))

    def from_above(i):
        return dot_parts((x_high[i + 1], x_low[i + 1]), operator(weight, i, 1))

    if first == 0:
        high, low = operator(weight, 0, 0)
        x_high[0, 0:phases], x_low[0, 0:phases] = high, low
        x_high[0, phases:rows], x_low[0, phases:rows] = split(base[0])
        kept[0, 0:phases] = high.astype(F32) + low.astype(F32)
        kept[0, phases:rows] = base[0]
    units = [(a, d - a) for d in range(max(first, 1), last) for a in range(d + 1)]
    for a, i in sorted(units, key=lambda unit: (unit[1] + 2 * unit[0], unit)):
        if a == 0:
            store(i, from_below(i))
        elif i > 0:
            store(i, from_below(i) + from_above(i))
        else:
            kept[a - first, 0:phases], kept[a - first, phases:rows] = store(0, from_above(0))


def products(wanted, here_from, weight, base, inv, down, up, pay):
    for i in wanted:
        here_from(i)
        here = split(inv[i])
        for k, block in ((0, down), (1, up)):
            if k in wanted[i]:
                place_operator(weight, i, k, dot_parts(here, split(block[i])))
        if 2 in wanted[i]:
            base[i] = dot_parts(split(pay[i]), here, dot_nt)


def prepare_kernel(inv_far, down_far, up_far, pay_far, weight, base, x_high, x_low, kept, inv, down, up, pay, sems):
    levels = pay.shape[0]
    cuts = ((0, 1), (1, SOON), (SOON, levels))

    def copies(part):
        at, end = cuts[part]
        pairs = [(inv_far, inv), (down_far, down), (up_far, up)]
        found = [
            pltpu.make_async_copy(far.at[at:end], near.at[at:end], sems.at[n, part])
            for n, (far, near) in enumerate(pairs)
        ]
        return found + ([pltpu.make_async_copy(pay_far, pay, sems.at[3, 0])] if part == 0 else [])

    def wait(i):
        for part, (at, _) in enumerate(cuts):
            if i == at:
                for copy in copies(part):
                    copy.wait()

    for part in range(len(cuts)):
        for copy in copies(part):
            copy.start()
    wanted = {i: (0, 1, 2) if i < SOON - 1 else (0, 2) for i in range(SOON)}
    products(wanted, wait, weight, base, inv, down, up, pay)
    response(0, SOON, x_high, x_low, weight, base, kept)
    wait(SOON)


def prepare_rest_kernel(weight_soon, base_soon, inv, down, up, pay, weight, base):
    levels, _, phases = pay.shape
    for i in range(SOON):
        rows = (4 if i < SOON - 1 else 2) * phases
        weight[i, 0:rows] = weight_soon[i, 0:rows]
    base[0:SOON] = base_soon[...]
    wanted = {i: (0, 1, 2) if i >= SOON else (1,) for i in range(SOON - 1, levels)}
    products(wanted, lambda i: None, weight, base, inv, down, up, pay)


def respond_kernel(places, weight, base, x_high_soon, x_low_soon, kept, x_high, x_low):
    @pl.when(among(places))
    def _():
        x_high[0:SOON] = x_high_soon[...]
        x_low[0:SOON] = x_low_soon[...]
        response(SOON, AHEAD, x_high, x_low, weight, base, kept)


VMEM = pl.BlockSpec(memory_space=pltpu.VMEM)
HBM = pl.BlockSpec(memory_space=pltpu.HBM)


def operators(levels, columns, phases):
    return [resident((levels, 4 * phases, phases), BF16), resident((levels, columns, phases), F32)]


def prepare(inverse_diag, down_block, up_block, reward):
    levels, columns, phases = reward.shape
    rows = phases + columns
    matrix = resident((levels, phases, phases), F32)
    *soon, x_high, x_low, kept_soon, inv, down, up, pay = pl.pallas_call(
        prepare_kernel,
        out_shape=operators(SOON, columns, phases)
        + [resident((SOON, rows, phases), BF16)] * 2
        + [resident((SOON, rows, phases), F32)]
        + [matrix] * 3
        + [resident((levels, columns, phases), F32)],
        in_specs=[HBM] * 4,
        out_specs=[VMEM] * 9,
        scratch_shapes=[pltpu.SemaphoreType.DMA((4, 3))],
        compiler_params=pltpu.CompilerParams(vmem_limit_bytes=16 * 2**20),
        name="prepare",
    )(*[pin(x, pltpu.HBM) for x in (inverse_diag, down_block, up_block, reward)])
    weights = pl.pallas_call(
        prepare_rest_kernel,
        out_shape=operators(levels, columns, phases),
        in_specs=[VMEM] * 6,
        out_specs=[VMEM] * 2,
        compiler_params=pltpu.CompilerParams(vmem_limit_bytes=16 * 2**20),
        name="prepare_rest",
    )(*[pin(x) for x in (*soon, inv, down, up, pay)])
    return weights, (x_high, x_low), kept_soon


def respond(places, weights, started):
    _, rows, phases = started[0].shape
    return pl.pallas_call(
        functools.partial(respond_kernel, tuple(places)),
        out_shape=resident((AHEAD - SOON, rows, phases), F32),
        in_specs=[VMEM] * 4,
        out_specs=VMEM,
        scratch_shapes=[pltpu.VMEM((AHEAD, rows, phases), BF16)] * 2,
        compiler_params=pltpu.CompilerParams(vmem_limit_bytes=16 * 2**20),
        name="respond",
    )(*[pin(x) for x in (*weights, *started)])


def stack(x):
    high = x.astype(BF16).astype(F32)
    return jnp.concatenate([high, x - high], axis=0).astype(BF16)


def fold(total):
    half = total.shape[0] // 2
    return total[:half] + total[half:]


def apply(terms):
    return fold(sum(dot(jnp.concatenate([x, x], axis=1), operator) for x, operator in terms))


def apply_each(values, operator, columns):
    phases = operator.shape[1]
    values = jnp.concatenate(values, axis=0) if len(values) > 1 else values[0]
    total = dot(values, operator[0:phases]) + dot(values, operator[phases:])
    return [fold(total[at : at + 2 * columns]) for at in range(0, total.shape[0], 2 * columns)]


def whole(operator):
    return jnp.concatenate(split(operator), axis=0)


def kept_at(soon, late, j):
    return soon[j] if j < SOON else late[j - SOON]


def carry_terms(soon, late, past, first, last):
    phases = soon.shape[2]
    columns = soon.shape[1] - phases
    above = {n: kept_at(soon, late, n - 1)[phases:] for n in range(max(first, 1), last + 1)}

    def add(j):
        pairs = [(n, n - j) for n in above if n - j in past]
        held = whole(kept_at(soon, late, j)[0:phases])
        for (n, _), term in zip(pairs, apply_each([past[m] for _, m in pairs], held, columns)):
            above[n] += term
        return held

    return above, [functools.partial(add, j) for j in range(last)]


def carried(soon, late, past, first, last):
    above, calls = carry_terms(soon, late, past, first, last)
    for call in calls:
        call()
    return above


def wave(first, weight, base, now, above, feedback, due, emit, chores):
    levels, _, phases = base.shape
    for turn in range(levels + 2 * (CHUNK - 1)):
        for k in range(CHUNK):
            i = turn - 2 * k
            if not (0 <= i < levels and due(i, k)):
                continue
            n = first + 1 + k
            terms = []
            if (i - 1, n) in now:
                terms.append((now[i - 1, n], weight[i, 0 : 2 * phases]))
            if n > 1 and not (i == levels - 1 and above is None):
                over = stack(above[n - 1]) if i == levels - 1 else now[i + 1, n - 1]
                terms.append((over, weight[i, 2 * phases : 4 * phases]))
            value = base[i] + apply(terms) if terms else base[i]
            now[i, n] = stack(value)
            emit(i, k, value)
            if i == levels - 1 and above is not None:
                for later in range(n, first + CHUNK):
                    above[later] += apply([(now[i, n], feedback[later - n])])
        if chores and levels - 2 - turn < len(chores):
            chores.pop(0)()


def edge_level(levels, k):
    return levels - 2 - k


def chunk_kernel(chunk, places, part, names, *refs):
    given = dict(zip(names, refs))
    new_state, *leaving = refs[len(names) :]
    leaving = leaving[0] if leaving else None
    weight, base = given["weight"], given["base"]
    levels, columns, phases = base.shape
    first = chunk * CHUNK

    @pl.when(jnp.logical_not(among(places)))
    def _():
        for name, target in (("state", new_state), ("leaving", leaving)):
            if target is not None:
                target[...] = given[name][...] if name in given else jnp.zeros_like(target)

    @pl.when(among(places))
    def _():
        zero = jnp.zeros((columns, phases), F32)
        above, feedback, chores = {first + k: zero for k in range(CHUNK)}, {}, []
        if "soon" not in given and part != "early":
            above = None
        elif part != "early":
            soon = given["soon"]

            def hold(j, call):
                feedback[j] = call()

            if first and "late" in given:
                past = {n + 1: stack(given["earlier"][n]) for n in range(first)}
                above, calls = carry_terms(soon, given["late"], past, first, first + CHUNK - 1)
            else:
                if not first:
                    above, _ = carry_terms(soon, None, {}, first, first + CHUNK - 1)
                elif "returned" in given:
                    above = {first + k: given["returned"][k] for k in range(CHUNK)}
                calls = [lambda j=j: whole(soon[j, 0:phases]) for j in range(SOON)]
            chores = [functools.partial(hold, j, call) for j, call in enumerate(calls)]
            while part == "late" and chores:
                chores.pop(0)()

        now = {}
        if part == "late":
            for k in range(CHUNK):
                now[edge_level(levels, k), first + 1 + k] = stack(given["edge"][k])
            new_state[...] = given["state"][...]
        elif first:
            for i in range(levels):
                now[i, first] = stack(given["state"][i])
        if part != "late" and "entering" in given:
            for k in range(CHUNK):
                now[-1, first + 1 + k] = stack(given["entering"][k])

        def due(i, k):
            return part == "all" or (i <= edge_level(levels, k)) == (part == "early")

        def emit(i, k, value):
            if k == CHUNK - 1:
                new_state[i] = value
            if leaving is not None and i == (edge_level(levels, k) if part == "early" else levels - 1):
                leaving[k] = value

        wave(first, weight, base, now, above, feedback, due, emit, chores)


def run_chunk(chunk, places, given, part="all", sends=True):
    given = {name: x for name, x in given.items() if x is not None}
    levels, columns, phases = given["base"].shape
    return pl.pallas_call(
        functools.partial(chunk_kernel, chunk, tuple(places), part, tuple(given)),
        out_shape=[resident((levels, columns, phases), F32)] + [resident((CHUNK, columns, phases), F32)] * sends,
        in_specs=[VMEM] * len(given),
        out_specs=[VMEM] * (1 + sends),
        compiler_params=pltpu.CompilerParams(vmem_limit_bytes=16 * 2**20),
        name="chunk",
    )(*[pin(x) for x in given.values()])


def among(places):
    return functools.reduce(jnp.logical_or, [lax.axis_index("lvl") == place for place in places])


def is_open(levels, a, i):
    return i + a < levels


def slot_of(levels, a, i):
    if not is_open(levels, a, i):
        return sum(range(1, a)) + i - (levels - a)
    return sum(levels - n if n < CHUNK else AHEAD - n for n in range(a)) + i


def get_answer(ways, levels, a, i, rows=slice(None)):
    high, low = ways[0:2] if is_open(levels, a, i) else ways[2:4]
    at = slot_of(levels, a, i)
    return high[at, rows], low[at, rows]


def spread_open_kernel(places, weight, base, high, low, kept):
    levels, columns, phases = base.shape
    rows = phases + columns

    def step(at, i, terms, keep=None):
        new = sum(dot_parts((high[x], low[x]), operator(weight, i, k)) for x, k in terms)
        unit, run = new[0:phases], new[phases:rows] + base[i]
        high[at, 0:phases], low[at, 0:phases] = split(unit)
        high[at, phases:rows], low[at, phases:rows] = split(run)
        if keep is not None:
            kept[keep, 0:phases], kept[keep, phases:rows] = unit, run

    @pl.when(among(places))
    def _():
        high[0, 0:phases], low[0, 0:phases] = operator(weight, 0, 0)
        high[0, phases:rows], low[0, phases:rows] = split(base[0])

        units = [(a, i) for a in range(AHEAD) for i in range(levels - a if a < CHUNK else AHEAD - a) if a + i]
        for a, i in sorted(units, key=lambda unit: (unit[1] + 2 * unit[0], unit)):
            terms = []
            if i > 0:
                terms.append((slot_of(levels, a, i - 1), 0))
            if a > 0:
                terms.append((slot_of(levels, a - 1, i + 1), 1))
            step(slot_of(levels, a, i), i, terms, a - SOON if i == 0 and a >= SOON else None)


def spread_close_kernel(
    places, weight, base, soon, open_high, open_low, before, high, low, state, leaving, feed_high, feed_low
):
    levels, columns, phases = base.shape
    rows = phases + columns
    top = levels - 1
    ways = (open_high, open_low, high, low)

    @pl.when(jnp.logical_not(among(places)))
    def _():
        state[...] = before[...]

    @pl.when(among(places))
    def _():
        for j in range(CHUNK - 1):
            feed_high[j], feed_low[j] = split(soon[j, 0:phases])
        units = [(a, i) for a in range(1, CHUNK) for i in range(levels - a, levels)]
        for a, i in sorted(units, key=lambda unit: (unit[1] + 2 * unit[0], unit[1])):
            new = dot_parts(get_answer(ways, levels, a, i - 1), operator(weight, i, 0))
            if i < top:
                over = get_answer(ways, levels, a - 1, i + 1)
            else:
                back = sum(
                    dot_parts(get_answer(ways, levels, a - 1 - j, top), (feed_high[j], feed_low[j])) for j in range(a)
                )
                end = back[phases:rows] + soon[a - 1, phases:rows]
                over = split(jnp.concatenate([back[0:phases], end], axis=0))
            new += dot_parts(over, operator(weight, i, 1))
            at = slot_of(levels, a, i)
            high[at, 0:phases], low[at, 0:phases] = split(new[0:phases])
            high[at, phases:rows], low[at, phases:rows] = split(new[phases:rows] + base[i])

        def run(a, i):
            return sum(part.astype(F32) for part in get_answer(ways, levels, a, i, slice(phases, rows)))

        for i in range(levels):
            state[i] = run(CHUNK - 1, i)
        for a in range(CHUNK):
            leaving[a] = run(a, top)


def spread_open(places, weight, base):
    levels, columns, phases = base.shape
    assert levels > AHEAD and levels >= 2 * CHUNK - 1
    rows = phases + columns
    slots = slot_of(levels, AHEAD, 0)
    *ways, kept = pl.pallas_call(
        functools.partial(spread_open_kernel, tuple(places)),
        out_shape=[resident((slots, rows, phases), BF16)] * 2 + [resident((AHEAD - SOON, rows, phases), F32)],
        in_specs=[VMEM] * 2,
        out_specs=[VMEM] * 3,
        compiler_params=pltpu.CompilerParams(vmem_limit_bytes=16 * 2**20),
        name="spread_open",
    )(*[pin(x) for x in (weight, base)])
    return ways, kept


def spread_close(places, weight, base, soon, ways, state):
    levels, columns, phases = base.shape
    rows = phases + columns
    *more, state, leaving = pl.pallas_call(
        functools.partial(spread_close_kernel, tuple(places)),
        out_shape=[resident((sum(range(CHUNK)), rows, phases), BF16)] * 2
        + [resident((levels, columns, phases), F32), resident((CHUNK, columns, phases), F32)],
        in_specs=[VMEM] * 6,
        out_specs=[VMEM] * 4,
        scratch_shapes=[pltpu.VMEM((CHUNK - 1, phases, phases), BF16)] * 2,
        compiler_params=pltpu.CompilerParams(vmem_limit_bytes=16 * 2**20),
        name="spread_close",
    )(*[pin(x) for x in (weight, base, soon, *ways, state)])
    return [*ways, *more], state, leaving


def finish_leaving_kernel(place, *refs, levels):
    *ways, entering, leaving, before, new = refs
    columns, phases = entering.shape[1:]

    @pl.when(lax.axis_index("lvl") != place)
    def _():
        new[...] = before[...]

    @pl.when(lax.axis_index("lvl") == place)
    def _():
        values = [stack(entering[k]) for k in range(CHUNK)]
        total = [leaving[k] for k in range(CHUNK)]
        for a in range(CHUNK):
            pair = jnp.concatenate(get_answer(ways, levels, a, levels - 1, slice(0, phases)), axis=0)
            for k, term in enumerate(apply_each(values[: CHUNK - a], pair, columns)):
                total[a + k] += term
        for k in range(CHUNK):
            new[k] = total[k]


def finish_leaving(place, ways, entering, leaving, before, levels):
    return pl.pallas_call(
        functools.partial(finish_leaving_kernel, place, levels=levels),
        out_shape=resident(leaving.shape, F32),
        in_specs=[VMEM] * 7,
        out_specs=VMEM,
        compiler_params=pltpu.CompilerParams(vmem_limit_bytes=8 * 2**20),
        name="finish_leaving",
    )(*[pin(x) for x in (*ways, entering, leaving, before)])


def finish_state_kernel(place, *refs):
    *ways, entering, state, new = refs
    levels, _, phases = state.shape

    @pl.when(lax.axis_index("lvl") != place)
    def _():
        new[...] = state[...]

    @pl.when(lax.axis_index("lvl") == place)
    def _():
        values = [stack(entering[CHUNK - 1 - a]) for a in range(CHUNK)]
        for i in range(levels):
            terms = []
            for a in range(CHUNK):
                pair = jnp.concatenate(get_answer(ways, levels, a, i, slice(0, phases)), axis=0)
                terms.append((values[a], pair))
            new[i] = state[i] + apply(terms)


def finish_state(place, ways, entering, state, last):
    return pl.pallas_call(
        functools.partial(finish_state_kernel, place),
        out_shape=(jax.ShapeDtypeStruct if last else resident)(state.shape, F32),
        in_specs=[VMEM] * 6,
        out_specs=VMEM,
        compiler_params=pltpu.CompilerParams(vmem_limit_bytes=8 * 2**20),
        name="finish_state",
    )(*[pin(x) for x in (*ways, entering, state)])


def answer_kernel(step, soon, late, entering, returned):
    @pl.when(lax.axis_index("lvl") == step)
    def _():
        past = {n + 1: stack(entering[n]) for n in range(CHUNK)}
        above = carried(soon, late, past, CHUNK, 2 * CHUNK - 1)
        for k in range(CHUNK):
            returned[k] = above[CHUNK + k]


def answer(step, soon, late, entering):
    return pl.pallas_call(
        functools.partial(answer_kernel, step),
        out_shape=resident(entering.shape, F32),
        in_specs=[VMEM] * 3,
        out_specs=VMEM,
        compiler_params=pltpu.CompilerParams(vmem_limit_bytes=8 * 2**20),
        name="answer",
    )(*[pin(x) for x in (soon, late, entering)])


def local(inverse_diag, down_block, up_block, reward):
    given = reward.shape[1]
    columns = -(-given // 16) * 16
    if columns != given:
        reward = jnp.pad(reward, ((0, 0), (0, columns - given), (0, 0)))
    count = lax.axis_size("lvl")
    assert CHUNKS == 2 and count > 1
    top = count - 1
    ready = [d for d in range(1, count) if d % 2 == 0 or d == top]
    odd = [d for d in range(1, top, 2)]
    weights, begun, soon_here = prepare(inverse_diag, down_block, up_block, reward)
    weight, base = weights
    late_odd = respond(odd, weights, begun) if odd else None
    ways, late_here = spread_open(ready, weight, base)
    soon_odd = lax.ppermute(soon_here, "lvl", [(d + 1, d) for d in range(1, top, 2)])
    soon = lax.ppermute(soon_here, "lvl", [(d + 1, d) for d in range(0, top, 2)])
    late = lax.ppermute(late_odd, "lvl", [(d, d - 1) for d in odd]) if odd else None
    soon, late_here, late_odd = lax.optimization_barrier((soon, late_here, late_odd))
    late_top = None
    own = {"weight": weight, "base": base, "soon": soon}
    state = leaving = entering = parted = None
    for step in range(count + 1):
        place = step - 1
        earlier = leaving
        returned = edge = None
        if step % 2 == 0 and 0 < step < count:
            returned = lax.ppermute(answer(step, soon_here, late_here, entering), "lvl", [(step, place)])
            given_early = {"weight": weight, "base": base, "entering": entering_next, "state": state}
            state, edge = run_chunk(1, [place], given_early, "early")
        if place in ready and place < top:
            leaving = finish_leaving(place, ways, entering, parted, leaving, base.shape[0])
        if step in ready:
            if step < top:
                leaving = finish_leaving(step, ways, entering, parted_first, leaving, base.shape[0])
        elif step < count:
            state, leaving = run_chunk(
                0, [step], {**own, "soon": soon_odd if step % 2 else soon, "entering": entering, "state": state, "leaving": leaving}
            )
        if step == 1 and top > 1:
            sent_first = lax.ppermute(leaving, "lvl", [(1, 2)])
        if step == 1:
            top_sent, leaving = lax.optimization_barrier((late_here, leaving))
            late_top = lax.ppermute(top_sent, "lvl", [(top, top - 1)]) if top % 2 else None
            first_late = late if odd else late_top
            given_first = {**own, "late": first_late, "earlier": earlier, "state": state, "leaving": leaving}
            state, leaving = run_chunk(1, [0], given_first)
        if step in ready and step > 1:
            state = finish_state(step, ways, entering, state, False)
        if returned is not None:
            given_rest = {**own, "soon": soon_odd, "returned": returned, "edge": edge, "state": state, "leaving": leaving}
            state, leaving = run_chunk(1, [place], given_rest, "late")
        came = entering
        if step < count:
            pairs = [(d, d + 1) for d in (place, step) if 0 <= d < top]
            if step == 1 and top > 1:
                entering_next = lax.ppermute(leaving, "lvl", [(0, 1)])
                entering = sent_first
            else:
                entering = entering_next = lax.ppermute(leaving, "lvl", pairs) if pairs else None
        if step == 1:
            ways_then, leaving = lax.optimization_barrier((ways, leaving))
            ways, state, parted_first = spread_close(ready, weight, base, soon, ways_then, state)
            if entering is not None:
                entering, state = lax.optimization_barrier((entering, state))
        if place in ready:
            state = finish_state(place, ways, came, state, step == count)
        if step in ready:
            if step == 1:
                state = finish_state(step, ways, came, state, False)
            if step == top:
                (state,) = run_chunk(1, [step], {"weight": weight, "base": base, "state": state}, sends=False)
            else:
                extra = {"late": late_top if step == top - 1 else late, "earlier": leaving}
                state, parted = run_chunk(1, [step], {**own, **extra, "state": state})
    return state[:, :given] if columns != given else state


def solution(mesh):
    placed = (
        P(("grp", "lvl"), None, None),
        P(("grp", "lvl"), None, None),
        P(("grp", "lvl"), None, None),
        P(("grp", "lvl"), "col", None),
    )
    return jax.shard_map(
        local, mesh=mesh, in_specs=placed, out_specs=P(("grp", "lvl"), "col", None), check_vma=False
    )
```
